256 devices in a mesh: row: 16 (over x_hi, z), col: 16 (over x_lo, y, core).
Axes of the slice: x: 4 (x_hi: 2, x_lo: 2; x = x_hi * 2 + x_lo), y: 4, z: 8, core: 2. Of those that a mesh axis runs over, the one named last changes fastest.
Arguments:
- inputs: bfloat16 [64, 1024, 2048], P(None, 'row', 'col'), may hold values from -6 to 6
- cotangent: bfloat16 [64, 1024, 2048], P(None, 'row', 'col'), may hold values from -6 to 6
- spectral_weight: bfloat16 [2, 128, 128, 4096], P(None, 'row', 'col'), may hold values from -12 to 12
- point_weight: bfloat16 [64, 64], replicated, may hold values from -0.75 to 0.75
- bias: float32 [64], replicated, may hold values from -3 to 3
Outputs:
- grad_input: bfloat16 [64, 1024, 2048], P(None, 'row', 'col')
- spectral_grad: float32 [2, 128, 128, 4096], P(None, 'row', 'col')
- pointwise_grad: float32 [64, 64], replicated
- bias_grad: float32 [64], replicated
The draws below stay inside these ranges and needn't reach their ends.
All inputs are finite; a program needn't handle non-finite values.
Results may differ from the reference program's by a relative error of at most 0.015.
Values may be sent and summed in bfloat16 or wider, within the bound.
A program may use at most 128 MiB of HBM per device.

```python
import math
import jax
import jax.numpy as jnp
from jax import lax

C = 64
K1 = 128
K2 = 128
TY = 64
NY = 1024
NX = 2048
N_ROW = 16


def with_spikes(entries, own_key, source, target, shards_of, factor):
    def block_of(axis_at):
        return (jnp.arange(entries.shape[axis_at]) // (entries.shape[axis_at] // shards_of)).reshape((-1,) + (1,) * (entries.ndim - 1 - axis_at))

    first = jax.random.permutation(own_key, shards_of)[block_of(target)]
    second = (block_of(target) + shards_of // 2) % shards_of
    return jnp.where((block_of(source) == first) | (block_of(source) == second), factor * entries, entries)


def steps_of(stream_key, dims, split, low, largest):
    gain = 1.0
    for dim, blocks in split:
        steps = jax.random.uniform(jax.random.fold_in(jax.random.fold_in(stream_key, 6), dim), (blocks,), jnp.float32, low / len(split), largest / len(split))
        gain = gain * jnp.repeat(jnp.exp(steps), dims[dim] // blocks).reshape((-1,) + (1,) * (len(dims) - 1 - dim))
    return gain


def bell_draw(stream_key, shape, scale, limit, split=(), held_as=jnp.bfloat16):
    drawn = jax.random.normal(stream_key, shape, jnp.float32) * scale
    if len(split) > 0:
        drawn = steps_of(stream_key, shape, split, -0.22, 0.18) * drawn
    return jnp.clip(drawn, min=-limit, max=limit).astype(held_as)


def noise_with(key, extent, deviation, most, shards, heavy, held_as=jnp.bfloat16):
    array = deviation * jax.random.normal(key, extent, jnp.float32)
    if shards:
        array = array * steps_of(key, extent, shards, -0.22, 0.18)
    return jnp.clip(with_spikes(array, jax.random.fold_in(key, 3), *heavy), -most, most).astype(held_as)


def setup_inputs(seed: int = 0) -> dict:
    arg_keys = jax.random.split(jax.random.key(seed), 6)
    return {
        "inputs": bell_draw(arg_keys[0], (C, NY, NX), 1.0, 6.0, ((1, 16), (2, 16))),
        "cotangent": bell_draw(arg_keys[1], (C, NY, NX), 1.0, 6.0, ((1, 16), (2, 16))),
        "spectral_weight": noise_with(arg_keys[2], (2, K1, K2, C * C), 1.5, 12.0, ((1, 16), (2, 16)), (1, 2, 16, 2.0)),
        "point_weight": bell_draw(arg_keys[3], (C, C), C ** -0.5, 0.75),
        "bias": bell_draw(arg_keys[4], (C,), 0.5, 3.0, (), jnp.float32),
    }


def angles(first, second, total):
    phase = jnp.mod(first[:, None] * second[None, :], total).astype(jnp.float32) * (2.0 * math.pi / total)
    return (jnp.cos(phase).astype(jnp.bfloat16), jnp.sin(phase).astype(jnp.bfloat16))

def widen(table):
    return lax.optimization_barrier(table).astype(jnp.float32)

def normal_slope(value):
    cumul = 0.5 * (1.0 + jax.scipy.special.erf(value * (1.0 / math.sqrt(2.0))))
    dens = jnp.exp(-0.5 * value * value) * (1.0 / math.sqrt(2.0 * math.pi))
    return cumul + value * dens

def reference(inputs, cotangent, spectral_weight, point_weight, bias):
    scale = float(NY * NX) ** (-0.5)
    highest = lax.Precision.HIGHEST
    xs = jnp.arange(NX, dtype=jnp.int32)
    ys = jnp.arange(NY, dtype=jnp.int32)
    modes_x = jnp.arange(K2, dtype=jnp.int32)
    modes_y = jnp.arange(K1, dtype=jnp.int32) - K1 // 2
    cos_x, sin_x = angles(xs, modes_x, NX)
    fwd_x = jnp.stack([widen(cos_x), -widen(sin_x)], 1)
    cos_y, sin_y = angles(ys, modes_y, NY)
    cos_yf, sin_yf = (widen(cos_y), widen(sin_y))
    inv_cos_x, inv_sin_x = angles(modes_x, xs, NX)
    inv_x = jnp.stack([widen(inv_cos_x), -widen(inv_sin_x)], 0)
    inv_cos_y, inv_sin_y = angles(modes_y, ys, NY)
    inv_cy, inv_sy = (widen(inv_cos_y), widen(inv_sin_y))
    point = point_weight.astype(jnp.float32)
    weight = spectral_weight.astype(jnp.float32).reshape(2, K1, K2, C, C)

    def slab(field, index):
        return lax.dynamic_slice_in_dim(field, index * TY, TY, 1).astype(jnp.float32)

    def transform(field):

        def part(index):
            return jnp.einsum('cyx,xpk->cypk', slab(field, index), fwd_x)
        stacked = lax.map(part, jnp.arange(N_ROW))
        whole = stacked.transpose(1, 0, 2, 3, 4).reshape(C, NY, 2, K2)
        real_part, imag_part = (whole[:, :, 0], whole[:, :, 1])
        out_r = jnp.einsum('cyk,yj->jkc', real_part, cos_yf, precision=highest) + jnp.einsum('cyk,yj->jkc', imag_part, sin_yf, precision=highest)
        out_i = jnp.einsum('cyk,yj->jkc', imag_part, cos_yf, precision=highest) - jnp.einsum('cyk,yj->jkc', real_part, sin_yf, precision=highest)
        return jnp.stack([out_r, out_i], 1) * scale

    def spatial(spectrum, index):
        spec_r = spectrum[:, 0].astype(jnp.float32)
        spec_i = spectrum[:, 1].astype(jnp.float32)
        block_c = lax.dynamic_slice_in_dim(inv_cy, index * TY, TY, 1)
        block_s = lax.dynamic_slice_in_dim(inv_sy, index * TY, TY, 1)
        part_r = jnp.einsum('jkc,jy->cyk', spec_r, block_c) - jnp.einsum('jkc,jy->cyk', spec_i, block_s)
        part_i = jnp.einsum('jkc,jy->cyk', spec_r, block_s) + jnp.einsum('jkc,jy->cyk', spec_i, block_c)
        middle = jnp.stack([part_r, part_i], 2).astype(jnp.bfloat16).astype(jnp.float32)
        return jnp.einsum('cypk,pkx->cyx', middle, inv_x) * scale
    u_hat = transform(inputs)
    ur, ui = (u_hat[:, 0], u_hat[:, 1])
    s_r = jnp.einsum('jkc,jkco->jko', ur, weight[0], precision=highest) - jnp.einsum('jkc,jkco->jko', ui, weight[1], precision=highest)
    s_i = jnp.einsum('jkc,jkco->jko', ur, weight[1], precision=highest) + jnp.einsum('jkc,jkco->jko', ui, weight[0], precision=highest)
    s_hat = jnp.stack([s_r, s_i], 1).astype(jnp.bfloat16)

    def forward_block(index):
        field = slab(inputs, index)
        upstream = slab(cotangent, index)
        z = spatial(s_hat, index) + jnp.einsum('cyx,co->oyx', field, point) + bias[:, None, None]
        slope16 = (upstream * normal_slope(z)).astype(jnp.bfloat16)
        slope = slope16.astype(jnp.float32)
        return (slope16, jnp.einsum('cyx,oyx->co', field, slope), lax.optimization_barrier(jnp.sum(slope, axis=(1, 2))))
    dz_blocks, p_terms, b_terms = lax.map(forward_block, jnp.arange(N_ROW))
    dz = dz_blocks.transpose(1, 0, 2, 3).reshape(C, NY, NX)
    g_hat = transform(dz)
    gr, gi = (g_hat[:, 0], g_hat[:, 1])
    grad_r = jnp.einsum('jko,jkc->jkco', gr, ur) + jnp.einsum('jko,jkc->jkco', gi, ui)
    grad_i = jnp.einsum('jko,jkc->jkco', gi, ur) - jnp.einsum('jko,jkc->jkco', gr, ui)
    spectral_grad = jnp.stack([grad_r, grad_i], 0).reshape(2, K1, K2, C * C)
    du_r = jnp.einsum('jkco,jko->jkc', weight[0], gr, precision=highest) + jnp.einsum('jkco,jko->jkc', weight[1], gi, precision=highest)
    du_i = jnp.einsum('jkco,jko->jkc', weight[0], gi, precision=highest) - jnp.einsum('jkco,jko->jkc', weight[1], gr, precision=highest)
    du_hat = jnp.stack([du_r, du_i], 1).astype(jnp.bfloat16)

    def backward_block(index):
        slope = slab(dz, index)
        return (spatial(du_hat, index) + jnp.einsum('oyx,co->cyx', slope, point)).astype(jnp.bfloat16)
    grad_blocks = lax.map(backward_block, jnp.arange(N_ROW))
    grad_input = grad_blocks.transpose(1, 0, 2, 3).reshape(C, NY, NX)
    pointwise_grad = lax.optimization_barrier(jnp.sum(p_terms, axis=0)) * scale
    bias_grad = lax.optimization_barrier(jnp.sum(b_terms, axis=0)) * scale
    return (grad_input, spectral_grad, pointwise_grad, bias_grad)
```

```python
import functools
import math

import jax
import jax.numpy as jnp
import ml_dtypes
import numpy as np
from jax import lax
from jax.experimental import pallas as pl
from jax.experimental.pallas import tpu as pltpu
from jax.sharding import PartitionSpec as P

C = 64
K1 = 128
K2 = 128
NY = 1024
NX = 2048
TY = 64
TX = 128
N = 16
SCALE = float(NY * NX) ** (-0.5)
MESH = pl.DeviceIdType.MESH
BF = jnp.bfloat16
F32 = jnp.float32

X1, Y1, T1, T2, Y2, X2, X3, Y3, T3, T4, Y4, X4, Z1, Z2, Z3 = range(15)


def trig(first, second, total):
    phase = np.mod(first[:, None] * second[None, :], total).astype(np.float32) * np.float32(
        2.0 * math.pi / total
    )
    return np.cos(phase).astype(ml_dtypes.bfloat16), np.sin(phase).astype(ml_dtypes.bfloat16)


@functools.cache
def tables():
    cos, sin = trig(np.arange(K2), np.arange(NX), NX)
    tx = np.stack([cos.reshape(N, 8, NX), -sin.reshape(N, 8, NX)], 1).reshape(2 * K2, 4, NX // 4)
    tx = np.ascontiguousarray(tx.transpose(1, 0, 2))
    cos, sin = trig(np.arange(K1) - K1 // 2, np.arange(NY), NY)
    ty = np.stack([cos.reshape(K1, N, TY), sin.reshape(K1, N, TY)], 2).reshape(K1, 2 * NY)
    tyi = np.concatenate([cos, sin], 0)
    c, m, _ = np.meshgrid(np.arange(4), np.arange(N), np.arange(8), indexing="ij")
    e1 = ((4 * m + c).reshape(-1, 1) == np.arange(C)).astype(ml_dtypes.bfloat16)
    e = (np.arange(C)[:, None] == np.arange(C * C)[None, :] // C).astype(ml_dtypes.bfloat16)
    sel = (np.arange(C * 16)[:, None] // 16 == np.arange(C)[None, :]).astype(ml_dtypes.bfloat16)
    return tx, ty, tyi, e1, e, sel


def dot(a, b):
    return lax.dot_general(a, b, (((1,), (0,)), ((), ())), preferred_element_type=F32)


def dot_t(a, b):
    return lax.dot_general(a, b, (((1,), (1,)), ((), ())), preferred_element_type=F32)


def normal_slope(value):
    cumul = 0.5 * (1.0 + lax.erf(value * (1.0 / math.sqrt(2.0))))
    dens = jnp.exp(-0.5 * value * value) * (1.0 / math.sqrt(2.0 * math.pi))
    return cumul + value * dens


def kernel(
    inp, cot, w, pw, bias, tx, ty, tyi, e1, e, sel,
    gin, sg, pg, bg,
    inp_v, cot_v, w_v, tx_v, ty_v, tyi_v, e1_v, e_v, sel_v,
    xr, yr, tr, xsend, ysend, tsend,
    zsend, zr, f2_v, dz_v, dz2_v, kron_v, zp_v, gz_v, s_v, ue_v, sg_v, gin_v,
    send_sem, recv_sem, loc_sem,
):
    row = lax.axis_index("row")
    col = lax.axis_index("col")
    diag = row == col
    lane_lo = lax.broadcasted_iota(jnp.int32, (16, 128), 1) < 64
    mask_j = (lax.broadcasted_iota(jnp.int32, (8, 8, 128), 2) & 7) == lax.broadcasted_iota(
        jnp.int32, (8, 8, 128), 0
    )

    def wrap(i):
        return lax.rem(i, N)

    def remote(src, dst, phase, to, slot, device):
        return pltpu.make_async_remote_copy(
            src_ref=src,
            dst_ref=dst,
            send_sem=send_sem.at[phase, to],
            recv_sem=recv_sem.at[phase, slot],
            device_id=device,
            device_id_type=MESH,
        )

    def wait_recv(dst, phase, slot):
        remote(dst, dst, phase, slot, slot, (row, col)).wait_recv()

    def send_row(src_of, dst, phase):
        @pl.loop(1, N)
        def _(d):
            r = wrap(row + d)
            remote(src_of(r), dst.at[row], phase, r, row, (r, col)).start()

    def send_col(src_of, dst, phase):
        @pl.loop(1, N)
        def _(d):
            m = wrap(col + d)
            remote(src_of(m), dst.at[col], phase, m, col, (row, m)).start()

    def wait_all(dst, phase, own):
        @pl.loop(1, N)
        def _(d):
            slot = wrap(own + d)
            wait_recv(dst.at[slot], phase, slot)

    def send_t(src, dst, phase, to_modes):
        @pl.loop(0, N)
        def _(i):
            @pl.when(jnp.logical_not(jnp.logical_and(diag, i == row)))
            def _():
                if to_modes:
                    remote(src.at[i], dst.at[col], phase, i, col, (i, row)).start()
                else:
                    remote(src.at[i], dst.at[row], phase, i, row, (col, i)).start()

        @pl.when(diag)
        def _():
            dst[row] = src[row]

    def wait_t(dst, phase):
        @pl.loop(0, N)
        def _(i):
            @pl.when(jnp.logical_not(jnp.logical_and(diag, i == row)))
            def _():
                wait_recv(dst.at[i], phase, i)

    barrier = pltpu.get_barrier_semaphore()

    @pl.loop(1, N)
    def _(d):
        pl.semaphore_signal(barrier, inc=1, device_id=(row, wrap(col + d)), device_id_type=MESH)
        pl.semaphore_signal(barrier, inc=1, device_id=(wrap(row + d), col), device_id_type=MESH)

    @pl.loop(0, N)
    def _(i):
        @pl.when(jnp.logical_not(jnp.logical_and(diag, i == row)))
        def _():
            pl.semaphore_signal(barrier, inc=1, device_id=(col, i), device_id_type=MESH)
            pl.semaphore_signal(barrier, inc=1, device_id=(i, row), device_id_type=MESH)

    loads = [
        pltpu.make_async_copy(src, dst, loc_sem.at[i])
        for i, (src, dst) in enumerate(
            [
                (sel, sel_v),
                (inp, inp_v),
                (tx, tx_v),
                (ty, ty_v),
                (w, w_v),
                (e1, e1_v),
                (e, e_v),
                (tyi, tyi_v),
                (cot, cot_v),
                (inp.at[pl.ds(4 * col, 4)], xr.at[0, col]),
            ]
        )
    ]
    for load in loads:
        load.start()
    pl.semaphore_wait(barrier, jnp.where(diag, 4 * N - 4, 4 * N - 2))

    send_col(lambda m: inp.at[pl.ds(4 * m, 4)], xr.at[0], X1)

    def pack(src, dst):
        for b in range(4):
            dst[:, 128 * b : 128 * b + 128] = src[:, 16 * b : 16 * b + 16, :].reshape(1024, 128)

    def build_kron(which):
        @pl.loop(0, 4)
        def _(i):
            rows = pl.ds(pl.multiple_of(256 * i, 256), 256)
            part = (dot_t if which == 0 else dot)(sel_v[rows, :], pw[...]).astype(BF)
            for j in range(4):
                full = dot_t(part, sel_v[256 * j : 256 * j + 256, :])
                same = (lax.broadcasted_iota(jnp.int32, (256, 256), 0) & 15) == (
                    lax.broadcasted_iota(jnp.int32, (256, 256), 1) & 15
                )
                kron_v[which, rows, 256 * j : 256 * j + 256] = jnp.where(same, full, 0.0).astype(BF)

    def apply_kron(which, src, dst):
        @pl.loop(0, 4)
        def _(i):
            rows = pl.ds(pl.multiple_of(256 * i, 256), 256)
            out = pl.ds(pl.multiple_of(16 * i, 16), 16)
            for h in range(2):
                res = dot(kron_v[which, rows, :], src[:, 256 * h : 256 * h + 256])
                for t in range(2):
                    y = 32 * h + 16 * t
                    dst[out, y : y + 16, :] = res[:, 128 * t : 128 * t + 128].reshape(16, 16, 128)

    def forward_x(src, phase, dst):
        acc = jnp.zeros((256, 256), F32)
        for i in range(4):
            g = lax.rem(lax.div(col, 4) + i, 4)
            blocks = []
            for t in range(4):
                slot = 4 * g + t

                @pl.when(slot != col)
                def _(slot=slot):
                    wait_recv(src.at[slot], phase, slot)

                blocks.append(src[slot].reshape(256, 128))
            acc = acc + dot_t(tx_v[g], jnp.concatenate(blocks, 1))
        dst[...] = acc.astype(BF).reshape(N, 16, 256)

    def forward_y(src, dst):
        acc = jnp.zeros((K1, 64), F32)
        for q in range(4):
            parts = []
            for t in range(4):
                b = src[4 * q + t].astype(F32)
                jb = jnp.concatenate([b[8:16], -b[0:8]], 0)
                rows = []
                for h in range(2):
                    bh = b[:, 128 * h : 128 * h + 128]
                    jh = jb[:, 128 * h : 128 * h + 128]
                    rows.append(jnp.where(lane_lo, bh, pltpu.roll(jh, 64, 1)))
                    rows.append(jnp.where(lane_lo, pltpu.roll(bh, 64, 1), jh))
                parts.append(jnp.concatenate(rows, 0).astype(BF))
            acc = acc + dot_t(ty_v[:, 512 * q : 512 * q + 512], jnp.concatenate(parts, 1))
        res = (acc * SCALE).astype(BF).astype(F32)
        dst[:, :, 0:64] = res.reshape(N, 8, 64)

    def to_modes(src):
        xt = src[...].reshape(128, 128).T
        rows = []
        for ri in range(2):
            cols = []
            for c in range(4):
                at = (2 * c + ri) * 8
                tile = xt[at : at + 8]
                cols.append(jnp.where(mask_j, tile[None], 0.0).reshape(64, 128))
            rows.append(jnp.concatenate(cols, 1))
        return dot(jnp.concatenate(rows, 0).astype(BF), e1_v[...])

    def from_modes(spec, dst):
        full = dot_t(spec.astype(BF), e1_v[...])
        tiles = []
        for c in range(4):
            for ri in range(2):
                part = full[64 * ri : 64 * ri + 64, 128 * c : 128 * c + 128].reshape(8, 8, 128)
                tiles.append(jnp.sum(jnp.where(mask_j, part, 0.0), axis=0))
        xt = jnp.concatenate(tiles + [jnp.zeros((64, 128), F32)], 0)
        dst[...] = xt.T.reshape(N, 8, 128)

    def inverse_y(src, dst):
        ht = src[...].reshape(128, 128).T
        first, second = [], []
        for c in range(4):
            hr, hi = ht[16 * c : 16 * c + 8], ht[16 * c + 8 : 16 * c + 16]
            first += [hr, hi]
            second += [-hi, hr]
        h = jnp.concatenate([jnp.concatenate(first, 0), jnp.concatenate(second, 0)], 1).astype(BF)
        d = dot(h, tyi_v[...])
        for a in range(8):
            for p in range(2):
                t0 = d[32 * p : 32 * p + 16, 128 * a : 128 * a + 128]
                t1 = d[32 * p + 16 : 32 * p + 32, 128 * a : 128 * a + 128]
                at = slice(128 * p, 128 * p + 128)
                dst[2 * a, :, at] = jnp.where(lane_lo, t0, pltpu.roll(t1, 64, 1)).astype(BF)
                dst[2 * a + 1, :, at] = jnp.where(lane_lo, pltpu.roll(t0, 64, 1), t1).astype(BF)

    def inverse_x(src, out, dst, phase):
        yt = src[...].reshape(256, 256).astype(F32).T.astype(BF)
        for i in range(4):
            g = lax.rem(lax.div(col, 4) + 1 + i, 4)
            res = (dot(yt, tx_v[g]) * SCALE).astype(BF)
            for t in range(4):
                m = 4 * g + t
                out[m] = res[:, 128 * t : 128 * t + 128].reshape(4, TY, TX)

                @pl.when(m != col)
                def _(m=m):
                    remote(out.at[m], dst.at[col], phase, m, col, (row, m)).start()

                @pl.when(m == col)
                def _(m=m):
                    dst[m] = out[m]

    tsend[...] = jnp.zeros_like(tsend)
    zsend[...] = jnp.zeros_like(zsend)
    loads[0].wait()
    build_kron(0)
    build_kron(1)
    loads[1].wait()
    pack(inp_v, f2_v)
    apply_kron(0, f2_v, zp_v)
    loads[2].wait()
    loads[9].wait()
    forward_x(xr.at[0], X1, ysend.at[0])
    send_row(lambda r: ysend.at[0, r], yr.at[0], Y1)
    yr[0, row] = ysend[0, row]
    loads[3].wait()
    wait_all(yr.at[0], Y1, row)
    forward_y(yr.at[0], tsend.at[0])
    send_t(tsend.at[0], tr.at[0], T1, True)
    loads[4].wait()
    loads[5].wait()
    loads[6].wait()
    wait_t(tr.at[0], T1)

    u = to_modes(tr.at[0]).astype(BF)

    def fold(t):
        return t[:, 0:128] + t[:, 128:256] + t[:, 256:384] + t[:, 384:512]

    def mix(i, carry):
        sr, si = carry
        at = pl.ds(pl.multiple_of(i * 512, 512), 512)
        ue = dot(u, e_v[:, at])
        ue_v[:, at] = ue
        ur, ui = ue[0:64], ue[64:128]
        wr = w_v[0, :, :, at].astype(F32).reshape(64, 512)
        wi = w_v[1, :, :, at].astype(F32).reshape(64, 512)
        return sr + fold(wr * ur - wi * ui), si + fold(wr * ui + wi * ur)

    zero = jnp.zeros((64, 128), F32)
    sr, si = lax.fori_loop(0, 8, mix, (zero, zero))
    both = jnp.concatenate([sr, si], 0)
    both = both + pltpu.roll(both, 64, 1)
    from_modes(both[:, 0:64], tsend.at[1])
    send_t(tsend.at[1], tr.at[1], T2, False)

    loads[7].wait()
    wait_t(tr.at[1], T2)
    inverse_y(tr.at[1], ysend.at[1])
    send_row(lambda r: ysend.at[1, r], yr.at[1], Y2)
    yr[1, row] = ysend[1, row]
    wait_all(yr.at[1], Y2, row)
    inverse_x(yr.at[1], xsend.at[0], xr.at[1], X2)

    loads[8].wait()

    @pl.loop(0, N)
    def _(i):
        m = wrap(col + i)

        @pl.when(i != 0)
        def _():
            wait_recv(xr.at[1, m], X2, m)

        at = pl.ds(4 * m, 4)
        for c in range(4):
            z = xr[1, m, c].astype(F32) + zp_v[4 * m + c] + bias[4 * m + c]
            dz = cot_v[4 * m + c].astype(F32) * normal_slope(z)
            dz_v[4 * m + c] = dz.astype(BF)

        @pl.when(i != 0)
        def _():
            remote(dz_v.at[at], xr.at[2, col], X3, m, col, (row, m)).start()

        @pl.when(i == 0)
        def _():
            xr[2, m] = dz_v[at]

    pack(dz_v, dz2_v)

    @pl.loop(0, 4)
    def _(o):
        cols = pl.ds(pl.multiple_of(256 * o, 256), 256)
        dzo = dz2_v[cols, :]
        same = (lax.broadcasted_iota(jnp.int32, (256, 256), 0) & 15) == (
            lax.broadcasted_iota(jnp.int32, (256, 256), 1) & 15
        )
        for i in range(4):
            prod = dot_t(f2_v[256 * i : 256 * i + 256, :], dzo)
            prod = jnp.where(same, prod, 0.0).reshape(16, 16, 256)
            s_v[16 * i : 16 * i + 16, cols] = jnp.sum(prod, axis=1)
        s_v[64:72, cols] = dot_t(jnp.ones((16, 512), BF), dzo)[0:8]

    terms = s_v[...]
    high = terms.astype(BF)
    low = (terms - high.astype(F32)).astype(BF)
    terms = dot(high, sel_v[...]) + dot(low, sel_v[...])
    zsend[:, 0:4, 0:64] = terms[0:64].reshape(N, 4, 64)
    zsend[0, 4:5, 0:64] = terms[64:65]
    send_col(lambda m: zsend.at[m], zr.at[0], Z1)
    zr[0, col] = zsend[col]
    apply_kron(1, dz2_v, gz_v)

    forward_x(xr.at[2], X3, ysend.at[2])
    send_row(lambda r: ysend.at[2, r], yr.at[2], Y3)
    yr[2, row] = ysend[2, row]
    wait_all(zr.at[0], Z1, col)
    zr[3, 0] = jnp.sum(zr[0], axis=0)
    send_row(lambda r: zr.at[3, 0], zr.at[1], Z2)
    zr[1, row] = zr[3, 0]
    wait_all(yr.at[2], Y3, row)
    forward_y(yr.at[2], tsend.at[2])
    send_t(tsend.at[2], tr.at[2], T3, True)
    wait_all(zr.at[1], Z2, row)
    zr[3, 1] = jnp.sum(zr[1], axis=0)
    send_col(lambda m: zr.at[3, 1], zr.at[2], Z3)
    zr[2, col] = zr[3, 1]
    wait_t(tr.at[2], T3)

    g = to_modes(tr.at[2])
    g = jnp.concatenate([g, g], 1)
    gr, gi = g[0:64], g[64:128]
    gr4, gi4 = jnp.concatenate([gr] * 4, 1), jnp.concatenate([gi] * 4, 1)

    def mix_back(i, acc):
        at = pl.ds(pl.multiple_of(i * 512, 512), 512)
        wr = w_v[0, :, :, at].astype(F32).reshape(64, 512)
        wi = w_v[1, :, :, at].astype(F32).reshape(64, 512)
        both = jnp.concatenate([wr * gr4 + wi * gi4, wr * gi4 - wi * gr4], 0).astype(BF)
        return acc + dot_t(both, e_v[:, at])

    du = lax.fori_loop(0, 8, mix_back, jnp.zeros((128, 64), F32))
    from_modes(du, tsend.at[3])
    send_t(tsend.at[3], tr.at[3], T4, False)

    @pl.loop(0, 8)
    def _(i):
        at = pl.ds(pl.multiple_of(i * 512, 512), 512)
        ur, ui = ue_v[0:64, at], ue_v[64:128, at]
        sg_v[0, :, :, at] = (gr4 * ur + gi4 * ui).reshape(8, 8, 512)
        sg_v[1, :, :, at] = (gi4 * ur - gr4 * ui).reshape(8, 8, 512)

    out_sg = pltpu.make_async_copy(sg_v, sg, loc_sem.at[0])
    out_sg.start()

    wait_t(tr.at[3], T4)
    inverse_y(tr.at[3], ysend.at[3])
    send_row(lambda r: ysend.at[3, r], yr.at[3], Y4)
    yr[3, row] = ysend[3, row]
    wait_all(zr.at[2], Z3, col)
    pg[...] = zr[2, :, 0:4, 0:64].reshape(64, 64) * SCALE
    bg[...] = zr[2, 0, 4:5, 0:64] * SCALE
    wait_all(yr.at[3], Y4, row)
    inverse_x(yr.at[3], xsend.at[1], xr.at[3], X4)

    @pl.loop(0, N)
    def _(i):
        m = wrap(col + i)

        @pl.when(i != 0)
        def _():
            wait_recv(xr.at[3, m], X4, m)

        at = pl.ds(4 * m, 4)
        gin_v[at] = (xr[3, m].astype(F32) + gz_v[at]).astype(BF)

    out_gin = pltpu.make_async_copy(gin_v, gin, loc_sem.at[1])
    out_gin.start()

    def wait_send(src, phase, to):
        remote(src, src, phase, to, to, (row, col)).wait_send()

    @pl.loop(1, N)
    def _(d):
        m = wrap(col + d)
        r = wrap(row + d)
        wait_send(inp.at[pl.ds(4 * m, 4)], X1, m)
        wait_send(xsend.at[0, m], X2, m)
        wait_send(dz_v.at[pl.ds(4 * m, 4)], X3, m)
        wait_send(xsend.at[1, m], X4, m)
        wait_send(zsend.at[m], Z1, m)
        wait_send(zr.at[3, 1], Z3, m)
        wait_send(zr.at[3, 0], Z2, r)
        for i, phase in enumerate((Y1, Y2, Y3, Y4)):
            wait_send(ysend.at[i, r], phase, r)

    @pl.loop(0, N)
    def _(i):
        @pl.when(jnp.logical_not(jnp.logical_and(diag, i == row)))
        def _():
            for k, phase in enumerate((T1, T2, T3, T4)):
                wait_send(tsend.at[k, i], phase, i)

    out_sg.wait()
    out_gin.wait()


def body(inputs, cotangent, spectral_weight, point_weight, bias):
    any_spec = pl.BlockSpec(memory_space=pl.ANY)
    vmem = pl.BlockSpec(memory_space=pltpu.VMEM)
    smem = pl.BlockSpec(memory_space=pltpu.SMEM)
    consts = [jnp.asarray(t) for t in tables()]
    field = (C, TY, TX)
    grad_input, spectral_grad, pointwise_grad, bias_grad = pl.pallas_call(
        kernel,
        out_shape=(
            jax.ShapeDtypeStruct(field, BF),
            jax.ShapeDtypeStruct((2, 8, 8, C * C), F32),
            jax.ShapeDtypeStruct((C, C), F32),
            jax.ShapeDtypeStruct((1, C), F32),
        ),
        in_specs=[any_spec, any_spec, any_spec, vmem, smem] + [any_spec] * 6,
        out_specs=(any_spec, any_spec, vmem, vmem),
        scratch_shapes=[
            pltpu.VMEM(field, BF),
            pltpu.VMEM(field, BF),
            pltpu.VMEM((2, 8, 8, C * C), BF),
            *[pltpu.VMEM(t.shape, BF) for t in consts],
            pltpu.VMEM((4, N, 4, TY, TX), BF),
            pltpu.VMEM((4, N, 16, 256), BF),
            pltpu.VMEM((4, N, 8, 128), F32),
            pltpu.VMEM((2, N, 4, TY, TX), BF),
            pltpu.VMEM((4, N, 16, 256), BF),
            pltpu.VMEM((4, N, 8, 128), F32),
            pltpu.VMEM((N, 8, 128), F32),
            pltpu.VMEM((4, N, 8, 128), F32),
            pltpu.VMEM((1024, 512), BF),
            pltpu.VMEM(field, BF),
            pltpu.VMEM((1024, 512), BF),
            pltpu.VMEM((2, 1024, 1024), BF),
            pltpu.VMEM(field, F32),
            pltpu.VMEM(field, F32),
            pltpu.VMEM((72, 1024), F32),
            pltpu.VMEM((128, C * C), F32),
            pltpu.VMEM((2, 8, 8, C * C), F32),
            pltpu.VMEM(field, BF),
            pltpu.SemaphoreType.DMA((15, N)),
            pltpu.SemaphoreType.DMA((15, N)),
            pltpu.SemaphoreType.DMA((10,)),
        ],
        compiler_params=pltpu.CompilerParams(
            collective_id=0, has_side_effects=True, vmem_limit_bytes=52 * 1024 * 1024
        ),
    )(inputs, cotangent, spectral_weight, point_weight, bias, *consts)
    return grad_input, spectral_grad, pointwise_grad, bias_grad.reshape(C)


def solution(mesh):
    in_specs = (P(None, "row", "col"), P(None, "row", "col"), P(None, "row", "col", None), P(), P())
    out_specs = (P(None, "row", "col"), P(None, "row", "col", None), P(), P())
    return jax.shard_map(body, mesh=mesh, in_specs=in_specs, out_specs=out_specs, check_vma=False)
```

```python
import functools
import math

import jax
import jax.numpy as jnp
import ml_dtypes
import numpy as np
from jax import lax
from jax.experimental import pallas as pl
from jax.experimental.pallas import tpu as pltpu
from jax.sharding import PartitionSpec as P

C = 64
K1 = 128
K2 = 128
NY = 1024
NX = 2048
TY = 64
TX = 128
N = 16
SCALE = float(NY * NX) ** (-0.5)
MESH = pl.DeviceIdType.MESH
VMEM_BYTES = 60 * 1024 * 1024
BF = jnp.bfloat16
F32 = jnp.float32

CHIPS = ((1, 2), (0, 1), (0, 3), (1, 1), (0, 2), (1, 0), (1, 3), (0, 0))
COL_ORDER = ((1, 2, 0), (0, 1, 0), (1, 2, 1), (0, 3, 0), (0, 1, 1), (1, 1, 0), (0, 3, 1), (0, 2, 0), (1, 1, 1), (1, 0, 0))
COL_ORDER += ((0, 2, 1), (1, 3, 0), (1, 0, 1), (1, 3, 1), (0, 0, 1))
ROW_ORDER = tuple((x, z) for z in (4, 3, 5, 2, 6, 1, 7, 0) for x in (0, 1) if (x, z) != (0, 0))

X1, Y1, T1, T2, Y2, X2, X3, Y3, T3, T4, Y4, X4, Z1, Z2, Z3 = range(15)


def trig(first, second, total):
    phase = np.mod(first[:, None] * second[None, :], total).astype(np.float32) * np.float32(
        2.0 * math.pi / total
    )
    return np.cos(phase).astype(ml_dtypes.bfloat16), np.sin(phase).astype(ml_dtypes.bfloat16)


@functools.cache
def tables():
    cos, sin = trig(np.arange(K2), np.arange(NX), NX)
    tx = np.stack([cos.reshape(N, 8, NX), -sin.reshape(N, 8, NX)], 1).reshape(2 * K2, 8, NX // 8)
    tx = tx.transpose(1, 0, 2)
    cos, sin = trig(np.arange(K1) - K1 // 2, np.arange(NY), NY)
    ty = np.stack([cos.reshape(K1, N, TY), sin.reshape(K1, N, TY)], 2).reshape(K1, 8, 256)
    ty = ty.transpose(1, 0, 2).reshape(4, 256, 256)
    tyi = np.concatenate([cos, sin], 0).reshape(2 * K1, 4, 256).transpose(1, 0, 2)
    return np.ascontiguousarray(np.concatenate([tx, ty, tyi], 0))


def dot(a, b):
    return lax.dot_general(a, b, (((1,), (0,)), ((), ())), preferred_element_type=F32)


def dot_t(a, b):
    return lax.dot_general(a, b, (((1,), (1,)), ((), ())), preferred_element_type=F32)


def normal_slope(value):
    cumul = 0.5 * (1.0 + lax.erf(value * (1.0 / math.sqrt(2.0))))
    dens = jnp.exp(-0.5 * value * value) * (1.0 / math.sqrt(2.0 * math.pi))
    return cumul + value * dens


def kernel(
    inp, cot, w, pw_hbm, bias_hbm, tab,
    gin, ug, zsum,
    pw, bias, inp_v, cot_v, w_v, tab_v, e1_v, e_v, sel_v,
    xr, yr, tr, xsend, ysend, tsend,
    zsend, zr, f2_v, dz_v, dz2_v, kron_v, zp_v, gz_v, s_v, ug_v, gin_v,
    send_sem, recv_sem, loc_sem,
):
    row = lax.axis_index("row")
    col = lax.axis_index("col")
    col_x, col_y, col_c = lax.div(col, 8), lax.rem(lax.div(col, 2), 4), lax.rem(col, 2)
    lane_lo = lax.broadcasted_iota(jnp.int32, (16, 128), 1) < 64
    mask_j = (lax.broadcasted_iota(jnp.int32, (8, 8, 128), 2) & 7) == lax.broadcasted_iota(
        jnp.int32, (8, 8, 128), 0
    )

    def wrap(i):
        return lax.rem(i, N)

    def remote(src, dst, phase, to, slot, device):
        return pltpu.make_async_remote_copy(
            src_ref=src,
            dst_ref=dst,
            send_sem=send_sem.at[phase, to],
            recv_sem=recv_sem.at[phase, slot],
            device_id=device,
            device_id_type=MESH,
        )

    def wait_recv(dst, phase, slot):
        remote(dst, dst, phase, slot, slot, (row, col)).wait_recv()

    pending = []

    def finish():
        for wait in pending:
            wait()

    def sent(src_of, phase, own):
        def wait():
            @pl.loop(1, N)
            def _(d):
                to = wrap(own + d)
                remote(src_of(to), src_of(to), phase, to, to, (row, col)).wait_send()

        pending.append(wait)

    def row_partner(x, z):
        z = jnp.where(col_c == 0, z, 8 - z)
        return 8 * (lax.div(row, 8) ^ x) + lax.rem(lax.rem(row, 8) + z, 8)

    def col_partner(x, y, c, own_core):
        y = jnp.where(own_core == 0, y, 4 - y)
        return 8 * (col_x ^ x) + 2 * lax.rem(col_y + y, 4) + (col_c ^ c)

    def send_row(src_of, dst, phase, slot):
        for x, z in ROW_ORDER:
            r = row_partner(x, z)
            remote(src_of(r), dst.at[slot], phase, r, slot, (r, col)).start()

        sent(src_of, phase, row)

    def send_block(src, dst, m, phase):
        remote(src, dst.at[col], phase, m, col, (row, m)).start()

    def send_col(src_of, dst, phase):
        for x, y, c in COL_ORDER:
            m = col_partner(x, y, c, col_c)
            send_block(src_of(m), dst, m, phase)

        sent(src_of, phase, col)

    def wait_all(dst, phase, own):
        @pl.loop(1, N)
        def _(d):
            slot = wrap(own + d)
            wait_recv(dst.at[slot], phase, slot)

    block = wrap(row + col)
    top = row == 0

    def send_t(src, dst, phase, to_modes):
        own = row if to_modes else col

        @pl.loop(0, N)
        def _(i):
            @pl.when(jnp.logical_not(jnp.logical_and(top, i == own)))
            def _():
                if to_modes:
                    remote(src.at[i], dst.at[col], phase, i, col, (i, block)).start()
                else:
                    target = (wrap(col + N - i), i)
                    remote(src.at[i], dst.at[row], phase, i, row, target).start()

        @pl.when(top)
        def _():
            dst[col if to_modes else row] = src[own]

        def wait():
            @pl.loop(0, N)
            def _(i):
                @pl.when(jnp.logical_not(jnp.logical_and(top, i == own)))
                def _():
                    remote(src.at[i], src.at[i], phase, i, i, (row, col)).wait_send()

        pending.append(wait)

    def wait_t(dst, phase, to_modes):
        own = col if to_modes else row

        @pl.loop(0, N)
        def _(i):
            @pl.when(jnp.logical_not(jnp.logical_and(top, i == own)))
            def _():
                wait_recv(dst.at[i], phase, i)

    barrier = pltpu.get_barrier_semaphore()

    @pl.loop(1, N)
    def _(d):
        pl.semaphore_signal(barrier, inc=1, device_id=(row, wrap(col + d)), device_id_type=MESH)
        pl.semaphore_signal(barrier, inc=1, device_id=(wrap(row + d), col), device_id_type=MESH)

    @pl.loop(0, N)
    def _(i):
        @pl.when(jnp.logical_not(jnp.logical_and(top, i == row)))
        def _():
            pl.semaphore_signal(barrier, inc=1, device_id=(i, block), device_id_type=MESH)

        @pl.when(jnp.logical_not(jnp.logical_and(top, i == col)))
        def _():
            target = (wrap(col + N - i), i)
            pl.semaphore_signal(barrier, inc=1, device_id=target, device_id_type=MESH)

    loads = [
        pltpu.make_async_copy(src, dst, loc_sem.at[i])
        for i, (src, dst) in enumerate(
            [
                (pw_hbm, pw),
                (bias_hbm, bias),
                (inp, inp_v),
                (tab, tab_v),
                (inp.at[pl.ds(4 * col, 4)], xr.at[0, col]),
                (w, w_v),
                (cot, cot_v),
            ]
        )
    ]
    for load in loads:
        load.start()
    pl.semaphore_wait(barrier, jnp.where(top, 4 * N - 4, 4 * N - 2))

    send_col(lambda m: inp.at[pl.ds(4 * m, 4)], xr.at[0], X1)

    def pack(src, dst):
        for b in range(4):
            dst[:, 128 * b : 128 * b + 128] = src[:, 16 * b : 16 * b + 16, :].reshape(1024, 128)

    def build_kron(which):
        @pl.loop(0, 4)
        def _(i):
            rows = pl.ds(pl.multiple_of(256 * i, 256), 256)
            part = (dot_t if which == 0 else dot)(sel_v[rows, :], pw[...]).astype(BF)
            for j in range(4):
                full = dot_t(part, sel_v[256 * j : 256 * j + 256, :])
                same = (lax.broadcasted_iota(jnp.int32, (256, 256), 0) & 15) == (
                    lax.broadcasted_iota(jnp.int32, (256, 256), 1) & 15
                )
                kron_v[which, rows, 256 * j : 256 * j + 256] = jnp.where(same, full, 0.0).astype(BF)

    def apply_kron(which, src, dst):
        @pl.loop(0, 4)
        def _(i):
            rows = pl.ds(pl.multiple_of(256 * i, 256), 256)
            out = pl.ds(pl.multiple_of(16 * i, 16), 16)
            for h in range(2):
                res = dot(kron_v[which, rows, :], src[:, 256 * h : 256 * h + 256])
                for t in range(2):
                    y = 32 * h + 16 * t
                    dst[out, y : y + 16, :] = res[:, 128 * t : 128 * t + 128].reshape(16, 16, 128)

    def forward_x(src, phase, dst):
        acc = jnp.zeros((256, 256), F32)
        for x, y in CHIPS:
            chip = 4 * (col_x ^ x) + lax.rem(col_y + y, 4)
            blocks = []
            for c in range(2):
                slot = 2 * chip + c

                @pl.when(slot != col)
                def _(slot=slot):
                    wait_recv(src.at[slot], phase, slot)

                blocks.append(src[slot].reshape(256, 128))
            acc = acc + dot_t(tab_v[chip], jnp.concatenate(blocks, 1))
        dst[...] = acc.astype(BF).reshape(N, 16, 256)

    def forward_y(src, dst):
        acc = jnp.zeros((K1, 64), F32)
        for q in range(4):
            parts = []
            for t in range(4):
                b = src[4 * q + t].astype(F32)
                jb = jnp.concatenate([b[8:16], -b[0:8]], 0)
                rows = []
                for h in range(2):
                    bh = b[:, 128 * h : 128 * h + 128]
                    jh = jb[:, 128 * h : 128 * h + 128]
                    rows.append(jnp.where(lane_lo, bh, pltpu.roll(jh, 64, 1)))
                    rows.append(jnp.where(lane_lo, pltpu.roll(bh, 64, 1), jh))
                parts.append(jnp.concatenate(rows, 0).astype(BF))
            for h in range(2):
                table = tab_v[8 + q, 128 * h : 128 * h + 128, :]
                acc = acc + dot_t(table, jnp.concatenate(parts[2 * h : 2 * h + 2], 1))
        res = (acc * SCALE).astype(BF).astype(F32)
        res = res.reshape(N, 8, 64)
        dst[...] = jnp.concatenate([res[:, 0:4], res[:, 4:8]], 2)

    def unpack_t(src):
        x = src[...]
        x = jnp.concatenate([x, pltpu.roll(x, 64, 2)], 1)
        return x.reshape(128, 128).T

    def to_modes(src):
        xt = unpack_t(src)
        rows = []
        for ri in range(2):
            cols = []
            for c in range(4):
                at = (2 * c + ri) * 8
                tile = xt[at : at + 8]
                cols.append(jnp.where(mask_j, tile[None], 0.0).reshape(64, 128))
            rows.append(jnp.concatenate(cols, 1))
        return dot(jnp.concatenate(rows, 0).astype(BF), e1_v[...])

    def from_modes(spec, dst):
        full = dot_t(spec.astype(BF), e1_v[...])
        tiles = []
        for c in range(4):
            for ri in range(2):
                part = full[64 * ri : 64 * ri + 64, 128 * c : 128 * c + 128].reshape(8, 8, 128)
                tiles.append(jnp.sum(jnp.where(mask_j, part, 0.0), axis=0))
        xt = jnp.concatenate(tiles + [jnp.zeros((64, 128), F32)], 0)
        x = xt.T.reshape(N, 8, 128)
        dst[...] = jnp.concatenate([x[:, 0:4, 0:64], x[:, 4:8, 0:64]], 2)

    def inverse_y(src, dst):
        ht = unpack_t(src)
        first, second = [], []
        for c in range(4):
            hr, hi = ht[16 * c : 16 * c + 8], ht[16 * c + 8 : 16 * c + 16]
            first += [hr, hi]
            second += [-hi, hr]
        h = jnp.concatenate([jnp.concatenate(first, 0), jnp.concatenate(second, 0)], 1).astype(BF)
        d = jnp.concatenate([dot(h, tab_v[12 + i]) for i in range(4)], 1)
        for a in range(8):
            for p in range(2):
                t0 = d[32 * p : 32 * p + 16, 128 * a : 128 * a + 128]
                t1 = d[32 * p + 16 : 32 * p + 32, 128 * a : 128 * a + 128]
                at = slice(128 * p, 128 * p + 128)
                dst[2 * a, :, at] = jnp.where(lane_lo, t0, pltpu.roll(t1, 64, 1)).astype(BF)
                dst[2 * a + 1, :, at] = jnp.where(lane_lo, pltpu.roll(t0, 64, 1), t1).astype(BF)

    def inverse_x(src, out, dst, phase):
        yt = src[...].reshape(256, 256).astype(F32).T.astype(BF)
        late = None
        for x, y in CHIPS:
            chip = 4 * (col_x ^ x) + lax.rem(col_y + jnp.where(col_c == 0, y, 4 - y), 4)
            res = (dot(yt, tab_v[chip]) * SCALE).astype(BF)
            for c in range(2):
                out[2 * chip + c] = res[:, 128 * c : 128 * c + 128].reshape(4, TY, TX)
            m = 2 * chip + col_c
            if (x, y) != (0, 0):
                send_block(out.at[m], dst, m, phase)
            else:
                dst[m] = out[m]
            if late is not None:
                send_block(out.at[late], dst, late, phase)
            late = m ^ 1
        send_block(out.at[late], dst, late, phase)

        sent(lambda m: out.at[m], phase, col)

    lane = lax.broadcasted_iota(jnp.int32, (1024, 64), 1)
    first = lax.broadcasted_iota(jnp.int32, (1024, 64), 0)
    sel_v[...] = jnp.where((first >> 4) == lane, 1.0, 0.0).astype(BF)
    zsend[...] = jnp.zeros_like(zsend)
    loads[0].wait()
    build_kron(0)
    loads[2].wait()
    pack(inp_v, f2_v)
    apply_kron(0, f2_v, zp_v)
    first, lane = first[0:512], lane[0:512]
    at = (((first >> 3) & 15) << 2) + (first >> 7)
    e1_v[...] = jnp.where(at == lane, 1.0, 0.0).astype(BF)

    @pl.loop(0, 8)
    def _(i):
        channel = (lax.broadcasted_iota(jnp.int32, (64, 512), 1) >> 6) + 8 * i
        own = lax.broadcasted_iota(jnp.int32, (64, 512), 0)
        at = pl.ds(pl.multiple_of(i * 512, 512), 512)
        e_v[:, at] = jnp.where(channel == own, 1.0, 0.0).astype(BF)

    loads[3].wait()
    loads[4].wait()
    forward_x(xr.at[0], X1, ysend.at[0])
    send_row(lambda r: ysend.at[0, wrap(r + col)], yr.at[0], Y1, row)
    yr[0, row] = ysend[0, block]
    build_kron(1)
    wait_all(yr.at[0], Y1, row)
    forward_y(yr.at[0], tsend.at[0])
    send_t(tsend.at[0], tr.at[0], T1, True)
    loads[5].wait()
    wait_t(tr.at[0], T1, True)

    u = to_modes(tr.at[0])
    ug_v[0] = u
    u = u.astype(BF)

    def fold(t):
        return t[:, 0:128] + t[:, 128:256] + t[:, 256:384] + t[:, 384:512]

    def mix(i, carry):
        sr, si = carry
        at = pl.ds(pl.multiple_of(i * 512, 512), 512)
        ue = dot(u, e_v[:, at])
        ur, ui = ue[0:64], ue[64:128]
        wr = w_v[0, :, :, at].astype(F32).reshape(64, 512)
        wi = w_v[1, :, :, at].astype(F32).reshape(64, 512)
        return sr + fold(wr * ur - wi * ui), si + fold(wr * ui + wi * ur)

    zero = jnp.zeros((64, 128), F32)
    sr, si = lax.fori_loop(0, 8, mix, (zero, zero))
    both = jnp.concatenate([sr, si], 0)
    both = both + pltpu.roll(both, 64, 1)
    from_modes(both[:, 0:64], tsend.at[1])
    send_t(tsend.at[1], tr.at[1], T2, False)

    wait_t(tr.at[1], T2, False)
    inverse_y(tr.at[1], ysend.at[1])
    send_row(lambda r: ysend.at[1, r], yr.at[1], Y2, block)
    yr[1, block] = ysend[1, row]
    wait_all(yr.at[1], Y2, block)
    inverse_x(yr.at[1], xsend.at[0], xr.at[1], X2)

    loads[1].wait()
    loads[6].wait()
    def slope(m):
        for c in range(4):
            z = xr[1, m, c].astype(F32) + zp_v[4 * m + c] + bias[4 * m + c]
            dz = cot_v[4 * m + c].astype(F32) * normal_slope(z)
            dz_v[4 * m + c] = dz.astype(BF)

    slope(col)
    xr[2, col] = dz_v[pl.ds(4 * col, 4)]
    for x, y, c in COL_ORDER:
        m = col_partner(x, 4 - y, c, col_c ^ c)
        wait_recv(xr.at[1, m], X2, m)
        slope(m)
        send_block(dz_v.at[pl.ds(4 * m, 4)], xr.at[2], m, X3)
    sent(lambda m: dz_v.at[pl.ds(4 * m, 4)], X3, col)

    pack(dz_v, dz2_v)

    @pl.loop(0, 4)
    def _(o):
        cols = pl.ds(pl.multiple_of(256 * o, 256), 256)
        dzo = dz2_v[cols, :]
        same = (lax.broadcasted_iota(jnp.int32, (256, 256), 0) & 15) == (
            lax.broadcasted_iota(jnp.int32, (256, 256), 1) & 15
        )
        for i in range(4):
            prod = dot_t(f2_v[256 * i : 256 * i + 256, :], dzo)
            prod = jnp.where(same, prod, 0.0).reshape(16, 16, 256)
            s_v[16 * i : 16 * i + 16, cols] = jnp.sum(prod, axis=1)
        s_v[64:72, cols] = dot_t(jnp.ones((16, 512), BF), dzo)[0:8]

    terms = s_v[...]
    high = terms.astype(BF)
    low = (terms - high.astype(F32)).astype(BF)
    terms = dot(high, sel_v[...]) + dot(low, sel_v[...])
    zsend[:, 0:4, 0:64] = terms[0:64].reshape(N, 4, 64)
    zsend[0, 4:5, 0:64] = terms[64:65]
    send_col(lambda m: zsend.at[m], zr.at[0], Z1)
    zr[0, col] = zsend[col]
    apply_kron(1, dz2_v, gz_v)

    forward_x(xr.at[2], X3, ysend.at[2])
    send_row(lambda r: ysend.at[2, wrap(r + col)], yr.at[2], Y3, row)
    yr[2, row] = ysend[2, block]
    wait_all(yr.at[2], Y3, row)
    forward_y(yr.at[2], tsend.at[2])
    send_t(tsend.at[2], tr.at[2], T3, True)
    wait_all(zr.at[0], Z1, col)
    zr[3, 0] = jnp.sum(zr[0], axis=0)
    send_row(lambda r: zr.at[3, 0], zr.at[1], Z2, row)
    zr[1, row] = zr[3, 0]
    wait_t(tr.at[2], T3, True)

    g = to_modes(tr.at[2])
    ug_v[1] = g
    g = jnp.concatenate([g, g], 1)
    gr, gi = g[0:64], g[64:128]
    gr4, gi4 = jnp.concatenate([gr] * 4, 1), jnp.concatenate([gi] * 4, 1)

    def mix_back(i, acc):
        at = pl.ds(pl.multiple_of(i * 512, 512), 512)
        wr = w_v[0, :, :, at].astype(F32).reshape(64, 512)
        wi = w_v[1, :, :, at].astype(F32).reshape(64, 512)
        both = jnp.concatenate([wr * gr4 + wi * gi4, wr * gi4 - wi * gr4], 0).astype(BF)
        return acc + dot_t(both, e_v[:, at])

    du = lax.fori_loop(0, 8, mix_back, jnp.zeros((128, 64), F32))
    from_modes(du, tsend.at[3])
    send_t(tsend.at[3], tr.at[3], T4, False)

    wait_all(zr.at[1], Z2, row)
    zr[3, 1] = jnp.sum(zr[1], axis=0)
    send_col(lambda m: zr.at[3, 1], zr.at[2], Z3)
    zr[2, col] = zr[3, 1]
    out_ug = pltpu.make_async_copy(ug_v, ug, loc_sem.at[0])
    out_ug.start()

    wait_t(tr.at[3], T4, False)
    inverse_y(tr.at[3], ysend.at[3])
    send_row(lambda r: ysend.at[3, r], yr.at[3], Y4, block)
    yr[3, block] = ysend[3, row]
    wait_all(zr.at[2], Z3, col)
    out_z = pltpu.make_async_copy(zr.at[2], zsum, loc_sem.at[2])
    out_z.start()
    pending.append(out_z.wait)
    wait_all(yr.at[3], Y4, block)
    inverse_x(yr.at[3], xsend.at[1], xr.at[3], X4)
    def finish_block(m):
        at = pl.ds(4 * m, 4)
        gin_v[at] = (xr[3, m].astype(F32) + gz_v[at]).astype(BF)

    finish_block(col)
    for x, y, c in COL_ORDER:
        m = col_partner(x, 4 - y, c, col_c ^ c)
        wait_recv(xr.at[3, m], X4, m)
        finish_block(m)

    out_gin = pltpu.make_async_copy(gin_v, gin, loc_sem.at[1])
    out_gin.start()

    pending.append(out_ug.wait)
    pending.append(out_gin.wait)
    finish()


def last_kernel(gin, ug, zsum, gin_out, sg, pg, bg):
    step = pl.program_id(0)
    gin_out[...] = gin[...]

    @pl.when(step == 0)
    def _():
        pg[...] = zsum[:, 0:4, 0:64].reshape(C, C) * SCALE
        bg[...] = zsum[0, 4:5, 0:64] * SCALE

    channel = (lax.broadcasted_iota(jnp.int32, (64, 1024), 1) >> 6) + 16 * step
    own = lax.broadcasted_iota(jnp.int32, (64, 1024), 0)
    ue = dot(ug[0].astype(BF), jnp.where(channel == own, 1.0, 0.0).astype(BF))
    g = jnp.concatenate([ug[1]] * 16, 1)
    ur, ui, gr, gi = ue[0:64], ue[64:128], g[0:64], g[64:128]
    sg[0] = (gr * ur + gi * ui).reshape(8, 8, 1024)
    sg[1] = (gi * ur - gr * ui).reshape(8, 8, 1024)


def body(inputs, cotangent, spectral_weight, point_weight, bias):
    any_spec = pl.BlockSpec(memory_space=pl.ANY)
    field = (C, TY, TX)
    table = jnp.asarray(tables())
    grad_input, modes, sums = pl.pallas_call(
        kernel,
        out_shape=(
            jax.ShapeDtypeStruct(field, BF),
            jax.ShapeDtypeStruct((2, 128, C), F32),
            jax.ShapeDtypeStruct((N, 8, 128), F32),
        ),
        in_specs=[any_spec] * 6,
        out_specs=(any_spec, any_spec, any_spec),
        scratch_shapes=[
            pltpu.VMEM((C, C), BF),
            pltpu.SMEM((C,), F32),
            pltpu.VMEM(field, BF),
            pltpu.VMEM(field, BF),
            pltpu.VMEM((2, 8, 8, C * C), BF),
            pltpu.VMEM(table.shape, BF),
            pltpu.VMEM((512, 64), BF),
            pltpu.VMEM((64, C * C), BF),
            pltpu.VMEM((1024, 64), BF),
            pltpu.VMEM((4, N, 4, TY, TX), BF),
            pltpu.VMEM((4, N, 16, 256), BF),
            pltpu.VMEM((4, N, 4, 128), F32),
            pltpu.VMEM((2, N, 4, TY, TX), BF),
            pltpu.VMEM((4, N, 16, 256), BF),
            pltpu.VMEM((4, N, 4, 128), F32),
            pltpu.VMEM((N, 8, 128), F32),
            pltpu.VMEM((4, N, 8, 128), F32),
            pltpu.VMEM((1024, 512), BF),
            pltpu.VMEM(field, BF),
            pltpu.VMEM((1024, 512), BF),
            pltpu.VMEM((2, 1024, 1024), BF),
            pltpu.VMEM(field, F32),
            pltpu.VMEM(field, F32),
            pltpu.VMEM((72, 1024), F32),
            pltpu.VMEM((2, 128, C), F32),
            pltpu.VMEM(field, BF),
            pltpu.SemaphoreType.DMA((15, N)),
            pltpu.SemaphoreType.DMA((15, N)),
            pltpu.SemaphoreType.DMA((10,)),
        ],
        compiler_params=pltpu.CompilerParams(
            collective_id=0, has_side_effects=True, vmem_limit_bytes=VMEM_BYTES
        ),
    )(inputs, cotangent, spectral_weight, point_weight, bias, table)
    channels = pl.BlockSpec((C // 4, TY, TX), lambda i: (i, 0, 0))
    whole = lambda shape: pl.BlockSpec(shape, lambda i: (0,) * len(shape))
    grad_input, spectral_grad, pointwise_grad, bias_grad = pl.pallas_call(
        last_kernel,
        grid=(4,),
        out_shape=(
            jax.ShapeDtypeStruct(field, BF),
            jax.ShapeDtypeStruct((2, 8, 8, C * C), F32),
            jax.ShapeDtypeStruct((C, C), F32),
            jax.ShapeDtypeStruct((1, C), F32),
        ),
        in_specs=[channels, whole((2, 128, C)), whole((N, 8, 128))],
        out_specs=(
            channels,
            pl.BlockSpec((2, 8, 8, 1024), lambda i: (0, 0, 0, i)),
            whole((C, C)),
            whole((1, C)),
        ),
    )(grad_input, modes, sums)
    return grad_input, spectral_grad, pointwise_grad, bias_grad.reshape(C)


def solution(mesh):
    in_specs = (P(None, "row", "col"), P(None, "row", "col"), P(None, "row", "col", None), P(), P())
    out_specs = (P(None, "row", "col"), P(None, "row", "col", None), P(), P())
    return jax.shard_map(body, mesh=mesh, in_specs=in_specs, out_specs=out_specs, check_vma=False)
```

```python
import functools
import math

import jax
import jax.numpy as jnp
import ml_dtypes
import numpy as np
from jax import lax
from jax.experimental import pallas as pl
from jax.experimental.pallas import tpu as pltpu
from jax.sharding import PartitionSpec as P

C = 64
K1 = 128
K2 = 128
NY = 1024
NX = 2048
TY = 64
TX = 128
N = 16
SCALE = float(NY * NX) ** (-0.5)
MESH = pl.DeviceIdType.MESH
VMEM_BYTES = 60 * 1024 * 1024
BF = jnp.bfloat16
F32 = jnp.float32

CHIPS = ((1, 2), (0, 1), (0, 3), (1, 1), (0, 2), (1, 0), (1, 3), (0, 0))
COL_ORDER = ((1, 2, 0), (0, 1, 0), (1, 2, 1), (0, 3, 0), (0, 1, 1), (1, 1, 0), (0, 3, 1), (0, 2, 0), (1, 1, 1), (1, 0, 0))
COL_ORDER += ((0, 2, 1), (1, 3, 0), (1, 0, 1), (1, 3, 1), (0, 0, 1))
ROW_ORDER = tuple((x, z) for z in (4, 3, 5, 2, 6, 1, 7, 0) for x in (0, 1) if (x, z) != (0, 0))

X1, Y1, T1, T2, Y2, X2, X3, Y3, T3, T4, Y4, X4, Z1, Z2, Z3 = range(15)


def trig(first, second, total):
    phase = np.mod(first[:, None] * second[None, :], total).astype(np.float32) * np.float32(
        2.0 * math.pi / total
    )
    return np.cos(phase).astype(ml_dtypes.bfloat16), np.sin(phase).astype(ml_dtypes.bfloat16)


@functools.cache
def tables():
    cos, sin = trig(np.arange(K2), np.arange(NX), NX)
    tx = np.stack([cos.reshape(N, 8, NX), -sin.reshape(N, 8, NX)], 1).reshape(2 * K2, 8, NX // 8)
    tx = tx.transpose(1, 0, 2)
    cos, sin = trig(np.arange(K1) - K1 // 2, np.arange(NY), NY)
    ty = np.stack([cos.reshape(K1, N, TY), sin.reshape(K1, N, TY)], 2).reshape(K1, 8, 256)
    ty = ty.transpose(1, 0, 2).reshape(4, 256, 256)
    tyi = np.concatenate([cos, sin], 0).reshape(2 * K1, 4, 256).transpose(1, 0, 2)
    return np.ascontiguousarray(np.concatenate([tx, ty, tyi], 0))


def dot(a, b):
    return lax.dot_general(a, b, (((1,), (0,)), ((), ())), preferred_element_type=F32)


def dot_t(a, b):
    return lax.dot_general(a, b, (((1,), (1,)), ((), ())), preferred_element_type=F32)


def normal_slope(value):
    cumul = 0.5 * (1.0 + lax.erf(value * (1.0 / math.sqrt(2.0))))
    dens = jnp.exp(-0.5 * value * value) * (1.0 / math.sqrt(2.0 * math.pi))
    return cumul + value * dens


def kernel(
    inp, cot, w, pw_hbm, bias_hbm, tab,
    gin, ug, zsum,
    pw, bias, inp_v, cot_v, w_v, tab_v, e1_v, e_v, sel_v,
    xr, yr, tr, xsend, ysend, tsend,
    zsend, zr, f2_v, dz_v, dz2_v, kron_v, zp_v, gz_v, s_v, ug_v, gin_v,
    send_sem, recv_sem, loc_sem,
):
    row = lax.axis_index("row")
    col = lax.axis_index("col")
    col_x, col_y, col_c = lax.div(col, 8), lax.rem(lax.div(col, 2), 4), lax.rem(col, 2)
    lane_lo = lax.broadcasted_iota(jnp.int32, (16, 128), 1) < 64
    mask_j = (lax.broadcasted_iota(jnp.int32, (8, 8, 128), 2) & 7) == lax.broadcasted_iota(
        jnp.int32, (8, 8, 128), 0
    )

    def wrap(i):
        return lax.rem(i, N)

    def remote(src, dst, phase, slot, device):
        return pltpu.make_async_remote_copy(
            src_ref=src,
            dst_ref=dst,
            send_sem=send_sem.at[phase],
            recv_sem=recv_sem.at[phase, slot],
            device_id=device,
            device_id_type=MESH,
        )

    def wait_recv(dst, phase, slot=0):
        remote(dst, dst, phase, slot, (row, col)).wait_recv()

    def wait_sent(like, phase):
        remote(like, like, phase, 0, (row, col)).wait_send()

    def keep(src, dst, phase):
        pltpu.make_async_copy(src, dst, recv_sem.at[phase, 0]).start()

    pending = []

    def finish():
        for wait in pending:
            wait()

    def sent(like, phase):
        pending.append(lambda: wait_sent(like, phase))

    def row_partner(x, z):
        z = jnp.where(col_c == 0, z, 8 - z)
        return 8 * (lax.div(row, 8) ^ x) + lax.rem(lax.rem(row, 8) + z, 8)

    def col_partner(x, y, c, own_core):
        y = jnp.where(own_core == 0, y, 4 - y)
        return 8 * (col_x ^ x) + 2 * lax.rem(col_y + y, 4) + (col_c ^ c)

    def ordered(k):
        words = [0, 0]
        for i, (x, y, c) in enumerate(COL_ORDER):
            words[i // 8] |= (8 * x + 2 * y + c) << (4 * (i % 8))
        words = [w - (1 << 32) if w >> 31 else w for w in words]
        code = (jnp.where(k < 8, words[0], words[1]) >> (4 * lax.rem(k, 8))) & 15
        return code >> 3, (code >> 1) & 3, code & 1

    def send_block(src, dst, m, phase):
        remote(src, dst.at[col], phase, col, (row, m)).start()

    def send_row(src_of, dst, phase, slot, like):
        for x, z in ROW_ORDER:
            r = row_partner(x, z)
            remote(src_of(r), dst.at[slot], phase, 0, (r, col)).start()
        keep(src_of(row), dst.at[slot], phase)
        sent(like, phase)

    def send_col(src_of, dst, phase, like):
        for x, y, c in COL_ORDER:
            m = col_partner(x, y, c, col_c)
            remote(src_of(m), dst.at[col], phase, 0, (row, m)).start()
        keep(src_of(col), dst.at[col], phase)
        sent(like, phase)

    block = wrap(row + col)
    top = row == 0

    def send_t(src, dst, phase, to_modes):
        own = row if to_modes else col
        slot = col if to_modes else row

        @pl.loop(0, N)
        def _(i):
            target = (i, block) if to_modes else (wrap(col + N - i), i)
            is_own = jnp.logical_and(top, i == own)

            @pl.when(jnp.logical_not(is_own))
            def _():
                remote(src.at[i], dst.at[slot], phase, 0, target).start()

            @pl.when(is_own)
            def _():
                keep(src.at[i], dst.at[slot], phase)

        def wait():
            @pl.when(top)
            def _():
                wait_sent(src.at[pl.ds(0, N - 1)], phase)

            @pl.when(jnp.logical_not(top))
            def _():
                wait_sent(src, phase)

        pending.append(wait)

    barrier = pltpu.get_barrier_semaphore()

    @pl.loop(1, N)
    def _(d):
        pl.semaphore_signal(barrier, inc=1, device_id=(row, wrap(col + d)), device_id_type=MESH)
        pl.semaphore_signal(barrier, inc=1, device_id=(wrap(row + d), col), device_id_type=MESH)

    loads = [
        pltpu.make_async_copy(src, dst, loc_sem.at[i])
        for i, (src, dst) in enumerate(
            [
                (pw_hbm, pw),
                (bias_hbm, bias),
                (inp, inp_v),
                (tab, tab_v),
                (inp.at[pl.ds(4 * col, 4)], xr.at[0, col]),
                (w, w_v),
                (cot, cot_v),
            ]
        )
    ]
    for load in loads:
        load.start()
    pl.semaphore_wait(barrier, 2 * N - 2)

    for x, y, c in COL_ORDER:
        m = col_partner(x, y, c, col_c)
        send_block(inp.at[pl.ds(4 * m, 4)], xr.at[0], m, X1)
    sent(inp.at[pl.ds(0, 4 * N - 4)], X1)

    def pack(src, dst):
        for b in range(4):
            dst[:, 128 * b : 128 * b + 128] = src[:, 16 * b : 16 * b + 16, :].reshape(1024, 128)

    def build_kron(which):
        @pl.loop(0, 4)
        def _(i):
            rows = pl.ds(pl.multiple_of(256 * i, 256), 256)
            part = (dot_t if which == 0 else dot)(sel_v[rows, :], pw[...]).astype(BF)
            for j in range(4):
                full = dot_t(part, sel_v[256 * j : 256 * j + 256, :])
                same = (lax.broadcasted_iota(jnp.int32, (256, 256), 0) & 15) == (
                    lax.broadcasted_iota(jnp.int32, (256, 256), 1) & 15
                )
                kron_v[which, rows, 256 * j : 256 * j + 256] = jnp.where(same, full, 0.0).astype(BF)

    def apply_kron(which, src, dst):
        @pl.loop(0, 4)
        def _(i):
            rows = pl.ds(pl.multiple_of(256 * i, 256), 256)
            out = pl.ds(pl.multiple_of(16 * i, 16), 16)
            for h in range(2):
                res = dot(kron_v[which, rows, :], src[:, 256 * h : 256 * h + 256])
                for t in range(2):
                    y = 32 * h + 16 * t
                    dst[out, y : y + 16, :] = res[:, 128 * t : 128 * t + 128].reshape(16, 16, 128)

    def forward_x(src, phase, dst):
        acc = jnp.zeros((256, 256), F32)
        for x, y in CHIPS:
            chip = 4 * (col_x ^ x) + lax.rem(col_y + y, 4)
            blocks = []
            for c in range(2):
                slot = 2 * chip + c

                @pl.when(slot != col)
                def _(slot=slot):
                    wait_recv(src.at[slot], phase, slot)

                blocks.append(src[slot].reshape(256, 128))
            acc = acc + dot_t(tab_v[chip], jnp.concatenate(blocks, 1))
        dst[...] = acc.astype(BF).reshape(N, 16, 256)

    def forward_y(src, dst):
        acc = jnp.zeros((K1, 64), F32)
        for q in range(4):
            parts = []
            for t in range(4):
                b = src[4 * q + t].astype(F32)
                jb = jnp.concatenate([b[8:16], -b[0:8]], 0)
                rows = []
                for h in range(2):
                    bh = b[:, 128 * h : 128 * h + 128]
                    jh = jb[:, 128 * h : 128 * h + 128]
                    rows.append(jnp.where(lane_lo, bh, pltpu.roll(jh, 64, 1)))
                    rows.append(jnp.where(lane_lo, pltpu.roll(bh, 64, 1), jh))
                parts.append(jnp.concatenate(rows, 0).astype(BF))
            for h in range(2):
                table = tab_v[8 + q, 128 * h : 128 * h + 128, :]
                acc = acc + dot_t(table, jnp.concatenate(parts[2 * h : 2 * h + 2], 1))
        res = (acc * SCALE).astype(BF).astype(F32)
        res = res.reshape(N, 8, 64)
        dst[...] = jnp.concatenate([res[:, 0:4], res[:, 4:8]], 2)

    def unpack_t(src):
        x = src[...]
        x = jnp.concatenate([x, pltpu.roll(x, 64, 2)], 1)
        return x.reshape(128, 128).T

    def to_modes(src):
        xt = unpack_t(src)
        rows = []
        for ri in range(2):
            cols = []
            for c in range(4):
                at = (2 * c + ri) * 8
                tile = xt[at : at + 8]
                cols.append(jnp.where(mask_j, tile[None], 0.0).reshape(64, 128))
            rows.append(jnp.concatenate(cols, 1))
        return dot(jnp.concatenate(rows, 0).astype(BF), e1_v[...])

    def from_modes(spec, dst):
        full = dot_t(spec.astype(BF), e1_v[...])
        tiles = []
        for c in range(4):
            for ri in range(2):
                part = full[64 * ri : 64 * ri + 64, 128 * c : 128 * c + 128].reshape(8, 8, 128)
                tiles.append(jnp.sum(jnp.where(mask_j, part, 0.0), axis=0))
        xt = jnp.concatenate(tiles + [jnp.zeros((64, 128), F32)], 0)
        x = xt.T.reshape(N, 8, 128)
        dst[...] = jnp.concatenate([x[:, 0:4, 0:64], x[:, 4:8, 0:64]], 2)

    def inverse_y(src, dst):
        ht = unpack_t(src)
        first, second = [], []
        for c in range(4):
            hr, hi = ht[16 * c : 16 * c + 8], ht[16 * c + 8 : 16 * c + 16]
            first += [hr, hi]
            second += [-hi, hr]
        h = jnp.concatenate([jnp.concatenate(first, 0), jnp.concatenate(second, 0)], 1).astype(BF)
        d = jnp.concatenate([dot(h, tab_v[12 + i]) for i in range(4)], 1)
        for a in range(8):
            for p in range(2):
                t0 = d[32 * p : 32 * p + 16, 128 * a : 128 * a + 128]
                t1 = d[32 * p + 16 : 32 * p + 32, 128 * a : 128 * a + 128]
                at = slice(128 * p, 128 * p + 128)
                dst[2 * a, :, at] = jnp.where(lane_lo, t0, pltpu.roll(t1, 64, 1)).astype(BF)
                dst[2 * a + 1, :, at] = jnp.where(lane_lo, pltpu.roll(t0, 64, 1), t1).astype(BF)

    def inverse_x(src, out, dst, phase):
        yt = src[...].reshape(256, 256).astype(F32).T.astype(BF)
        late = None
        for x, y in CHIPS:
            chip = 4 * (col_x ^ x) + lax.rem(col_y + jnp.where(col_c == 0, y, 4 - y), 4)
            res = (dot(yt, tab_v[chip]) * SCALE).astype(BF)
            for c in range(2):
                out[2 * chip + c] = res[:, 128 * c : 128 * c + 128].reshape(4, TY, TX)
            m = 2 * chip + col_c
            if (x, y) != (0, 0):
                send_block(out.at[m], dst, m, phase)
            else:
                dst[m] = out[m]
            if late is not None:
                send_block(out.at[late], dst, late, phase)
            late = m ^ 1
        send_block(out.at[late], dst, late, phase)

        sent(out.at[pl.ds(0, N - 1)], phase)

    lane = lax.broadcasted_iota(jnp.int32, (1024, 64), 1)
    first = lax.broadcasted_iota(jnp.int32, (1024, 64), 0)
    sel_v[...] = jnp.where((first >> 4) == lane, 1.0, 0.0).astype(BF)
    zsend[...] = jnp.zeros_like(zsend)
    loads[0].wait()
    build_kron(0)
    loads[2].wait()
    pack(inp_v, f2_v)
    apply_kron(0, f2_v, zp_v)
    first, lane = first[0:512], lane[0:512]
    at = (((first >> 3) & 15) << 2) + (first >> 7)
    e1_v[...] = jnp.where(at == lane, 1.0, 0.0).astype(BF)

    @pl.loop(0, 8)
    def _(i):
        channel = (lax.broadcasted_iota(jnp.int32, (64, 512), 1) >> 6) + 8 * i
        own = lax.broadcasted_iota(jnp.int32, (64, 512), 0)
        at = pl.ds(pl.multiple_of(i * 512, 512), 512)
        e_v[:, at] = jnp.where(channel == own, 1.0, 0.0).astype(BF)

    loads[3].wait()
    loads[4].wait()
    forward_x(xr.at[0], X1, ysend.at[0])
    send_row(lambda r: ysend.at[0, wrap(r + col)], yr.at[0], Y1, row, ysend.at[0, pl.ds(0, N - 1)])
    build_kron(1)
    wait_recv(yr.at[0], Y1)
    forward_y(yr.at[0], tsend.at[0])
    send_t(tsend.at[0], tr.at[0], T1, True)
    loads[5].wait()
    wait_recv(tr.at[0], T1)

    u = to_modes(tr.at[0])
    ug_v[0] = u
    u = u.astype(BF)

    def fold(t):
        return t[:, 0:128] + t[:, 128:256] + t[:, 256:384] + t[:, 384:512]

    def mix(i, carry):
        sr, si = carry
        at = pl.ds(pl.multiple_of(i * 512, 512), 512)
        ue = dot(u, e_v[:, at])
        ur, ui = ue[0:64], ue[64:128]
        wr = w_v[0, :, :, at].astype(F32).reshape(64, 512)
        wi = w_v[1, :, :, at].astype(F32).reshape(64, 512)
        return sr + fold(wr * ur - wi * ui), si + fold(wr * ui + wi * ur)

    zero = jnp.zeros((64, 128), F32)
    sr, si = lax.fori_loop(0, 8, mix, (zero, zero))
    both = jnp.concatenate([sr, si], 0)
    both = both + pltpu.roll(both, 64, 1)
    from_modes(both[:, 0:64], tsend.at[1])
    send_t(tsend.at[1], tr.at[1], T2, False)

    wait_recv(tr.at[1], T2)
    inverse_y(tr.at[1], ysend.at[1])
    send_row(lambda r: ysend.at[1, r], yr.at[1], Y2, block, ysend.at[1, pl.ds(0, N - 1)])
    wait_recv(yr.at[1], Y2)
    inverse_x(yr.at[1], xsend.at[0], xr.at[1], X2)

    loads[1].wait()
    loads[6].wait()
    def slope(m):
        for c in range(4):
            z = xr[1, m, c].astype(F32) + zp_v[4 * m + c] + bias[4 * m + c]
            dz = cot_v[4 * m + c].astype(F32) * normal_slope(z)
            dz_v[4 * m + c] = dz.astype(BF)

    slope(col)
    xr[2, col] = dz_v[pl.ds(4 * col, 4)]

    @pl.loop(0, N - 1)
    def _(k):
        x, y, c = ordered(k)
        m = col_partner(x, 4 - y, c, col_c ^ c)
        wait_recv(xr.at[1, m], X2, m)
        slope(m)
        send_block(dz_v.at[pl.ds(4 * m, 4)], xr.at[2], m, X3)

    sent(dz_v.at[pl.ds(0, 4 * N - 4)], X3)

    pack(dz_v, dz2_v)

    @pl.loop(0, 4)
    def _(o):
        cols = pl.ds(pl.multiple_of(256 * o, 256), 256)
        dzo = dz2_v[cols, :]
        same = (lax.broadcasted_iota(jnp.int32, (256, 256), 0) & 15) == (
            lax.broadcasted_iota(jnp.int32, (256, 256), 1) & 15
        )
        for i in range(4):
            prod = dot_t(f2_v[256 * i : 256 * i + 256, :], dzo)
            prod = jnp.where(same, prod, 0.0).reshape(16, 16, 256)
            s_v[16 * i : 16 * i + 16, cols] = jnp.sum(prod, axis=1)
        s_v[64:72, cols] = dot_t(jnp.ones((16, 512), BF), dzo)[0:8]

    terms = s_v[...]
    high = terms.astype(BF)
    low = (terms - high.astype(F32)).astype(BF)
    terms = dot(high, sel_v[...]) + dot(low, sel_v[...])
    zsend[:, 0:4, 0:64] = terms[0:64].reshape(N, 4, 64)
    zsend[0, 4:5, 0:64] = terms[64:65]
    send_col(lambda m: zsend.at[m], zr.at[0], Z1, zsend.at[pl.ds(0, N - 1)])
    apply_kron(1, dz2_v, gz_v)

    forward_x(xr.at[2], X3, ysend.at[2])
    send_row(lambda r: ysend.at[2, wrap(r + col)], yr.at[2], Y3, row, ysend.at[2, pl.ds(0, N - 1)])
    wait_recv(yr.at[2], Y3)
    forward_y(yr.at[2], tsend.at[2])
    send_t(tsend.at[2], tr.at[2], T3, True)
    wait_recv(zr.at[0], Z1)
    zr[3, 0] = jnp.sum(zr[0], axis=0)
    send_row(lambda r: zr.at[3, 0], zr.at[1], Z2, row, zsend.at[pl.ds(0, N - 1)])
    wait_recv(tr.at[2], T3)

    g = to_modes(tr.at[2])
    ug_v[1] = g
    g = jnp.concatenate([g, g], 1)
    gr, gi = g[0:64], g[64:128]
    gr4, gi4 = jnp.concatenate([gr] * 4, 1), jnp.concatenate([gi] * 4, 1)

    def mix_back(i, acc):
        at = pl.ds(pl.multiple_of(i * 512, 512), 512)
        wr = w_v[0, :, :, at].astype(F32).reshape(64, 512)
        wi = w_v[1, :, :, at].astype(F32).reshape(64, 512)
        both = jnp.concatenate([wr * gr4 + wi * gi4, wr * gi4 - wi * gr4], 0).astype(BF)
        return acc + dot_t(both, e_v[:, at])

    du = lax.fori_loop(0, 8, mix_back, jnp.zeros((128, 64), F32))
    from_modes(du, tsend.at[3])
    send_t(tsend.at[3], tr.at[3], T4, False)

    wait_recv(zr.at[1], Z2)
    zr[3, 1] = jnp.sum(zr[1], axis=0)
    send_col(lambda m: zr.at[3, 1], zr.at[2], Z3, zsend.at[pl.ds(0, N - 1)])
    out_ug = pltpu.make_async_copy(ug_v, ug, loc_sem.at[0])
    out_ug.start()

    wait_recv(tr.at[3], T4)
    inverse_y(tr.at[3], ysend.at[3])
    send_row(lambda r: ysend.at[3, r], yr.at[3], Y4, block, ysend.at[3, pl.ds(0, N - 1)])
    wait_recv(zr.at[2], Z3)
    out_z = pltpu.make_async_copy(zr.at[2], zsum, loc_sem.at[2])
    out_z.start()
    pending.append(out_z.wait)
    wait_recv(yr.at[3], Y4)
    inverse_x(yr.at[3], xsend.at[1], xr.at[3], X4)
    def finish_block(m):
        at = pl.ds(4 * m, 4)
        gin_v[at] = (xr[3, m].astype(F32) + gz_v[at]).astype(BF)

    finish_block(col)

    @pl.loop(0, N - 1)
    def _(k):
        x, y, c = ordered(k)
        m = col_partner(x, 4 - y, c, col_c ^ c)
        wait_recv(xr.at[3, m], X4, m)
        finish_block(m)

    out_gin = pltpu.make_async_copy(gin_v, gin, loc_sem.at[1])
    out_gin.start()

    pending.append(out_ug.wait)
    pending.append(out_gin.wait)
    finish()


def last_kernel(gin, ug, zsum, gin_out, sg, pg, bg, gin_v, ug_v, z_v, sg_v, sem):
    pieces = ((ug, ug_v), (gin, gin_v), (zsum, z_v))
    loads = [pltpu.make_async_copy(a, b, sem.at[i]) for i, (a, b) in enumerate(pieces)]
    for load in loads:
        load.start()
    loads[0].wait()
    u = ug_v[0].astype(BF)
    g = jnp.concatenate([ug_v[1]] * 8, 1)
    gr, gi = g[0:64], g[64:128]
    own = lax.broadcasted_iota(jnp.int32, (64, 512), 0)
    group = lax.broadcasted_iota(jnp.int32, (64, 512), 1) >> 6
    out = pltpu.make_async_copy(gin_v, gin_out, sem.at[1])
    for i in range(8):
        at = slice(512 * i, 512 * i + 512)
        ue = dot(u, jnp.where(group + 8 * i == own, 1.0, 0.0).astype(BF))
        ur, ui = ue[0:64], ue[64:128]
        sg_v[0, :, :, at] = (gr * ur + gi * ui).reshape(8, 8, 512)
        sg_v[1, :, :, at] = (gi * ur - gr * ui).reshape(8, 8, 512)
        pltpu.make_async_copy(sg_v.at[:, :, :, at], sg.at[:, :, :, at], sem.at[3]).start()
        if i == 0:
            loads[1].wait()
            out.start()
    loads[2].wait()
    pg[...] = z_v[:, 0:4, 0:64].reshape(C, C) * SCALE
    bg[...] = z_v[0, 4:5, 0:64] * SCALE
    pltpu.make_async_copy(sg_v, sg, sem.at[3]).wait()
    out.wait()


def body(inputs, cotangent, spectral_weight, point_weight, bias):
    any_spec = pl.BlockSpec(memory_space=pl.ANY)
    field = (C, TY, TX)
    table = jnp.asarray(tables())
    grad_input, modes, sums = pl.pallas_call(
        kernel,
        out_shape=(
            jax.ShapeDtypeStruct(field, BF),
            jax.ShapeDtypeStruct((2, 128, C), F32),
            jax.ShapeDtypeStruct((N, 8, 128), F32),
        ),
        in_specs=[any_spec] * 6,
        out_specs=(any_spec, any_spec, any_spec),
        scratch_shapes=[
            pltpu.VMEM((C, C), BF),
            pltpu.SMEM((C,), F32),
            pltpu.VMEM(field, BF),
            pltpu.VMEM(field, BF),
            pltpu.VMEM((2, 8, 8, C * C), BF),
            pltpu.VMEM(table.shape, BF),
            pltpu.VMEM((512, 64), BF),
            pltpu.VMEM((64, C * C), BF),
            pltpu.VMEM((1024, 64), BF),
            pltpu.VMEM((4, N, 4, TY, TX), BF),
            pltpu.VMEM((4, N, 16, 256), BF),
            pltpu.VMEM((4, N, 4, 128), F32),
            pltpu.VMEM((2, N, 4, TY, TX), BF),
            pltpu.VMEM((4, N, 16, 256), BF),
            pltpu.VMEM((4, N, 4, 128), F32),
            pltpu.VMEM((N, 8, 128), F32),
            pltpu.VMEM((4, N, 8, 128), F32),
            pltpu.VMEM((1024, 512), BF),
            pltpu.VMEM(field, BF),
            pltpu.VMEM((1024, 512), BF),
            pltpu.VMEM((2, 1024, 1024), BF),
            pltpu.VMEM(field, F32),
            pltpu.VMEM(field, F32),
            pltpu.VMEM((72, 1024), F32),
            pltpu.VMEM((2, 128, C), F32),
            pltpu.VMEM(field, BF),
            pltpu.SemaphoreType.DMA((15,)),
            pltpu.SemaphoreType.DMA((15, N)),
            pltpu.SemaphoreType.DMA((10,)),
        ],
        compiler_params=pltpu.CompilerParams(
            collective_id=0, has_side_effects=True, vmem_limit_bytes=VMEM_BYTES
        ),
    )(inputs, cotangent, spectral_weight, point_weight, bias, table)
    whole = lambda shape: pl.BlockSpec(shape, lambda i: (0,) * len(shape))
    grad_input, spectral_grad, pointwise_grad, bias_grad = pl.pallas_call(
        last_kernel,
        grid=(1,),
        out_shape=(
            jax.ShapeDtypeStruct(field, BF),
            jax.ShapeDtypeStruct((2, 8, 8, C * C), F32),
            jax.ShapeDtypeStruct((C, C), F32),
            jax.ShapeDtypeStruct((1, C), F32),
        ),
        in_specs=[any_spec] * 3,
        out_specs=(any_spec, any_spec, whole((C, C)), whole((1, C))),
        scratch_shapes=[
            pltpu.VMEM(field, BF),
            pltpu.VMEM((2, 128, C), F32),
            pltpu.VMEM((N, 8, 128), F32),
            pltpu.VMEM((2, 8, 8, C * C), F32),
            pltpu.SemaphoreType.DMA((4,)),
        ],
        compiler_params=pltpu.CompilerParams(vmem_limit_bytes=VMEM_BYTES),
    )(grad_input, modes, sums)
    return grad_input, spectral_grad, pointwise_grad, bias_grad.reshape(C)


def solution(mesh):
    in_specs = (P(None, "row", "col"), P(None, "row", "col"), P(None, "row", "col", None), P(), P())
    out_specs = (P(None, "row", "col"), P(None, "row", "col", None), P(), P())
    return jax.shard_map(body, mesh=mesh, in_specs=in_specs, out_specs=out_specs, check_vma=False)
```

```python
import functools
import math

import jax
import jax.numpy as jnp
import ml_dtypes
import numpy as np
from jax import lax
from jax.experimental import pallas as pl
from jax.experimental.pallas import tpu as pltpu
from jax.sharding import PartitionSpec as P

C = 64
K1 = 128
K2 = 128
NY = 1024
NX = 2048
TY = 64
TX = 128
N = 16
SCALE = float(NY * NX) ** (-0.5)
MESH = pl.DeviceIdType.MESH
VMEM_BYTES = 60 * 1024 * 1024
BF = jnp.bfloat16
F32 = jnp.float32

CHIPS = ((1, 2), (0, 1), (0, 3), (1, 1), (0, 2), (1, 0), (1, 3), (0, 0))
COL_ORDER = ((1, 2, 0), (0, 1, 0), (1, 2, 1), (0, 3, 0), (0, 1, 1), (1, 1, 0), (0, 3, 1), (0, 2, 0), (1, 1, 1), (1, 0, 0))
COL_ORDER += ((0, 2, 1), (1, 3, 0), (1, 0, 1), (1, 3, 1), (0, 0, 1))
ROW_ORDER = tuple((x, z) for z in (4, 3, 5, 2, 6, 1, 7, 0) for x in (0, 1) if (x, z) != (0, 0))

X1, Y1, T1, T2, Y2, X2, X3, Y3, T3, T4, Y4, X4, Z1, Z2, Z3 = range(15)


def trig(first, second, total):
    phase = np.mod(first[:, None] * second[None, :], total).astype(np.float32) * np.float32(
        2.0 * math.pi / total
    )
    return np.cos(phase).astype(ml_dtypes.bfloat16), np.sin(phase).astype(ml_dtypes.bfloat16)


@functools.cache
def tables():
    cos, sin = trig(np.arange(K2), np.arange(NX), NX)
    tx = np.stack([cos.reshape(N, 8, NX), -sin.reshape(N, 8, NX)], 1).reshape(2 * K2, 8, NX // 8)
    tx = tx.transpose(1, 0, 2)
    cos, sin = trig(np.arange(K1) - K1 // 2, np.arange(NY), NY)
    ty = np.stack([cos.reshape(K1, N, TY), sin.reshape(K1, N, TY)], 2).reshape(K1, 8, 256)
    ty = ty.transpose(1, 0, 2).reshape(4, 256, 256)
    tyi = np.concatenate([cos, sin], 0).reshape(2 * K1, 4, 256).transpose(1, 0, 2)
    return np.ascontiguousarray(np.concatenate([tx, ty, tyi], 0))


def dot(a, b):
    return lax.dot_general(a, b, (((1,), (0,)), ((), ())), preferred_element_type=F32)


def dot_t(a, b):
    return lax.dot_general(a, b, (((1,), (1,)), ((), ())), preferred_element_type=F32)


def normal_slope(value):
    cumul = 0.5 * (1.0 + lax.erf(value * (1.0 / math.sqrt(2.0))))
    dens = jnp.exp(-0.5 * value * value) * (1.0 / math.sqrt(2.0 * math.pi))
    return cumul + value * dens


def kernel(
    inp, cot, w, pw_hbm, bias_hbm, tab,
    gin, ug, zsum,
    pw, bias, inp_v, cot_v, w_v, tab_v, e1_v, e_v, sel_v,
    xr, yr, tr, xsend, ysend, tsend,
    zsend, zr, f2_v, dz_v, dz2_v, kron_v, zp_v, gz_v, s_v, ug_v, gin_v,
    send_sem, recv_sem, loc_sem,
):
    row = lax.axis_index("row")
    col = lax.axis_index("col")
    col_x, col_y, col_c = lax.div(col, 8), lax.rem(lax.div(col, 2), 4), lax.rem(col, 2)
    lane_lo = lax.broadcasted_iota(jnp.int32, (16, 128), 1) < 64
    mask_j = (lax.broadcasted_iota(jnp.int32, (8, 8, 128), 2) & 7) == lax.broadcasted_iota(
        jnp.int32, (8, 8, 128), 0
    )

    def wrap(i):
        return lax.rem(i, N)

    def remote(src, dst, phase, slot, device):
        return pltpu.make_async_remote_copy(
            src_ref=src,
            dst_ref=dst,
            send_sem=send_sem.at[phase],
            recv_sem=recv_sem.at[phase, slot],
            device_id=device,
            device_id_type=MESH,
        )

    def wait_recv(dst, phase, slot=0):
        remote(dst, dst, phase, slot, (row, col)).wait_recv()

    def wait_sent(like, phase):
        remote(like, like, phase, 0, (row, col)).wait_send()

    def keep(src, dst, phase, half=0):
        pltpu.make_async_copy(src, dst, recv_sem.at[phase, half]).start()

    pending = []

    def finish():
        for wait in pending:
            wait()

    def sent(like, phase):
        pending.append(lambda: wait_sent(like, phase))

    def row_partner(x, z):
        z = jnp.where(col_c == 0, z, 8 - z)
        return 8 * (lax.div(row, 8) ^ x) + lax.rem(lax.rem(row, 8) + z, 8)

    def col_partner(x, y, c, own_core):
        y = jnp.where(own_core == 0, y, 4 - y)
        return 8 * (col_x ^ x) + 2 * lax.rem(col_y + y, 4) + (col_c ^ c)

    def ordered(k):
        words = [0, 0]
        for i, (x, y, c) in enumerate(COL_ORDER):
            words[i // 8] |= (8 * x + 2 * y + c) << (4 * (i % 8))
        words = [w - (1 << 32) if w >> 31 else w for w in words]
        code = (jnp.where(k < 8, words[0], words[1]) >> (4 * lax.rem(k, 8))) & 15
        return code >> 3, (code >> 1) & 3, code & 1

    def send_block(src, dst, m, phase, half):
        remote(src, dst.at[half, col], phase, N * half + col, (row, m)).start()

    def send_row(src_of, dst, phase, slot, like, half=0):
        for x, z in ROW_ORDER:
            r = row_partner(x, z)
            remote(src_of(r), dst.at[slot], phase, half, (r, col)).start()
        keep(src_of(row), dst.at[slot], phase, half)
        sent(like, phase)

    def send_col(src_of, dst, phase, like):
        for x, y, c in COL_ORDER:
            m = col_partner(x, y, c, col_c)
            remote(src_of(m), dst.at[col], phase, 0, (row, m)).start()
        keep(src_of(col), dst.at[col], phase)
        sent(like, phase)

    block = wrap(row + col)
    top = row == 0

    def send_t(src, dst, phase, to_modes):
        own = row if to_modes else col
        slot = col if to_modes else row

        @pl.loop(0, N)
        def _(i):
            target = (i, block) if to_modes else (wrap(col + N - i), i)
            is_own = jnp.logical_and(top, i == own)

            @pl.when(jnp.logical_not(is_own))
            def _():
                remote(src.at[i], dst.at[slot], phase, 0, target).start()

            @pl.when(is_own)
            def _():
                keep(src.at[i], dst.at[slot], phase)

        def wait():
            @pl.when(top)
            def _():
                wait_sent(src.at[pl.ds(0, N - 1)], phase)

            @pl.when(jnp.logical_not(top))
            def _():
                wait_sent(src, phase)

        pending.append(wait)

    barrier = pltpu.get_barrier_semaphore()

    @pl.loop(1, N)
    def _(d):
        pl.semaphore_signal(barrier, inc=1, device_id=(row, wrap(col + d)), device_id_type=MESH)
        pl.semaphore_signal(barrier, inc=1, device_id=(wrap(row + d), col), device_id_type=MESH)

    loads = [
        pltpu.make_async_copy(src, dst, loc_sem.at[i])
        for i, (src, dst) in enumerate(
            [
                (pw_hbm, pw),
                (bias_hbm, bias),
                (inp, inp_v),
                (tab, tab_v),
                (inp.at[pl.ds(4 * col, 2)], xr.at[0, 0, col]),
                (inp.at[pl.ds(4 * col + 2, 2)], xr.at[0, 1, col]),
                (w, w_v),
                (cot, cot_v),
            ]
        )
    ]
    for load in loads:
        load.start()
    pl.semaphore_wait(barrier, 2 * N - 2)

    for half in range(2):
        for x, y, c in COL_ORDER:
            m = col_partner(x, y, c, col_c)
            send_block(inp.at[pl.ds(4 * m + 2 * half, 2)], xr.at[0], m, X1, half)
    sent(inp.at[pl.ds(0, 4 * N - 4)], X1)

    def pack(src, dst):
        for b in range(4):
            dst[:, 128 * b : 128 * b + 128] = src[:, 16 * b : 16 * b + 16, :].reshape(1024, 128)

    def build_kron(which):
        @pl.loop(0, 4)
        def _(i):
            rows = pl.ds(pl.multiple_of(256 * i, 256), 256)
            part = (dot_t if which == 0 else dot)(sel_v[rows, :], pw[...]).astype(BF)
            for j in range(4):
                full = dot_t(part, sel_v[256 * j : 256 * j + 256, :])
                same = (lax.broadcasted_iota(jnp.int32, (256, 256), 0) & 15) == (
                    lax.broadcasted_iota(jnp.int32, (256, 256), 1) & 15
                )
                kron_v[which, rows, 256 * j : 256 * j + 256] = jnp.where(same, full, 0.0).astype(BF)

    def apply_kron(which, src, dst):
        @pl.loop(0, 4)
        def _(i):
            rows = pl.ds(pl.multiple_of(256 * i, 256), 256)
            out = pl.ds(pl.multiple_of(16 * i, 16), 16)
            for h in range(2):
                res = dot(kron_v[which, rows, :], src[:, 256 * h : 256 * h + 256])
                for t in range(2):
                    y = 32 * h + 16 * t
                    dst[out, y : y + 16, :] = res[:, 128 * t : 128 * t + 128].reshape(16, 16, 128)

    def forward_x(src, phase, dst, half):
        acc = jnp.zeros((256, 128), F32)
        for x, y in CHIPS:
            chip = 4 * (col_x ^ x) + lax.rem(col_y + y, 4)
            blocks = []
            for c in range(2):
                slot = 2 * chip + c

                @pl.when(slot != col)
                def _(slot=slot):
                    wait_recv(src.at[half, slot], phase, N * half + slot)

                blocks.append(src[half, slot].reshape(128, 128))
            acc = acc + dot_t(tab_v[chip], jnp.concatenate(blocks, 1))
        dst[...] = acc.astype(BF).reshape(N, 16, 128)

    def forward_y(src):
        acc = jnp.zeros((K1, 32), F32)
        for q in range(8):
            parts = []
            for t in range(2):
                b = src[2 * q + t].astype(F32)
                jb = jnp.concatenate([b[8:16], -b[0:8]], 0)
                rows = [
                    jnp.where(lane_lo, b, pltpu.roll(jb, 64, 1)),
                    jnp.where(lane_lo, pltpu.roll(b, 64, 1), jb),
                ]
                parts.append(jnp.concatenate(rows, 0).astype(BF))
            table = tab_v[8 + q // 2, 128 * (q % 2) : 128 * (q % 2) + 128, :]
            acc = acc + dot_t(table, jnp.concatenate(parts, 1))
        return (acc * SCALE).astype(BF).astype(F32).reshape(N, 8, 32)

    def pack_t(first, second, dst):
        dst[...] = jnp.concatenate([first[:, 0:4], second[:, 0:4], first[:, 4:8], second[:, 4:8]], 2)

    def unpack_t(src):
        x = src[...]
        x = jnp.concatenate([x, pltpu.roll(x, 64, 2)], 1)
        return x.reshape(128, 128).T

    def to_modes(src):
        xt = unpack_t(src)
        rows = []
        for ri in range(2):
            cols = []
            for c in range(4):
                at = (2 * c + ri) * 8
                tile = xt[at : at + 8]
                cols.append(jnp.where(mask_j, tile[None], 0.0).reshape(64, 128))
            rows.append(jnp.concatenate(cols, 1))
        return dot(jnp.concatenate(rows, 0).astype(BF), e1_v[...])

    def from_modes(spec, dst):
        full = dot_t(spec.astype(BF), e1_v[...])
        tiles = []
        for c in range(4):
            for ri in range(2):
                part = full[64 * ri : 64 * ri + 64, 128 * c : 128 * c + 128].reshape(8, 8, 128)
                tiles.append(jnp.sum(jnp.where(mask_j, part, 0.0), axis=0))
        xt = jnp.concatenate(tiles + [jnp.zeros((64, 128), F32)], 0)
        x = xt.T.reshape(N, 8, 128)
        dst[...] = jnp.concatenate([x[:, 0:4, 0:64], x[:, 4:8, 0:64]], 2)

    def inverse_y(src):
        ht = unpack_t(src)
        first, second = [], []
        for c in range(4):
            hr, hi = ht[16 * c : 16 * c + 8], ht[16 * c + 8 : 16 * c + 16]
            first += [hr, hi]
            second += [-hi, hr]
        h = jnp.concatenate([jnp.concatenate(first, 0), jnp.concatenate(second, 0)], 1).astype(BF)
        return h

    def inverse_y_half(h, dst, half):
        h = h[32 * half : 32 * half + 32]
        d = jnp.concatenate([dot(h, tab_v[12 + i]) for i in range(4)], 1)
        for a in range(8):
            t0 = d[0:16, 128 * a : 128 * a + 128]
            t1 = d[16:32, 128 * a : 128 * a + 128]
            dst[2 * a] = jnp.where(lane_lo, t0, pltpu.roll(t1, 64, 1)).astype(BF)
            dst[2 * a + 1] = jnp.where(lane_lo, pltpu.roll(t0, 64, 1), t1).astype(BF)

    def inverse_x(src, out, dst, phase, half):
        yt = src[...].reshape(256, 128).astype(F32).T.astype(BF)
        late = None
        for x, y in CHIPS:
            chip = 4 * (col_x ^ x) + lax.rem(col_y + jnp.where(col_c == 0, y, 4 - y), 4)
            res = (dot(yt, tab_v[chip]) * SCALE).astype(BF)
            for c in range(2):
                out[half, 2 * chip + c] = res[:, 128 * c : 128 * c + 128].reshape(2, TY, TX)
            m = 2 * chip + col_c
            if (x, y) != (0, 0):
                send_block(out.at[half, m], dst, m, phase, half)
            else:
                dst[half, m] = out[half, m]
            if late is not None:
                send_block(out.at[half, late], dst, late, phase, half)
            late = m ^ 1
        send_block(out.at[half, late], dst, late, phase, half)

    lane = lax.broadcasted_iota(jnp.int32, (1024, 64), 1)
    first = lax.broadcasted_iota(jnp.int32, (1024, 64), 0)
    sel_v[...] = jnp.where((first >> 4) == lane, 1.0, 0.0).astype(BF)
    zsend[...] = jnp.zeros_like(zsend)
    loads[0].wait()
    build_kron(0)
    loads[2].wait()
    pack(inp_v, f2_v)
    apply_kron(0, f2_v, zp_v)
    first, lane = first[0:512], lane[0:512]
    at = (((first >> 3) & 15) << 2) + (first >> 7)
    e1_v[...] = jnp.where(at == lane, 1.0, 0.0).astype(BF)

    @pl.loop(0, 8)
    def _(i):
        channel = (lax.broadcasted_iota(jnp.int32, (64, 512), 1) >> 6) + 8 * i
        own = lax.broadcasted_iota(jnp.int32, (64, 512), 0)
        at = pl.ds(pl.multiple_of(i * 512, 512), 512)
        e_v[:, at] = jnp.where(channel == own, 1.0, 0.0).astype(BF)

    loads[3].wait()
    loads[4].wait()
    loads[5].wait()
    for half in range(2):
        forward_x(xr.at[0], X1, ysend.at[0, half], half)
        send_row(
            lambda r, half=half: ysend.at[0, half, wrap(r + col)],
            yr.at[0, half],
            Y1,
            row,
            ysend.at[0, half, pl.ds(0, N - 1)],
            half,
        )
    build_kron(1)
    wait_recv(yr.at[0, 0], Y1, 0)
    first_half = forward_y(yr.at[0, 0])
    wait_recv(yr.at[0, 1], Y1, 1)
    pack_t(first_half, forward_y(yr.at[0, 1]), tsend.at[0])
    send_t(tsend.at[0], tr.at[0], T1, True)
    loads[6].wait()
    wait_recv(tr.at[0], T1)

    u = to_modes(tr.at[0])
    ug_v[0] = u
    u = u.astype(BF)

    def fold(t):
        return t[:, 0:128] + t[:, 128:256] + t[:, 256:384] + t[:, 384:512]

    def mix(i, carry):
        sr, si = carry
        at = pl.ds(pl.multiple_of(i * 512, 512), 512)
        ue = dot(u, e_v[:, at])
        ur, ui = ue[0:64], ue[64:128]
        wr = w_v[0, :, :, at].astype(F32).reshape(64, 512)
        wi = w_v[1, :, :, at].astype(F32).reshape(64, 512)
        return sr + fold(wr * ur - wi * ui), si + fold(wr * ui + wi * ur)

    zero = jnp.zeros((64, 128), F32)
    sr, si = lax.fori_loop(0, 8, mix, (zero, zero), unroll=True)
    both = jnp.concatenate([sr, si], 0)
    both = both + pltpu.roll(both, 64, 1)
    from_modes(both[:, 0:64], tsend.at[1])
    send_t(tsend.at[1], tr.at[1], T2, False)

    wait_recv(tr.at[1], T2)
    spec = inverse_y(tr.at[1])
    for half in range(2):
        inverse_y_half(spec, ysend.at[1, half], half)
        send_row(
            lambda r, half=half: ysend.at[1, half, r],
            yr.at[1, half],
            Y2,
            block,
            ysend.at[1, half, pl.ds(0, N - 1)],
            half,
        )
    for half in range(2):
        wait_recv(yr.at[1, half], Y2, half)
        inverse_x(yr.at[1, half], xsend.at[0], xr.at[1], X2, half)
        sent(xsend.at[0, half, pl.ds(0, N - 1)], X2)

    loads[1].wait()
    loads[7].wait()
    def slope(m, half):
        for c in range(2):
            at = 4 * m + 2 * half + c
            z = xr[1, half, m, c].astype(F32) + zp_v[at] + bias[at]
            dz = cot_v[at].astype(F32) * normal_slope(z)
            dz_v[at] = dz.astype(BF)

    for half in range(2):
        slope(col, half)
        xr[2, half, col] = dz_v[pl.ds(4 * col + 2 * half, 2)]

        @pl.loop(0, N - 1)
        def _(k, half=half):
            x, y, c = ordered(k)
            m = col_partner(x, 4 - y, c, col_c ^ c)
            wait_recv(xr.at[1, half, m], X2, N * half + m)
            slope(m, half)
            send_block(dz_v.at[pl.ds(4 * m + 2 * half, 2)], xr.at[2], m, X3, half)

    sent(dz_v.at[pl.ds(0, 4 * N - 4)], X3)

    pack(dz_v, dz2_v)

    @pl.loop(0, 4)
    def _(o):
        cols = pl.ds(pl.multiple_of(256 * o, 256), 256)
        dzo = dz2_v[cols, :]
        same = (lax.broadcasted_iota(jnp.int32, (256, 256), 0) & 15) == (
            lax.broadcasted_iota(jnp.int32, (256, 256), 1) & 15
        )
        for i in range(4):
            prod = dot_t(f2_v[256 * i : 256 * i + 256, :], dzo)
            prod = jnp.where(same, prod, 0.0).reshape(16, 16, 256)
            s_v[16 * i : 16 * i + 16, cols] = jnp.sum(prod, axis=1)
        s_v[64:72, cols] = dot_t(jnp.ones((16, 512), BF), dzo)[0:8]

    terms = s_v[...]
    high = terms.astype(BF)
    low = (terms - high.astype(F32)).astype(BF)
    terms = dot(high, sel_v[...]) + dot(low, sel_v[...])
    zsend[:, 0:4, 0:64] = terms[0:64].reshape(N, 4, 64)
    zsend[0, 4:5, 0:64] = terms[64:65]
    send_col(lambda m: zsend.at[m], zr.at[0], Z1, zsend.at[pl.ds(0, N - 1)])
    apply_kron(1, dz2_v, gz_v)

    for half in range(2):
        forward_x(xr.at[2], X3, ysend.at[2, half], half)
        send_row(
            lambda r, half=half: ysend.at[2, half, wrap(r + col)],
            yr.at[2, half],
            Y3,
            row,
            ysend.at[2, half, pl.ds(0, N - 1)],
            half,
        )
    wait_recv(yr.at[2, 0], Y3, 0)
    first_half = forward_y(yr.at[2, 0])
    wait_recv(yr.at[2, 1], Y3, 1)
    pack_t(first_half, forward_y(yr.at[2, 1]), tsend.at[2])
    send_t(tsend.at[2], tr.at[2], T3, True)
    wait_recv(zr.at[0], Z1)
    zr[3, 0] = jnp.sum(zr[0], axis=0)
    send_row(lambda r: zr.at[3, 0], zr.at[1], Z2, row, zsend.at[pl.ds(0, N - 1)])
    wait_recv(tr.at[2], T3)

    g = to_modes(tr.at[2])
    ug_v[1] = g
    g = jnp.concatenate([g, g], 1)
    gr, gi = g[0:64], g[64:128]
    gr4, gi4 = jnp.concatenate([gr] * 4, 1), jnp.concatenate([gi] * 4, 1)

    def mix_back(i, acc):
        at = pl.ds(pl.multiple_of(i * 512, 512), 512)
        wr = w_v[0, :, :, at].astype(F32).reshape(64, 512)
        wi = w_v[1, :, :, at].astype(F32).reshape(64, 512)
        both = jnp.concatenate([wr * gr4 + wi * gi4, wr * gi4 - wi * gr4], 0).astype(BF)
        return acc + dot_t(both, e_v[:, at])

    du = lax.fori_loop(0, 8, mix_back, jnp.zeros((128, 64), F32), unroll=True)
    from_modes(du, tsend.at[3])
    send_t(tsend.at[3], tr.at[3], T4, False)

    wait_recv(zr.at[1], Z2)
    zr[3, 1] = jnp.sum(zr[1], axis=0)
    send_col(lambda m: zr.at[3, 1], zr.at[2], Z3, zsend.at[pl.ds(0, N - 1)])
    out_ug = pltpu.make_async_copy(ug_v, ug, loc_sem.at[0])
    out_ug.start()

    wait_recv(tr.at[3], T4)
    spec = inverse_y(tr.at[3])
    for half in range(2):
        inverse_y_half(spec, ysend.at[3, half], half)
        send_row(
            lambda r, half=half: ysend.at[3, half, r],
            yr.at[3, half],
            Y4,
            block,
            ysend.at[3, half, pl.ds(0, N - 1)],
            half,
        )
    wait_recv(zr.at[2], Z3)
    out_z = pltpu.make_async_copy(zr.at[2], zsum, loc_sem.at[2])
    out_z.start()
    pending.append(out_z.wait)
    for half in range(2):
        wait_recv(yr.at[3, half], Y4, half)
        inverse_x(yr.at[3, half], xsend.at[1], xr.at[3], X4, half)
        sent(xsend.at[1, half, pl.ds(0, N - 1)], X4)
    def finish_block(m, half):
        at = pl.ds(4 * m + 2 * half, 2)
        gin_v[at] = (xr[3, half, m].astype(F32) + gz_v[at]).astype(BF)

    for half in range(2):
        finish_block(col, half)

        @pl.loop(0, N - 1)
        def _(k, half=half):
            x, y, c = ordered(k)
            m = col_partner(x, 4 - y, c, col_c ^ c)
            wait_recv(xr.at[3, half, m], X4, N * half + m)
            finish_block(m, half)

    out_gin = pltpu.make_async_copy(gin_v, gin, loc_sem.at[1])
    out_gin.start()

    pending.append(out_ug.wait)
    pending.append(out_gin.wait)
    finish()


def last_kernel(gin, ug, zsum, gin_out, sg, pg, bg, gin_v, ug_v, z_v, sg_v, sem):
    pieces = ((ug, ug_v), (gin, gin_v), (zsum, z_v))
    loads = [pltpu.make_async_copy(a, b, sem.at[i]) for i, (a, b) in enumerate(pieces)]
    for load in loads:
        load.start()
    loads[0].wait()
    u = ug_v[0].astype(BF)
    g = jnp.concatenate([ug_v[1]] * 8, 1)
    gr, gi = g[0:64], g[64:128]
    own = lax.broadcasted_iota(jnp.int32, (64, 512), 0)
    group = lax.broadcasted_iota(jnp.int32, (64, 512), 1) >> 6
    out = pltpu.make_async_copy(gin_v, gin_out, sem.at[1])
    for i in range(8):
        at = slice(512 * i, 512 * i + 512)
        ue = dot(u, jnp.where(group + 8 * i == own, 1.0, 0.0).astype(BF))
        ur, ui = ue[0:64], ue[64:128]
        sg_v[0, :, :, at] = (gr * ur + gi * ui).reshape(8, 8, 512)
        sg_v[1, :, :, at] = (gi * ur - gr * ui).reshape(8, 8, 512)
        pltpu.make_async_copy(sg_v.at[:, :, :, at], sg.at[:, :, :, at], sem.at[3]).start()
        if i == 0:
            loads[1].wait()
            out.start()
    loads[2].wait()
    pg[...] = z_v[:, 0:4, 0:64].reshape(C, C) * SCALE
    bg[...] = z_v[0, 4:5, 0:64] * SCALE
    pltpu.make_async_copy(sg_v, sg, sem.at[3]).wait()
    out.wait()


def body(inputs, cotangent, spectral_weight, point_weight, bias):
    any_spec = pl.BlockSpec(memory_space=pl.ANY)
    field = (C, TY, TX)
    table = jnp.asarray(tables())
    grad_input, modes, sums = pl.pallas_call(
        kernel,
        out_shape=(
            jax.ShapeDtypeStruct(field, BF),
            jax.ShapeDtypeStruct((2, 128, C), F32),
            jax.ShapeDtypeStruct((N, 8, 128), F32),
        ),
        in_specs=[any_spec] * 6,
        out_specs=(any_spec, any_spec, any_spec),
        scratch_shapes=[
            pltpu.VMEM((C, C), BF),
            pltpu.SMEM((C,), F32),
            pltpu.VMEM(field, BF),
            pltpu.VMEM(field, BF),
            pltpu.VMEM((2, 8, 8, C * C), BF),
            pltpu.VMEM(table.shape, BF),
            pltpu.VMEM((512, 64), BF),
            pltpu.VMEM((64, C * C), BF),
            pltpu.VMEM((1024, 64), BF),
            pltpu.VMEM((4, 2, N, 2, TY, TX), BF),
            pltpu.VMEM((4, 2, N, 16, 128), BF),
            pltpu.VMEM((4, N, 4, 128), F32),
            pltpu.VMEM((2, 2, N, 2, TY, TX), BF),
            pltpu.VMEM((4, 2, N, 16, 128), BF),
            pltpu.VMEM((4, N, 4, 128), F32),
            pltpu.VMEM((N, 8, 128), F32),
            pltpu.VMEM((4, N, 8, 128), F32),
            pltpu.VMEM((1024, 512), BF),
            pltpu.VMEM(field, BF),
            pltpu.VMEM((1024, 512), BF),
            pltpu.VMEM((2, 1024, 1024), BF),
            pltpu.VMEM(field, F32),
            pltpu.VMEM(field, F32),
            pltpu.VMEM((72, 1024), F32),
            pltpu.VMEM((2, 128, C), F32),
            pltpu.VMEM(field, BF),
            pltpu.SemaphoreType.DMA((15,)),
            pltpu.SemaphoreType.DMA((15, 2 * N)),
            pltpu.SemaphoreType.DMA((10,)),
        ],
        compiler_params=pltpu.CompilerParams(
            collective_id=0, has_side_effects=True, vmem_limit_bytes=VMEM_BYTES
        ),
    )(inputs, cotangent, spectral_weight, point_weight, bias, table)
    whole = lambda shape: pl.BlockSpec(shape, lambda i: (0,) * len(shape))
    grad_input, spectral_grad, pointwise_grad, bias_grad = pl.pallas_call(
        last_kernel,
        grid=(1,),
        out_shape=(
            jax.ShapeDtypeStruct(field, BF),
            jax.ShapeDtypeStruct((2, 8, 8, C * C), F32),
            jax.ShapeDtypeStruct((C, C), F32),
            jax.ShapeDtypeStruct((1, C), F32),
        ),
        in_specs=[any_spec] * 3,
        out_specs=(any_spec, any_spec, whole((C, C)), whole((1, C))),
        scratch_shapes=[
            pltpu.VMEM(field, BF),
            pltpu.VMEM((2, 128, C), F32),
            pltpu.VMEM((N, 8, 128), F32),
            pltpu.VMEM((2, 8, 8, C * C), F32),
            pltpu.SemaphoreType.DMA((4,)),
        ],
        compiler_params=pltpu.CompilerParams(vmem_limit_bytes=VMEM_BYTES),
    )(grad_input, modes, sums)
    return grad_input, spectral_grad, pointwise_grad, bias_grad.reshape(C)


def solution(mesh):
    in_specs = (P(None, "row", "col"), P(None, "row", "col"), P(None, "row", "col", None), P(), P())
    out_specs = (P(None, "row", "col"), P(None, "row", "col", None), P(), P())
    return jax.shard_map(body, mesh=mesh, in_specs=in_specs, out_specs=out_specs, check_vma=False)
```

```python
import functools
import math

import jax
import jax.numpy as jnp
import ml_dtypes
import numpy as np
from jax import lax
from jax.experimental import pallas as pl
from jax.experimental.pallas import tpu as pltpu
from jax.sharding import PartitionSpec as P

C = 64
K1 = 128
K2 = 128
NY = 1024
NX = 2048
TY = 64
TX = 128
N = 16
SCALE = float(NY * NX) ** (-0.5)
MESH = pl.DeviceIdType.MESH
VMEM_BYTES = 60 * 1024 * 1024
BF = jnp.bfloat16
F32 = jnp.float32

CHIPS = ((1, 2), (0, 1), (0, 3), (1, 1), (0, 2), (1, 0), (1, 3), (0, 0))
COL_ORDER = ((1, 2, 0), (0, 1, 0), (1, 2, 1), (0, 3, 0), (0, 1, 1), (1, 1, 0), (0, 3, 1), (0, 2, 0), (1, 1, 1), (1, 0, 0))
COL_ORDER += ((0, 2, 1), (1, 3, 0), (1, 0, 1), (1, 3, 1), (0, 0, 1))
ROW_ORDER = tuple((x, z) for z in (4, 3, 5, 2, 6, 1, 7, 0) for x in (0, 1) if (x, z) != (0, 0))

X1, Y1, T1, T2, Y2, X2, X3, Y3, T3, T4, Y4, X4, Z1, Z2, Z3 = range(15)


def trig(first, second, total):
    phase = np.mod(first[:, None] * second[None, :], total).astype(np.float32) * np.float32(
        2.0 * math.pi / total
    )
    return np.cos(phase).astype(ml_dtypes.bfloat16), np.sin(phase).astype(ml_dtypes.bfloat16)


@functools.cache
def tables():
    cos, sin = trig(np.arange(K2), np.arange(NX), NX)
    tx = np.stack([cos.reshape(N, 8, NX), -sin.reshape(N, 8, NX)], 1).reshape(2 * K2, 8, NX // 8)
    tx = tx.transpose(1, 0, 2)
    cos, sin = trig(np.arange(K1) - K1 // 2, np.arange(NY), NY)
    ty = np.stack([cos.reshape(K1, N, TY), sin.reshape(K1, N, TY)], 2).reshape(K1, 8, 256)
    ty = ty.transpose(1, 0, 2).reshape(4, 256, 256)
    c4, s4 = (t.reshape(N, 8, N, TY).transpose(2, 3, 0, 1) for t in (cos, sin))
    back = np.stack([np.stack([c4, -s4], 3), np.stack([s4, c4], 3)], 1).reshape(N, 2 * TY, 2 * K1)
    cos, sin = trig(np.arange(K2), np.arange(NX), NX)
    txb = np.concatenate([cos, -sin], 0).reshape(2 * K2, 8, NX // 8).transpose(1, 0, 2)
    return np.ascontiguousarray(np.concatenate([tx, ty, txb], 0)), np.ascontiguousarray(back)


def dot(a, b):
    return lax.dot_general(a, b, (((1,), (0,)), ((), ())), preferred_element_type=F32)


def dot_t(a, b):
    return lax.dot_general(a, b, (((1,), (1,)), ((), ())), preferred_element_type=F32)


def normal_slope(value):
    cumul = 0.5 * (1.0 + lax.erf(value * (1.0 / math.sqrt(2.0))))
    dens = jnp.exp(-0.5 * value * value) * (1.0 / math.sqrt(2.0 * math.pi))
    return cumul + value * dens


def kernel(
    inp, cot, w, pw_hbm, bias_hbm, tab, back,
    gin, ug, zsum,
    pw, bias, inp_v, cot_v, w_v, tab_v, back_v, e1_v, e_v, sel_v,
    xr, yr, tr, xsend, ysend, tsend, gsend, gath,
    zsend, zr, f2_v, dz_v, dz2_v, kron_v, zp_v, gz_v, s_v, ug_v, gin_v,
    send_sem, recv_sem, loc_sem,
):
    row = lax.axis_index("row")
    col = lax.axis_index("col")
    col_x, col_y, col_c = lax.div(col, 8), lax.rem(lax.div(col, 2), 4), lax.rem(col, 2)
    lane_lo = lax.broadcasted_iota(jnp.int32, (16, 128), 1) < 64
    mask_j = (lax.broadcasted_iota(jnp.int32, (8, 8, 128), 2) & 7) == lax.broadcasted_iota(
        jnp.int32, (8, 8, 128), 0
    )

    mask_k = (lax.broadcasted_iota(jnp.int32, (8, 8, 128), 2) & 7) == lax.broadcasted_iota(
        jnp.int32, (8, 8, 128), 1
    )

    def wrap(i):
        return lax.rem(i, N)

    def remote(src, dst, phase, slot, device):
        return pltpu.make_async_remote_copy(
            src_ref=src,
            dst_ref=dst,
            send_sem=send_sem.at[phase],
            recv_sem=recv_sem.at[phase, slot],
            device_id=device,
            device_id_type=MESH,
        )

    def wait_recv(dst, phase, slot=0):
        remote(dst, dst, phase, slot, (row, col)).wait_recv()

    def wait_sent(like, phase):
        remote(like, like, phase, 0, (row, col)).wait_send()

    def keep(src, dst, phase, half=0):
        pltpu.make_async_copy(src, dst, recv_sem.at[phase, half]).start()

    pending = []

    def finish():
        for wait in pending:
            wait()

    def sent(like, phase):
        pending.append(lambda: wait_sent(like, phase))

    def row_partner(x, z):
        z = jnp.where(col_c == 0, z, 8 - z)
        return 8 * (lax.div(row, 8) ^ x) + lax.rem(lax.rem(row, 8) + z, 8)

    def col_partner(x, y, c, own_core):
        y = jnp.where(own_core == 0, y, 4 - y)
        return 8 * (col_x ^ x) + 2 * lax.rem(col_y + y, 4) + (col_c ^ c)

    def ordered(k):
        words = [0, 0]
        for i, (x, y, c) in enumerate(COL_ORDER):
            words[i // 8] |= (8 * x + 2 * y + c) << (4 * (i % 8))
        words = [w - (1 << 32) if w >> 31 else w for w in words]
        code = (jnp.where(k < 8, words[0], words[1]) >> (4 * lax.rem(k, 8))) & 15
        return code >> 3, (code >> 1) & 3, code & 1

    def send_block(src, dst, m, phase, half):
        remote(src, dst.at[half, col], phase, N * half + col, (row, m)).start()

    def send_row(src_of, dst, phase, slot, like, half=0):
        for x, z in ROW_ORDER:
            r = row_partner(x, z)
            remote(src_of(r), dst.at[slot], phase, half, (r, col)).start()
        keep(src_of(row), dst.at[slot], phase, half)
        sent(like, phase)

    def send_col(src_of, dst, phase, like):
        for x, y, c in COL_ORDER:
            m = col_partner(x, y, c, col_c)
            remote(src_of(m), dst.at[col], phase, 0, (row, m)).start()
        keep(src_of(col), dst.at[col], phase)
        sent(like, phase)

    block = wrap(row + col)
    top = row == 0

    def send_t(src, dst, phase):
        @pl.loop(0, N)
        def _(i):
            is_own = jnp.logical_and(top, i == row)

            @pl.when(jnp.logical_not(is_own))
            def _():
                remote(src.at[i], dst.at[col], phase, 0, (i, block)).start()

            @pl.when(is_own)
            def _():
                keep(src.at[i], dst.at[col], phase)

        def wait():
            @pl.when(top)
            def _():
                wait_sent(src.at[pl.ds(0, N - 1)], phase)

            @pl.when(jnp.logical_not(top))
            def _():
                wait_sent(src, phase)

        pending.append(wait)

    barrier = pltpu.get_barrier_semaphore()

    @pl.loop(1, N)
    def _(d):
        pl.semaphore_signal(barrier, inc=1, device_id=(row, wrap(col + d)), device_id_type=MESH)
        pl.semaphore_signal(barrier, inc=1, device_id=(wrap(row + d), col), device_id_type=MESH)

    loads = [
        pltpu.make_async_copy(src, dst, loc_sem.at[i])
        for i, (src, dst) in enumerate(
            [
                (pw_hbm, pw),
                (bias_hbm, bias),
                (inp, inp_v),
                (tab, tab_v),
                (inp.at[pl.ds(4 * col, 2)], xr.at[0, 0, col]),
                (inp.at[pl.ds(4 * col + 2, 2)], xr.at[0, 1, col]),
                (w, w_v),
                (cot, cot_v),
                (back.at[row], back_v),
            ]
        )
    ]
    for load in loads:
        load.start()
    pl.semaphore_wait(barrier, 2 * N - 2)

    for half in range(2):
        for x, y, c in COL_ORDER:
            m = col_partner(x, y, c, col_c)
            send_block(inp.at[pl.ds(4 * m + 2 * half, 2)], xr.at[0], m, X1, half)
    sent(inp.at[pl.ds(0, 4 * N - 4)], X1)

    def pack(src, dst):
        for b in range(4):
            dst[:, 128 * b : 128 * b + 128] = src[:, 16 * b : 16 * b + 16, :].reshape(1024, 128)

    def build_kron(which):
        @pl.loop(0, 4)
        def _(i):
            rows = pl.ds(pl.multiple_of(256 * i, 256), 256)
            part = (dot_t if which == 0 else dot)(sel_v[rows, :], pw[...]).astype(BF)
            for j in range(4):
                full = dot_t(part, sel_v[256 * j : 256 * j + 256, :])
                same = (lax.broadcasted_iota(jnp.int32, (256, 256), 0) & 15) == (
                    lax.broadcasted_iota(jnp.int32, (256, 256), 1) & 15
                )
                kron_v[which, rows, 256 * j : 256 * j + 256] = jnp.where(same, full, 0.0).astype(BF)

    def apply_kron(which, src, dst):
        @pl.loop(0, 4)
        def _(i):
            rows = pl.ds(pl.multiple_of(256 * i, 256), 256)
            out = pl.ds(pl.multiple_of(16 * i, 16), 16)
            for h in range(2):
                res = dot(kron_v[which, rows, :], src[:, 256 * h : 256 * h + 256])
                for t in range(2):
                    y = 32 * h + 16 * t
                    dst[out, y : y + 16, :] = res[:, 128 * t : 128 * t + 128].reshape(16, 16, 128)

    def forward_x(src, phase, dst, half):
        acc = jnp.zeros((256, 128), F32)
        for x, y in CHIPS:
            chip = 4 * (col_x ^ x) + lax.rem(col_y + y, 4)
            blocks = []
            for c in range(2):
                slot = 2 * chip + c

                @pl.when(slot != col)
                def _(slot=slot):
                    wait_recv(src.at[half, slot], phase, N * half + slot)

                blocks.append(src[half, slot].reshape(128, 128))
            acc = acc + dot_t(tab_v[chip], jnp.concatenate(blocks, 1))
        dst[...] = acc.astype(BF).reshape(N, 16, 128)

    def forward_y(src):
        acc = jnp.zeros((K1, 32), F32)
        for q in range(8):
            parts = []
            for t in range(2):
                b = src[2 * q + t].astype(F32)
                jb = jnp.concatenate([b[8:16], -b[0:8]], 0)
                rows = [
                    jnp.where(lane_lo, b, pltpu.roll(jb, 64, 1)),
                    jnp.where(lane_lo, pltpu.roll(b, 64, 1), jb),
                ]
                parts.append(jnp.concatenate(rows, 0).astype(BF))
            table = tab_v[8 + q // 2, 128 * (q % 2) : 128 * (q % 2) + 128, :]
            acc = acc + dot_t(table, jnp.concatenate(parts, 1))
        return (acc * SCALE).astype(BF).astype(F32).reshape(N, 8, 32)

    def pack_t(first, second, dst):
        dst[...] = jnp.concatenate([first[:, 0:4], second[:, 0:4], first[:, 4:8], second[:, 4:8]], 2)

    def unpack_t(src):
        x = src[...]
        x = jnp.concatenate([x, pltpu.roll(x, 64, 2)], 1)
        return x.reshape(128, 128).T

    def to_modes(src):
        xt = unpack_t(src)
        rows = []
        for ri in range(2):
            cols = []
            for c in range(4):
                at = (2 * c + ri) * 8
                tile = xt[at : at + 8]
                cols.append(jnp.where(mask_j, tile[None], 0.0).reshape(64, 128))
            rows.append(jnp.concatenate(cols, 1))
        return dot(jnp.concatenate(rows, 0).astype(BF), e1_v[...])

    def from_modes(spec, dst):
        full = dot_t(spec.astype(BF), e1_v[...])
        tiles = []
        for c in range(4):
            for ri in range(2):
                part = full[64 * ri : 64 * ri + 64, 128 * c : 128 * c + 128].reshape(8, 8, 128)
                tiles.append(jnp.sum(jnp.where(mask_k, part, 0.0), axis=1))
        xt = jnp.concatenate(tiles + [jnp.zeros((64, 128), F32)], 0)
        x = xt.T.reshape(N, 8, 128)
        dst[...] = jnp.concatenate([x[:, 0:4, 0:64], x[:, 4:8, 0:64]], 2)

    def spread_modes(src, dst):
        xt = unpack_t(src)
        for half in range(2):
            pair = [xt[32 * half + 16 * c : 32 * half + 16 * c + 16] for c in range(2)]
            dst[half] = jnp.concatenate(pair, 1).astype(BF)

    def inverse_x(src, out, dst, phase, half):
        d = dot(back_v[...], src[...].reshape(256, 256)).astype(BF)
        real, imag = d[0:TY], d[TY : 2 * TY]
        rows = [jnp.concatenate([real[:, at : at + 128], imag[:, at : at + 128]], 1) for at in (0, 128)]
        yt = jnp.concatenate(rows, 0)
        late = None
        for x, y in CHIPS:
            chip = 4 * (col_x ^ x) + lax.rem(col_y + jnp.where(col_c == 0, y, 4 - y), 4)
            res = (dot(yt, tab_v[12 + chip]) * SCALE).astype(BF)
            for c in range(2):
                out[half, 2 * chip + c] = res[:, 128 * c : 128 * c + 128].reshape(2, TY, TX)
            m = 2 * chip + col_c
            if (x, y) != (0, 0):
                send_block(out.at[half, m], dst, m, phase, half)
            else:
                dst[half, m] = out[half, m]
            if late is not None:
                send_block(out.at[half, late], dst, late, phase, half)
            late = m ^ 1
        send_block(out.at[half, late], dst, late, phase, half)

    lane = lax.broadcasted_iota(jnp.int32, (1024, 64), 1)
    first = lax.broadcasted_iota(jnp.int32, (1024, 64), 0)
    sel_v[...] = jnp.where((first >> 4) == lane, 1.0, 0.0).astype(BF)
    zsend[...] = jnp.zeros_like(zsend)
    loads[0].wait()
    build_kron(0)
    loads[2].wait()
    pack(inp_v, f2_v)
    apply_kron(0, f2_v, zp_v)
    first, lane = first[0:512], lane[0:512]
    at = (((first >> 3) & 15) << 2) + (first >> 7)
    e1_v[...] = jnp.where(at == lane, 1.0, 0.0).astype(BF)

    @pl.loop(0, 8)
    def _(i):
        channel = (lax.broadcasted_iota(jnp.int32, (64, 512), 1) >> 6) + 8 * i
        own = lax.broadcasted_iota(jnp.int32, (64, 512), 0)
        at = pl.ds(pl.multiple_of(i * 512, 512), 512)
        e_v[:, at] = jnp.where(channel == own, 1.0, 0.0).astype(BF)

    loads[3].wait()
    loads[4].wait()
    loads[5].wait()
    for half in range(2):
        forward_x(xr.at[0], X1, ysend.at[0, half], half)
        send_row(
            lambda r, half=half: ysend.at[0, half, wrap(r + col)],
            yr.at[0, half],
            Y1,
            row,
            ysend.at[0, half, pl.ds(0, N - 1)],
            half,
        )
    build_kron(1)
    wait_recv(yr.at[0, 0], Y1, 0)
    first_half = forward_y(yr.at[0, 0])
    wait_recv(yr.at[0, 1], Y1, 1)
    pack_t(first_half, forward_y(yr.at[0, 1]), tsend.at[0])
    send_t(tsend.at[0], tr.at[0], T1)
    loads[6].wait()
    loads[8].wait()
    wait_recv(tr.at[0], T1)

    u = to_modes(tr.at[0])
    ug_v[0] = u
    u = u.astype(BF)

    def fold(t):
        return t[:, 0:128] + t[:, 128:256] + t[:, 256:384] + t[:, 384:512]

    def mix(i, carry):
        sr, si = carry
        at = pl.ds(pl.multiple_of(i * 512, 512), 512)
        ue = dot(u, e_v[:, at])
        ur, ui = ue[0:64], ue[64:128]
        wr = w_v[0, :, :, at].astype(F32).reshape(64, 512)
        wi = w_v[1, :, :, at].astype(F32).reshape(64, 512)
        return sr + fold(wr * ur - wi * ui), si + fold(wr * ui + wi * ur)

    zero = jnp.zeros((64, 128), F32)
    sr, si = lax.fori_loop(0, 8, mix, (zero, zero), unroll=True)
    both = jnp.concatenate([sr, si], 0)
    both = both + pltpu.roll(both, 64, 1)
    from_modes(both[:, 0:64], tsend.at[1])
    send_col(lambda m: tsend.at[1, m], tr.at[1], T2, tsend.at[1, pl.ds(0, N - 1)])

    wait_recv(tr.at[1], T2)
    spread_modes(tr.at[1], gsend.at[0])
    for half in range(2):
        send_row(
            lambda r, half=half: gsend.at[0, half],
            gath.at[0, half],
            Y2,
            row,
            gath.at[0, half, pl.ds(0, N - 1)],
            half,
        )
    for half in range(2):
        wait_recv(gath.at[0, half], Y2, half)
        inverse_x(gath.at[0, half], xsend.at[0], xr.at[1], X2, half)
        sent(xsend.at[0, half, pl.ds(0, N - 1)], X2)

    loads[1].wait()
    loads[7].wait()
    def slope(m, half):
        for c in range(2):
            at = 4 * m + 2 * half + c
            z = xr[1, half, m, c].astype(F32) + zp_v[at] + bias[at]
            dz = cot_v[at].astype(F32) * normal_slope(z)
            dz_v[at] = dz.astype(BF)

    for half in range(2):
        slope(col, half)
        xr[2, half, col] = dz_v[pl.ds(4 * col + 2 * half, 2)]

        @pl.loop(0, N - 1)
        def _(k, half=half):
            x, y, c = ordered(k)
            m = col_partner(x, 4 - y, c, col_c ^ c)
            wait_recv(xr.at[1, half, m], X2, N * half + m)
            slope(m, half)
            send_block(dz_v.at[pl.ds(4 * m + 2 * half, 2)], xr.at[2], m, X3, half)

    sent(dz_v.at[pl.ds(0, 4 * N - 4)], X3)

    pack(dz_v, dz2_v)

    @pl.loop(0, 4)
    def _(o):
        cols = pl.ds(pl.multiple_of(256 * o, 256), 256)
        dzo = dz2_v[cols, :]
        same = (lax.broadcasted_iota(jnp.int32, (256, 256), 0) & 15) == (
            lax.broadcasted_iota(jnp.int32, (256, 256), 1) & 15
        )
        for i in range(4):
            prod = dot_t(f2_v[256 * i : 256 * i + 256, :], dzo)
            prod = jnp.where(same, prod, 0.0).reshape(16, 16, 256)
            s_v[16 * i : 16 * i + 16, cols] = jnp.sum(prod, axis=1)
        s_v[64:72, cols] = dot_t(jnp.ones((16, 512), BF), dzo)[0:8]

    terms = s_v[...]
    high = terms.astype(BF)
    low = (terms - high.astype(F32)).astype(BF)
    terms = dot(high, sel_v[...]) + dot(low, sel_v[...])
    zsend[:, 0:4, 0:64] = terms[0:64].reshape(N, 4, 64)
    zsend[0, 4:5, 0:64] = terms[64:65]
    send_col(lambda m: zsend.at[m], zr.at[0], Z1, zsend.at[pl.ds(0, N - 1)])
    apply_kron(1, dz2_v, gz_v)

    for half in range(2):
        forward_x(xr.at[2], X3, ysend.at[2, half], half)
        send_row(
            lambda r, half=half: ysend.at[2, half, wrap(r + col)],
            yr.at[2, half],
            Y3,
            row,
            ysend.at[2, half, pl.ds(0, N - 1)],
            half,
        )
    wait_recv(yr.at[2, 0], Y3, 0)
    first_half = forward_y(yr.at[2, 0])
    wait_recv(yr.at[2, 1], Y3, 1)
    pack_t(first_half, forward_y(yr.at[2, 1]), tsend.at[2])
    send_t(tsend.at[2], tr.at[2], T3)
    wait_recv(zr.at[0], Z1)
    zr[3, 0] = jnp.sum(zr[0], axis=0)
    send_row(lambda r: zr.at[3, 0], zr.at[1], Z2, row, zsend.at[pl.ds(0, N - 1)])
    wait_recv(tr.at[2], T3)

    g = to_modes(tr.at[2])
    ug_v[1] = g
    g = jnp.concatenate([g, g], 1)
    gr, gi = g[0:64], g[64:128]
    gr4, gi4 = jnp.concatenate([gr] * 4, 1), jnp.concatenate([gi] * 4, 1)

    def mix_back(i, acc):
        at = pl.ds(pl.multiple_of(i * 512, 512), 512)
        wr = w_v[0, :, :, at].astype(F32).reshape(64, 512)
        wi = w_v[1, :, :, at].astype(F32).reshape(64, 512)
        both = jnp.concatenate([wr * gr4 + wi * gi4, wr * gi4 - wi * gr4], 0).astype(BF)
        return acc + dot_t(both, e_v[:, at])

    du = lax.fori_loop(0, 8, mix_back, jnp.zeros((128, 64), F32), unroll=True)
    from_modes(du, tsend.at[3])
    send_col(lambda m: tsend.at[3, m], tr.at[3], T4, tsend.at[3, pl.ds(0, N - 1)])

    wait_recv(zr.at[1], Z2)
    zr[3, 1] = jnp.sum(zr[1], axis=0)
    send_col(lambda m: zr.at[3, 1], zr.at[2], Z3, zsend.at[pl.ds(0, N - 1)])
    out_ug = pltpu.make_async_copy(ug_v, ug, loc_sem.at[0])
    out_ug.start()
    pending.append(out_ug.wait)

    wait_recv(tr.at[3], T4)
    spread_modes(tr.at[3], gsend.at[1])
    for half in range(2):
        send_row(
            lambda r, half=half: gsend.at[1, half],
            gath.at[1, half],
            Y4,
            row,
            gath.at[1, half, pl.ds(0, N - 1)],
            half,
        )
    wait_recv(zr.at[2], Z3)
    out_z = pltpu.make_async_copy(zr.at[2], zsum, loc_sem.at[2])
    out_z.start()
    pending.append(out_z.wait)
    for half in range(2):
        wait_recv(gath.at[1, half], Y4, half)
        inverse_x(gath.at[1, half], xsend.at[1], xr.at[3], X4, half)
    finish()

    def finish_block(m, half):
        at = pl.ds(4 * m + 2 * half, 2)
        gin_v[at] = (xr[3, half, m].astype(F32) + gz_v[at]).astype(BF)
        pltpu.make_async_copy(gin_v.at[at], gin.at[at], loc_sem.at[1]).start()

    for half in range(2):
        finish_block(col, half)

        @pl.loop(0, N - 1)
        def _(k, half=half):
            x, y, c = ordered(k)
            m = col_partner(x, 4 - y, c, col_c ^ c)
            wait_recv(xr.at[3, half, m], X4, N * half + m)
            finish_block(m, half)

    wait_sent(xsend.at[1, 0, pl.ds(0, N - 1)], X4)
    wait_sent(xsend.at[1, 1, pl.ds(0, N - 1)], X4)
    pltpu.make_async_copy(gin_v, gin, loc_sem.at[1]).wait()


def last_kernel(
    gin, ug, zsum, gin_out, sg, pg, bg, gin_v, ug_v, z_v, sg_v, pg_v, bg_v, sem
):
    pieces = ((ug, ug_v), (gin, gin_v), (zsum, z_v))
    loads = [pltpu.make_async_copy(a, b, sem.at[i]) for i, (a, b) in enumerate(pieces)]
    for load in loads:
        load.start()
    loads[0].wait()
    u = ug_v[0].astype(BF)
    g = jnp.concatenate([ug_v[1]] * 8, 1)
    gr, gi = g[0:64], g[64:128]
    own = lax.broadcasted_iota(jnp.int32, (64, 512), 0)
    group = lax.broadcasted_iota(jnp.int32, (64, 512), 1) >> 6
    out = pltpu.make_async_copy(gin_v, gin_out, sem.at[1])
    for i in range(8):
        at = slice(512 * i, 512 * i + 512)
        ue = dot(u, jnp.where(group + 8 * i == own, 1.0, 0.0).astype(BF))
        ur, ui = ue[0:64], ue[64:128]
        sg_v[0, :, :, at] = (gr * ur + gi * ui).reshape(8, 8, 512)
        sg_v[1, :, :, at] = (gi * ur - gr * ui).reshape(8, 8, 512)
        pltpu.make_async_copy(sg_v.at[:, :, :, at], sg.at[:, :, :, at], sem.at[3]).start()
        if i == 0:
            loads[1].wait()
            out.start()
            loads[2].wait()
            pg_v[...] = z_v[:, 0:4, 0:64].reshape(C, C) * SCALE
            bg_v[...] = z_v[0, 4:5, 0:64] * SCALE
            sums = (
                pltpu.make_async_copy(pg_v, pg, sem.at[0]),
                pltpu.make_async_copy(bg_v, bg, sem.at[2]),
            )
            for copy in sums:
                copy.start()
    for copy in sums:
        copy.wait()
    out.wait()
    pltpu.make_async_copy(sg_v, sg, sem.at[3]).wait()


def body(inputs, cotangent, spectral_weight, point_weight, bias):
    any_spec = pl.BlockSpec(memory_space=pl.ANY)
    field = (C, TY, TX)
    table, back = (jnp.asarray(t) for t in tables())
    grad_input, modes, sums = pl.pallas_call(
        kernel,
        out_shape=(
            jax.ShapeDtypeStruct(field, BF),
            jax.ShapeDtypeStruct((2, 128, C), F32),
            jax.ShapeDtypeStruct((N, 8, 128), F32),
        ),
        in_specs=[any_spec] * 7,
        out_specs=(any_spec, any_spec, any_spec),
        scratch_shapes=[
            pltpu.VMEM((C, C), BF),
            pltpu.SMEM((C,), F32),
            pltpu.VMEM(field, BF),
            pltpu.VMEM(field, BF),
            pltpu.VMEM((2, 8, 8, C * C), BF),
            pltpu.VMEM(table.shape, BF),
            pltpu.VMEM(back.shape[1:], BF),
            pltpu.VMEM((512, 64), BF),
            pltpu.VMEM((64, C * C), BF),
            pltpu.VMEM((1024, 64), BF),
            pltpu.VMEM((4, 2, N, 2, TY, TX), BF),
            pltpu.VMEM((4, 2, N, 16, 128), BF),
            pltpu.VMEM((4, N, 4, 128), F32),
            pltpu.VMEM((2, 2, N, 2, TY, TX), BF),
            pltpu.VMEM((4, 2, N, 16, 128), BF),
            pltpu.VMEM((4, N, 4, 128), F32),
            pltpu.VMEM((2, 2, 16, 256), BF),
            pltpu.VMEM((2, 2, N, 16, 256), BF),
            pltpu.VMEM((N, 8, 128), F32),
            pltpu.VMEM((4, N, 8, 128), F32),
            pltpu.VMEM((1024, 512), BF),
            pltpu.VMEM(field, BF),
            pltpu.VMEM((1024, 512), BF),
            pltpu.VMEM((2, 1024, 1024), BF),
            pltpu.VMEM(field, F32),
            pltpu.VMEM(field, F32),
            pltpu.VMEM((72, 1024), F32),
            pltpu.VMEM((2, 128, C), F32),
            pltpu.VMEM(field, BF),
            pltpu.SemaphoreType.DMA((15,)),
            pltpu.SemaphoreType.DMA((15, 2 * N)),
            pltpu.SemaphoreType.DMA((10,)),
        ],
        compiler_params=pltpu.CompilerParams(
            collective_id=0, has_side_effects=True, vmem_limit_bytes=VMEM_BYTES
        ),
    )(inputs, cotangent, spectral_weight, point_weight, bias, table, back)
    grad_input, spectral_grad, pointwise_grad, bias_grad = pl.pallas_call(
        last_kernel,
        out_shape=(
            jax.ShapeDtypeStruct(field, BF),
            jax.ShapeDtypeStruct((2, 8, 8, C * C), F32),
            jax.ShapeDtypeStruct((C, C), F32),
            jax.ShapeDtypeStruct((1, C), F32),
        ),
        in_specs=[any_spec] * 3,
        out_specs=(any_spec,) * 4,
        scratch_shapes=[
            pltpu.VMEM(field, BF),
            pltpu.VMEM((2, 128, C), F32),
            pltpu.VMEM((N, 8, 128), F32),
            pltpu.VMEM((2, 8, 8, C * C), F32),
            pltpu.VMEM((C, C), F32),
            pltpu.VMEM((1, C), F32),
            pltpu.SemaphoreType.DMA((4,)),
        ],
        compiler_params=pltpu.CompilerParams(vmem_limit_bytes=VMEM_BYTES),
    )(grad_input, modes, sums)
    return grad_input, spectral_grad, pointwise_grad, bias_grad.reshape(C)


def solution(mesh):
    in_specs = (P(None, "row", "col"), P(None, "row", "col"), P(None, "row", "col", None), P(), P())
    out_specs = (P(None, "row", "col"), P(None, "row", "col", None), P(), P())
    return jax.shard_map(body, mesh=mesh, in_specs=in_specs, out_specs=out_specs, check_vma=False)
```

```python
import functools
import math

import jax
import jax.numpy as jnp
import ml_dtypes
import numpy as np
from jax import lax
from jax.experimental import pallas as pl
from jax.experimental.pallas import tpu as pltpu
from jax.sharding import PartitionSpec as P

C = 64
K1 = 128
K2 = 128
NY = 1024
NX = 2048
TY = 64
TX = 128
N = 16
SCALE = float(NY * NX) ** (-0.5)
MESH = pl.DeviceIdType.MESH
VMEM_BYTES = 60 * 1024 * 1024
BF = jnp.bfloat16
F32 = jnp.float32

CHIPS = ((1, 2), (0, 1), (0, 3), (1, 1), (0, 2), (1, 0), (1, 3), (0, 0))
COL_ORDER = ((1, 2, 0), (0, 1, 0), (1, 2, 1), (0, 3, 0), (0, 1, 1), (1, 1, 0), (0, 3, 1), (0, 2, 0), (1, 1, 1), (1, 0, 0))
COL_ORDER += ((0, 2, 1), (1, 3, 0), (1, 0, 1), (1, 3, 1), (0, 0, 1))
ROW_ORDER = tuple((x, z) for z in (4, 3, 5, 2, 6, 1, 7, 0) for x in (0, 1) if (x, z) != (0, 0))

X1, Y1, T1, T2, Y2, X2, X3, Y3, T3, T4, Y4, X4, Z1, Z2, Z3 = range(15)


def trig(first, second, total):
    phase = np.mod(first[:, None] * second[None, :], total).astype(np.float32) * np.float32(
        2.0 * math.pi / total
    )
    return np.cos(phase).astype(ml_dtypes.bfloat16), np.sin(phase).astype(ml_dtypes.bfloat16)


@functools.cache
def tables():
    cos, sin = trig(np.arange(K2), np.arange(NX), NX)
    tx = np.concatenate([cos, -sin], 0).reshape(2 * K2, 8, NX // 8).transpose(1, 0, 2)
    cos, sin = trig(np.arange(K1) - K1 // 2, np.arange(NY), NY)
    c4, s4 = (t.reshape(N, 8, N, TY).transpose(2, 3, 0, 1) for t in (cos, sin))
    back = np.stack([np.stack([c4, -s4], 3), np.stack([s4, c4], 3)], 1).reshape(N, 2 * TY, 2 * K1)
    return np.ascontiguousarray(tx), np.ascontiguousarray(back)


def dot(a, b):
    return lax.dot_general(a, b, (((1,), (0,)), ((), ())), preferred_element_type=F32)


def dot_t(a, b):
    return lax.dot_general(a, b, (((1,), (1,)), ((), ())), preferred_element_type=F32)


def normal_slope(value):
    cumul = 0.5 * (1.0 + lax.erf(value * (1.0 / math.sqrt(2.0))))
    dens = jnp.exp(-0.5 * value * value) * (1.0 / math.sqrt(2.0 * math.pi))
    return cumul + value * dens


def kernel(
    inp, cot, w, pw_hbm, bias_hbm, tab, back,
    gin, ug, zsum,
    pw, bias, inp_v, cot_v, w_v, tab_v, back_v, backt_v, e1_v, e_v, sel_v,
    xr, yr, tr, xsend, ysend, tsend, gsend, gath,
    zsend, zr, f2_v, dz_v, dz2_v, kron_v, zp_v, gz_v, s_v, ug_v, gin_v,
    send_sem, recv_sem, loc_sem,
):
    row = lax.axis_index("row")
    col = lax.axis_index("col")
    col_x, col_y, col_c = lax.div(col, 8), lax.rem(lax.div(col, 2), 4), lax.rem(col, 2)
    mask_k = (lax.broadcasted_iota(jnp.int32, (8, 8, 128), 2) & 7) == lax.broadcasted_iota(
        jnp.int32, (8, 8, 128), 1
    )

    def wrap(i):
        return lax.rem(i, N)

    def remote(src, dst, phase, slot, device):
        return pltpu.make_async_remote_copy(
            src_ref=src,
            dst_ref=dst,
            send_sem=send_sem.at[phase],
            recv_sem=recv_sem.at[phase, slot],
            device_id=device,
            device_id_type=MESH,
        )

    def wait_recv(dst, phase, slot=0):
        remote(dst, dst, phase, slot, (row, col)).wait_recv()

    def wait_sent(like, phase):
        remote(like, like, phase, 0, (row, col)).wait_send()

    def keep(src, dst, phase, half=0):
        pltpu.make_async_copy(src, dst, recv_sem.at[phase, half]).start()

    pending = []

    def finish():
        for wait in pending:
            wait()

    def sent(like, phase):
        pending.append(lambda: wait_sent(like, phase))

    def row_partner(x, z):
        z = jnp.where(col_c == 0, z, 8 - z)
        return 8 * (lax.div(row, 8) ^ x) + lax.rem(lax.rem(row, 8) + z, 8)

    def col_partner(x, y, c, own_core):
        y = jnp.where(own_core == 0, y, 4 - y)
        return 8 * (col_x ^ x) + 2 * lax.rem(col_y + y, 4) + (col_c ^ c)

    def ordered(k):
        words = [0, 0]
        for i, (x, y, c) in enumerate(COL_ORDER):
            words[i // 8] |= (8 * x + 2 * y + c) << (4 * (i % 8))
        words = [w - (1 << 32) if w >> 31 else w for w in words]
        code = (jnp.where(k < 8, words[0], words[1]) >> (4 * lax.rem(k, 8))) & 15
        return code >> 3, (code >> 1) & 3, code & 1

    def send_block(src, dst, m, phase, half):
        remote(src, dst.at[half, col], phase, N * half + col, (row, m)).start()

    def send_row(src_of, dst, phase, slot, like, half=0):
        for x, z in ROW_ORDER:
            r = row_partner(x, z)
            remote(src_of(r), dst.at[slot], phase, half, (r, col)).start()
        keep(src_of(row), dst.at[slot], phase, half)
        sent(like, phase)

    def send_col(src_of, dst, phase, like):
        for x, y, c in COL_ORDER:
            m = col_partner(x, y, c, col_c)
            remote(src_of(m), dst.at[col], phase, 0, (row, m)).start()
        keep(src_of(col), dst.at[col], phase)
        sent(like, phase)

    barrier = pltpu.get_barrier_semaphore()

    @pl.loop(1, N)
    def _(d):
        pl.semaphore_signal(barrier, inc=1, device_id=(row, wrap(col + d)), device_id_type=MESH)
        pl.semaphore_signal(barrier, inc=1, device_id=(wrap(row + d), col), device_id_type=MESH)

    loads = [
        pltpu.make_async_copy(src, dst, loc_sem.at[i])
        for i, (src, dst) in enumerate(
            [
                (pw_hbm, pw),
                (bias_hbm, bias),
                (inp, inp_v),
                (tab, tab_v),
                (inp.at[pl.ds(4 * col, 2)], xr.at[0, 0, col]),
                (inp.at[pl.ds(4 * col + 2, 2)], xr.at[0, 1, col]),
                (w, w_v),
                (cot, cot_v),
                (back.at[row], back_v),
            ]
        )
    ]
    for load in loads:
        load.start()
    pl.semaphore_wait(barrier, 2 * N - 2)

    for half in range(2):
        for x, y, c in COL_ORDER:
            m = col_partner(x, y, c, col_c)
            send_block(inp.at[pl.ds(4 * m + 2 * half, 2)], xr.at[0], m, X1, half)
    sent(inp.at[pl.ds(0, 4 * N - 4)], X1)

    def pack(src, dst):
        for b in range(4):
            dst[:, 128 * b : 128 * b + 128] = src[:, 16 * b : 16 * b + 16, :].reshape(1024, 128)

    def build_kron(which):
        @pl.loop(0, 4)
        def _(i):
            rows = pl.ds(pl.multiple_of(256 * i, 256), 256)
            part = (dot_t if which == 0 else dot)(sel_v[rows, :], pw[...]).astype(BF)
            for j in range(4):
                full = dot_t(part, sel_v[256 * j : 256 * j + 256, :])
                same = (lax.broadcasted_iota(jnp.int32, (256, 256), 0) & 15) == (
                    lax.broadcasted_iota(jnp.int32, (256, 256), 1) & 15
                )
                kron_v[which, rows, 256 * j : 256 * j + 256] = jnp.where(same, full, 0.0).astype(BF)

    def apply_kron(which, src, dst):
        @pl.loop(0, 4)
        def _(i):
            rows = pl.ds(pl.multiple_of(256 * i, 256), 256)
            out = pl.ds(pl.multiple_of(16 * i, 16), 16)
            for h in range(2):
                res = dot(kron_v[which, rows, :], src[:, 256 * h : 256 * h + 256])
                for t in range(2):
                    y = 32 * h + 16 * t
                    dst[out, y : y + 16, :] = res[:, 128 * t : 128 * t + 128].reshape(16, 16, 128)

    def forward_x(src, phase, dst, half):
        acc = jnp.zeros((128, 256), F32)
        for x, y in CHIPS:
            chip = 4 * (col_x ^ x) + lax.rem(col_y + y, 4)
            blocks = []
            for c in range(2):
                slot = 2 * chip + c

                @pl.when(slot != col)
                def _(slot=slot):
                    wait_recv(src.at[half, slot], phase, N * half + slot)

                blocks.append(src[half, slot].reshape(128, 128))
            acc = acc + dot_t(jnp.concatenate(blocks, 1), tab_v[chip])
        acc = acc.astype(BF)
        parts = [jnp.concatenate([acc[0:TY, at : at + 128], acc[TY : 2 * TY, at : at + 128]], 1) for at in (0, 128)]
        dst[...] = dot(backt_v[...], jnp.concatenate(parts, 0)).astype(BF).reshape(N, 16, 256)

    def forward_y(src):
        total = jnp.sum(src[...].astype(F32), axis=0) * SCALE
        return [total[:, 0:128], total[:, 128:256]]

    def pack_t(tiles, dst):
        xt = jnp.concatenate(tiles + [jnp.zeros((64, 128), F32)], 0).astype(BF).astype(F32)
        x = xt.T.reshape(N, 8, 128)
        dst[...] = jnp.concatenate([x[:, 0:4, 0:64], x[:, 4:8, 0:64]], 2)

    def unpack_t(src):
        x = src[...]
        x = jnp.concatenate([x, pltpu.roll(x, 64, 2)], 1)
        return x.reshape(128, 128).T

    def to_modes(src):
        xt = unpack_t(src)
        rows = []
        for ri in range(2):
            cols = []
            for c in range(4):
                at = (2 * c + ri) * 8
                tile = xt[at : at + 8]
                cols.append(jnp.where(mask_k, tile[:, None, :], 0.0).reshape(64, 128))
            rows.append(jnp.concatenate(cols, 1))
        return dot(jnp.concatenate(rows, 0).astype(BF), e1_v[...])

    def from_modes(spec, dst):
        full = dot_t(spec.astype(BF), e1_v[...])
        tiles = []
        for c in range(4):
            for ri in range(2):
                part = full[64 * ri : 64 * ri + 64, 128 * c : 128 * c + 128].reshape(8, 8, 128)
                tiles.append(jnp.sum(jnp.where(mask_k, part, 0.0), axis=1))
        xt = jnp.concatenate(tiles + [jnp.zeros((64, 128), F32)], 0)
        x = xt.T.reshape(N, 8, 128)
        dst[...] = jnp.concatenate([x[:, 0:4, 0:64], x[:, 4:8, 0:64]], 2)

    def spread_modes(src, dst):
        xt = unpack_t(src)
        for half in range(2):
            pair = [xt[32 * half + 16 * c : 32 * half + 16 * c + 16] for c in range(2)]
            dst[half] = jnp.concatenate(pair, 1).astype(BF)

    def inverse_x(src, out, dst, phase, half):
        d = dot(back_v[...], src[...].reshape(256, 256)).astype(BF)
        real, imag = d[0:TY], d[TY : 2 * TY]
        rows = [jnp.concatenate([real[:, at : at + 128], imag[:, at : at + 128]], 1) for at in (0, 128)]
        yt = jnp.concatenate(rows, 0)
        late = None
        for x, y in CHIPS:
            chip = 4 * (col_x ^ x) + lax.rem(col_y + jnp.where(col_c == 0, y, 4 - y), 4)
            res = (dot(yt, tab_v[chip]) * SCALE).astype(BF)
            for c in range(2):
                out[half, 2 * chip + c] = res[:, 128 * c : 128 * c + 128].reshape(2, TY, TX)
            m = 2 * chip + col_c
            if (x, y) != (0, 0):
                send_block(out.at[half, m], dst, m, phase, half)
            else:
                dst[half, m] = out[half, m]
            if late is not None:
                send_block(out.at[half, late], dst, late, phase, half)
            late = m ^ 1
        send_block(out.at[half, late], dst, late, phase, half)

    lane = lax.broadcasted_iota(jnp.int32, (1024, 64), 1)
    first = lax.broadcasted_iota(jnp.int32, (1024, 64), 0)
    sel_v[...] = jnp.where((first >> 4) == lane, 1.0, 0.0).astype(BF)
    zsend[...] = jnp.zeros_like(zsend)
    loads[0].wait()
    build_kron(0)
    loads[2].wait()
    pack(inp_v, f2_v)
    apply_kron(0, f2_v, zp_v)
    first, lane = first[0:512], lane[0:512]
    at = (((first >> 3) & 15) << 2) + (first >> 7)
    e1_v[...] = jnp.where(at == lane, 1.0, 0.0).astype(BF)

    @pl.loop(0, 8)
    def _(i):
        channel = (lax.broadcasted_iota(jnp.int32, (64, 512), 1) >> 6) + 8 * i
        own = lax.broadcasted_iota(jnp.int32, (64, 512), 0)
        at = pl.ds(pl.multiple_of(i * 512, 512), 512)
        e_v[:, at] = jnp.where(channel == own, 1.0, 0.0).astype(BF)

    loads[8].wait()
    backt_v[...] = back_v[...].astype(F32).T.astype(BF)
    loads[3].wait()
    loads[4].wait()
    loads[5].wait()
    for half in range(2):
        forward_x(xr.at[0], X1, ysend.at[0, half], half)
        send_row(
            lambda r, half=half: ysend.at[0, half, r],
            yr.at[0, half],
            Y1,
            row,
            ysend.at[0, half, pl.ds(0, N - 1)],
            half,
        )
    build_kron(1)
    wait_recv(yr.at[0, 0], Y1, 0)
    first_half = forward_y(yr.at[0, 0])
    wait_recv(yr.at[0, 1], Y1, 1)
    pack_t(first_half + forward_y(yr.at[0, 1]), tsend.at[0])
    send_col(lambda m: tsend.at[0, m], tr.at[0], T1, tsend.at[0, pl.ds(0, N - 1)])
    loads[6].wait()
    wait_recv(tr.at[0], T1)

    u = to_modes(tr.at[0])
    ug_v[0] = u
    u = u.astype(BF)

    def fold(t):
        return t[:, 0:128] + t[:, 128:256] + t[:, 256:384] + t[:, 384:512]

    def mix(i, carry):
        sr, si = carry
        at = pl.ds(pl.multiple_of(i * 512, 512), 512)
        ue = dot(u, e_v[:, at])
        ur, ui = ue[0:64], ue[64:128]
        wr = w_v[0, :, :, at].astype(F32).reshape(64, 512)
        wi = w_v[1, :, :, at].astype(F32).reshape(64, 512)
        return sr + fold(wr * ur - wi * ui), si + fold(wr * ui + wi * ur)

    zero = jnp.zeros((64, 128), F32)
    sr, si = lax.fori_loop(0, 8, mix, (zero, zero), unroll=True)
    both = jnp.concatenate([sr, si], 0)
    both = both + pltpu.roll(both, 64, 1)
    from_modes(both[:, 0:64], tsend.at[1])
    send_col(lambda m: tsend.at[1, m], tr.at[1], T2, tsend.at[1, pl.ds(0, N - 1)])

    wait_recv(tr.at[1], T2)
    spread_modes(tr.at[1], gsend.at[0])
    for half in range(2):
        send_row(
            lambda r, half=half: gsend.at[0, half],
            gath.at[0, half],
            Y2,
            row,
            gath.at[0, half, pl.ds(0, N - 1)],
            half,
        )
    for half in range(2):
        wait_recv(gath.at[0, half], Y2, half)
        inverse_x(gath.at[0, half], xsend.at[0], xr.at[1], X2, half)
        sent(xsend.at[0, half, pl.ds(0, N - 1)], X2)

    loads[1].wait()
    loads[7].wait()
    def slope(m, half):
        for c in range(2):
            at = 4 * m + 2 * half + c
            z = xr[1, half, m, c].astype(F32) + zp_v[at] + bias[at]
            dz = cot_v[at].astype(F32) * normal_slope(z)
            dz_v[at] = dz.astype(BF)

    for half in range(2):
        slope(col, half)
        xr[2, half, col] = dz_v[pl.ds(4 * col + 2 * half, 2)]

        @pl.loop(0, N - 1)
        def _(k, half=half):
            x, y, c = ordered(k)
            m = col_partner(x, 4 - y, c, col_c ^ c)
            wait_recv(xr.at[1, half, m], X2, N * half + m)
            slope(m, half)
            send_block(dz_v.at[pl.ds(4 * m + 2 * half, 2)], xr.at[2], m, X3, half)

    sent(dz_v.at[pl.ds(0, 4 * N - 4)], X3)

    pack(dz_v, dz2_v)

    @pl.loop(0, 4)
    def _(o):
        cols = pl.ds(pl.multiple_of(256 * o, 256), 256)
        dzo = dz2_v[cols, :]
        same = (lax.broadcasted_iota(jnp.int32, (256, 256), 0) & 15) == (
            lax.broadcasted_iota(jnp.int32, (256, 256), 1) & 15
        )
        for i in range(4):
            prod = dot_t(f2_v[256 * i : 256 * i + 256, :], dzo)
            prod = jnp.where(same, prod, 0.0).reshape(16, 16, 256)
            s_v[16 * i : 16 * i + 16, cols] = jnp.sum(prod, axis=1)
        s_v[64:72, cols] = dot_t(jnp.ones((16, 512), BF), dzo)[0:8]

    terms = s_v[...]
    high = terms.astype(BF)
    low = (terms - high.astype(F32)).astype(BF)
    terms = dot(high, sel_v[...]) + dot(low, sel_v[...])
    zsend[:, 0:4, 0:64] = terms[0:64].reshape(N, 4, 64)
    zsend[0, 4:5, 0:64] = terms[64:65]
    send_col(lambda m: zsend.at[m], zr.at[0], Z1, zsend.at[pl.ds(0, N - 1)])
    apply_kron(1, dz2_v, gz_v)

    for half in range(2):
        forward_x(xr.at[2], X3, ysend.at[1, half], half)
        send_row(
            lambda r, half=half: ysend.at[1, half, r],
            yr.at[1, half],
            Y3,
            row,
            ysend.at[1, half, pl.ds(0, N - 1)],
            half,
        )
    wait_recv(yr.at[1, 0], Y3, 0)
    first_half = forward_y(yr.at[1, 0])
    wait_recv(yr.at[1, 1], Y3, 1)
    pack_t(first_half + forward_y(yr.at[1, 1]), tsend.at[2])
    send_col(lambda m: tsend.at[2, m], tr.at[2], T3, tsend.at[2, pl.ds(0, N - 1)])
    wait_recv(zr.at[0], Z1)
    zr[3, 0] = jnp.sum(zr[0], axis=0)
    send_row(lambda r: zr.at[3, 0], zr.at[1], Z2, row, zsend.at[pl.ds(0, N - 1)])
    wait_recv(tr.at[2], T3)

    g = to_modes(tr.at[2])
    ug_v[1] = g
    g = jnp.concatenate([g, g], 1)
    gr, gi = g[0:64], g[64:128]
    gr4, gi4 = jnp.concatenate([gr] * 4, 1), jnp.concatenate([gi] * 4, 1)

    def mix_back(i, acc):
        at = pl.ds(pl.multiple_of(i * 512, 512), 512)
        wr = w_v[0, :, :, at].astype(F32).reshape(64, 512)
        wi = w_v[1, :, :, at].astype(F32).reshape(64, 512)
        both = jnp.concatenate([wr * gr4 + wi * gi4, wr * gi4 - wi * gr4], 0).astype(BF)
        return acc + dot_t(both, e_v[:, at])

    du = lax.fori_loop(0, 8, mix_back, jnp.zeros((128, 64), F32), unroll=True)
    from_modes(du, tsend.at[3])
    send_col(lambda m: tsend.at[3, m], tr.at[3], T4, tsend.at[3, pl.ds(0, N - 1)])

    wait_recv(zr.at[1], Z2)
    zr[3, 1] = jnp.sum(zr[1], axis=0)
    send_col(lambda m: zr.at[3, 1], zr.at[2], Z3, zsend.at[pl.ds(0, N - 1)])
    out_ug = pltpu.make_async_copy(ug_v, ug, loc_sem.at[0])
    out_ug.start()
    pending.append(out_ug.wait)

    wait_recv(tr.at[3], T4)
    spread_modes(tr.at[3], gsend.at[1])
    for half in range(2):
        send_row(
            lambda r, half=half: gsend.at[1, half],
            gath.at[1, half],
            Y4,
            row,
            gath.at[1, half, pl.ds(0, N - 1)],
            half,
        )
    wait_recv(zr.at[2], Z3)
    out_z = pltpu.make_async_copy(zr.at[2], zsum, loc_sem.at[2])
    out_z.start()
    pending.append(out_z.wait)
    for half in range(2):
        wait_recv(gath.at[1, half], Y4, half)
        inverse_x(gath.at[1, half], xsend.at[1], xr.at[3], X4, half)
    finish()

    def finish_block(m, half):
        at = pl.ds(4 * m + 2 * half, 2)
        gin_v[at] = (xr[3, half, m].astype(F32) + gz_v[at]).astype(BF)
        pltpu.make_async_copy(gin_v.at[at], gin.at[at], loc_sem.at[1]).start()

    for half in range(2):
        finish_block(col, half)

        @pl.loop(0, N - 1)
        def _(k, half=half):
            x, y, c = ordered(k)
            m = col_partner(x, 4 - y, c, col_c ^ c)
            wait_recv(xr.at[3, half, m], X4, N * half + m)
            finish_block(m, half)

    wait_sent(xsend.at[1, 0, pl.ds(0, N - 1)], X4)
    wait_sent(xsend.at[1, 1, pl.ds(0, N - 1)], X4)
    pltpu.make_async_copy(gin_v, gin, loc_sem.at[1]).wait()


def last_kernel(
    gin, ug, zsum, gin_out, sg, pg, bg, gin_v, ug_v, z_v, sg_v, pg_v, bg_v, sem
):
    pieces = ((ug, ug_v), (gin, gin_v), (zsum, z_v))
    loads = [pltpu.make_async_copy(a, b, sem.at[i]) for i, (a, b) in enumerate(pieces)]
    for load in loads:
        load.start()
    loads[0].wait()
    u = ug_v[0].astype(BF)
    g = jnp.concatenate([ug_v[1]] * 8, 1)
    gr, gi = g[0:64], g[64:128]
    own = lax.broadcasted_iota(jnp.int32, (64, 512), 0)
    group = lax.broadcasted_iota(jnp.int32, (64, 512), 1) >> 6
    out = pltpu.make_async_copy(gin_v, gin_out, sem.at[1])
    for i in range(8):
        at = slice(512 * i, 512 * i + 512)
        ue = dot(u, jnp.where(group + 8 * i == own, 1.0, 0.0).astype(BF))
        ur, ui = ue[0:64], ue[64:128]
        sg_v[0, :, :, at] = (gr * ur + gi * ui).reshape(8, 8, 512)
        sg_v[1, :, :, at] = (gi * ur - gr * ui).reshape(8, 8, 512)
        pltpu.make_async_copy(sg_v.at[:, :, :, at], sg.at[:, :, :, at], sem.at[3]).start()
        if i == 0:
            loads[1].wait()
            out.start()
            loads[2].wait()
            pg_v[...] = z_v[:, 0:4, 0:64].reshape(C, C) * SCALE
            bg_v[...] = z_v[0, 4:5, 0:64] * SCALE
            sums = (
                pltpu.make_async_copy(pg_v, pg, sem.at[0]),
                pltpu.make_async_copy(bg_v, bg, sem.at[2]),
            )
            for copy in sums:
                copy.start()
    for copy in sums:
        copy.wait()
    out.wait()
    pltpu.make_async_copy(sg_v, sg, sem.at[3]).wait()


def body(inputs, cotangent, spectral_weight, point_weight, bias):
    any_spec = pl.BlockSpec(memory_space=pl.ANY)
    field = (C, TY, TX)
    table, back = (jnp.asarray(t) for t in tables())
    grad_input, modes, sums = pl.pallas_call(
        kernel,
        out_shape=(
            jax.ShapeDtypeStruct(field, BF),
            jax.ShapeDtypeStruct((2, 128, C), F32),
            jax.ShapeDtypeStruct((N, 8, 128), F32),
        ),
        in_specs=[any_spec] * 7,
        out_specs=(any_spec, any_spec, any_spec),
        scratch_shapes=[
            pltpu.VMEM((C, C), BF),
            pltpu.SMEM((C,), F32),
            pltpu.VMEM(field, BF),
            pltpu.VMEM(field, BF),
            pltpu.VMEM((2, 8, 8, C * C), BF),
            pltpu.VMEM(table.shape, BF),
            pltpu.VMEM(back.shape[1:], BF),
            pltpu.VMEM((256, 128), BF),
            pltpu.VMEM((512, 64), BF),
            pltpu.VMEM((64, C * C), BF),
            pltpu.VMEM((1024, 64), BF),
            pltpu.VMEM((4, 2, N, 2, TY, TX), BF),
            pltpu.VMEM((2, 2, N, 16, 256), BF),
            pltpu.VMEM((4, N, 4, 128), F32),
            pltpu.VMEM((2, 2, N, 2, TY, TX), BF),
            pltpu.VMEM((2, 2, N, 16, 256), BF),
            pltpu.VMEM((4, N, 4, 128), F32),
            pltpu.VMEM((2, 2, 16, 256), BF),
            pltpu.VMEM((2, 2, N, 16, 256), BF),
            pltpu.VMEM((N, 8, 128), F32),
            pltpu.VMEM((4, N, 8, 128), F32),
            pltpu.VMEM((1024, 512), BF),
            pltpu.VMEM(field, BF),
            pltpu.VMEM((1024, 512), BF),
            pltpu.VMEM((2, 1024, 1024), BF),
            pltpu.VMEM(field, F32),
            pltpu.VMEM(field, F32),
            pltpu.VMEM((72, 1024), F32),
            pltpu.VMEM((2, 128, C), F32),
            pltpu.VMEM(field, BF),
            pltpu.SemaphoreType.DMA((15,)),
            pltpu.SemaphoreType.DMA((15, 2 * N)),
            pltpu.SemaphoreType.DMA((10,)),
        ],
        compiler_params=pltpu.CompilerParams(
            collective_id=0, has_side_effects=True, vmem_limit_bytes=VMEM_BYTES
        ),
    )(inputs, cotangent, spectral_weight, point_weight, bias, table, back)
    grad_input, spectral_grad, pointwise_grad, bias_grad = pl.pallas_call(
        last_kernel,
        out_shape=(
            jax.ShapeDtypeStruct(field, BF),
            jax.ShapeDtypeStruct((2, 8, 8, C * C), F32),
            jax.ShapeDtypeStruct((C, C), F32),
            jax.ShapeDtypeStruct((1, C), F32),
        ),
        in_specs=[any_spec] * 3,
        out_specs=(any_spec,) * 4,
        scratch_shapes=[
            pltpu.VMEM(field, BF),
            pltpu.VMEM((2, 128, C), F32),
            pltpu.VMEM((N, 8, 128), F32),
            pltpu.VMEM((2, 8, 8, C * C), F32),
            pltpu.VMEM((C, C), F32),
            pltpu.VMEM((1, C), F32),
            pltpu.SemaphoreType.DMA((4,)),
        ],
        compiler_params=pltpu.CompilerParams(vmem_limit_bytes=VMEM_BYTES),
    )(grad_input, modes, sums)
    return grad_input, spectral_grad, pointwise_grad, bias_grad.reshape(C)


def solution(mesh):
    in_specs = (P(None, "row", "col"), P(None, "row", "col"), P(None, "row", "col", None), P(), P())
    out_specs = (P(None, "row", "col"), P(None, "row", "col", None), P(), P())
    return jax.shard_map(body, mesh=mesh, in_specs=in_specs, out_specs=out_specs, check_vma=False)
```

```python
import functools
import math

import jax
import jax.numpy as jnp
import ml_dtypes
import numpy as np
from jax import lax
from jax.experimental import pallas as pl
from jax.experimental.pallas import tpu as pltpu
from jax.sharding import PartitionSpec as P

C = 64
K1 = 128
K2 = 128
NY = 1024
NX = 2048
TY = 64
TX = 128
N = 16
SCALE = float(NY * NX) ** (-0.5)
MESH = pl.DeviceIdType.MESH
VMEM_BYTES = 60 * 1024 * 1024
BF = jnp.bfloat16
F32 = jnp.float32

CHIPS = ((1, 2), (0, 1), (0, 3), (1, 1), (0, 2), (1, 0), (1, 3), (0, 0))
COL_ORDER = ((1, 2, 0), (0, 1, 0), (1, 2, 1), (0, 3, 0), (0, 1, 1), (1, 1, 0), (0, 3, 1), (0, 2, 0), (1, 1, 1), (1, 0, 0))
COL_ORDER += ((0, 2, 1), (1, 3, 0), (1, 0, 1), (1, 3, 1), (0, 0, 1))
ROW_ORDER = tuple((x, z) for z in (4, 3, 5, 2, 6, 1, 7, 0) for x in (0, 1) if (x, z) != (0, 0))

X1, Y1, T1, T2, Y2, X2, X3, Y3, T3, T4, Y4, X4, Z1, Z2, Z3 = range(15)


def trig(first, second, total):
    phase = np.mod(first[:, None] * second[None, :], total).astype(np.float32) * np.float32(
        2.0 * math.pi / total
    )
    return np.cos(phase).astype(ml_dtypes.bfloat16), np.sin(phase).astype(ml_dtypes.bfloat16)


@functools.cache
def tables():
    cos, sin = trig(np.arange(K2), np.arange(NX), NX)
    tx = np.concatenate([cos, -sin], 0).reshape(2 * K2, 8, NX // 8).transpose(1, 0, 2)
    cos, sin = trig(np.arange(K1) - K1 // 2, np.arange(NY), NY)
    c4, s4 = (t.reshape(N, 8, N, TY).transpose(2, 3, 0, 1) for t in (cos, sin))
    back = np.stack([np.stack([c4, -s4], 3), np.stack([s4, c4], 3)], 1).reshape(N, 2 * TY, 2 * K1)
    return np.ascontiguousarray(tx), np.ascontiguousarray(back)


def dot(a, b):
    return lax.dot_general(a, b, (((1,), (0,)), ((), ())), preferred_element_type=F32)


def dot_t(a, b):
    return lax.dot_general(a, b, (((1,), (1,)), ((), ())), preferred_element_type=F32)


def normal_slope(value):
    cumul = 0.5 * (1.0 + lax.erf(value * (1.0 / math.sqrt(2.0))))
    dens = jnp.exp(-0.5 * value * value) * (1.0 / math.sqrt(2.0 * math.pi))
    return cumul + value * dens


def kernel(
    inp, cot, w, pw_hbm, bias_hbm, tab, back,
    gin, ug, zsum,
    pw, bias, inp_v, cot_v, w_v, wide_v, tab_v, back_v, backt_v, e1_v, e_v, sel_v,
    xr, yr, tr, xsend, ysend, tsend, gsend, gath,
    zsend, zr, f2_v, dz_v, dz2_v, kron_v, zp_v, gz_v, s_v, ug_v, gin_v,
    send_sem, recv_sem, loc_sem,
):
    row = lax.axis_index("row")
    col = lax.axis_index("col")
    col_x, col_y, col_c = lax.div(col, 8), lax.rem(lax.div(col, 2), 4), lax.rem(col, 2)
    mask_k = (lax.broadcasted_iota(jnp.int32, (8, 8, 128), 2) & 7) == lax.broadcasted_iota(
        jnp.int32, (8, 8, 128), 1
    )

    def wrap(i):
        return lax.rem(i, N)

    def remote(src, dst, phase, slot, device):
        return pltpu.make_async_remote_copy(
            src_ref=src,
            dst_ref=dst,
            send_sem=send_sem.at[phase],
            recv_sem=recv_sem.at[phase, slot],
            device_id=device,
            device_id_type=MESH,
        )

    def wait_recv(dst, phase, slot=0):
        remote(dst, dst, phase, slot, (row, col)).wait_recv()

    def wait_sent(like, phase):
        remote(like, like, phase, 0, (row, col)).wait_send()

    def keep(src, dst, phase, half=0):
        pltpu.make_async_copy(src, dst, recv_sem.at[phase, half]).start()

    pending = []

    def finish():
        for wait in pending:
            wait()

    def sent(like, phase):
        pending.append(lambda: wait_sent(like, phase))

    def row_partner(x, z):
        z = jnp.where(col_c == 0, z, 8 - z)
        return 8 * (lax.div(row, 8) ^ x) + lax.rem(lax.rem(row, 8) + z, 8)

    def col_partner(x, y, c, own_core):
        y = jnp.where(own_core == 0, y, 4 - y)
        return 8 * (col_x ^ x) + 2 * lax.rem(col_y + y, 4) + (col_c ^ c)

    def ordered(k):
        words = [0, 0]
        for i, (x, y, c) in enumerate(COL_ORDER):
            words[i // 8] |= (8 * x + 2 * y + c) << (4 * (i % 8))
        words = [w - (1 << 32) if w >> 31 else w for w in words]
        code = (jnp.where(k < 8, words[0], words[1]) >> (4 * lax.rem(k, 8))) & 15
        return code >> 3, (code >> 1) & 3, code & 1

    def send_block(src, dst, m, phase, half):
        remote(src, dst.at[half, col], phase, N * half + col, (row, m)).start()

    def send_row(src_of, dst, phase, slot, like, half=0):
        for x, z in ROW_ORDER:
            r = row_partner(x, z)
            remote(src_of(r), dst.at[slot], phase, half, (r, col)).start()
        keep(src_of(row), dst.at[slot], phase, half)
        sent(like, phase)

    def send_col(src_of, dst, phase, like):
        for x, y, c in COL_ORDER:
            m = col_partner(x, y, c, col_c)
            remote(src_of(m), dst.at[col], phase, 0, (row, m)).start()
        keep(src_of(col), dst.at[col], phase)
        sent(like, phase)

    barrier = pltpu.get_barrier_semaphore()

    for x, z in ROW_ORDER:
        pl.semaphore_signal(barrier, inc=1, device_id=(row_partner(x, z), col), device_id_type=MESH)
    for x, y, c in COL_ORDER:
        m = col_partner(x, y, c, col_c)
        pl.semaphore_signal(barrier, inc=1, device_id=(row, m), device_id_type=MESH)

    loads = [
        pltpu.make_async_copy(src, dst, loc_sem.at[i])
        for i, (src, dst) in enumerate(
            [
                (pw_hbm, pw),
                (bias_hbm, bias),
                (inp, inp_v),
                (tab, tab_v),
                (inp.at[pl.ds(4 * col, 2)], xr.at[0, 0, col]),
                (inp.at[pl.ds(4 * col + 2, 2)], xr.at[0, 1, col]),
                (w, w_v),
                (cot, cot_v),
                (back.at[row], back_v),
            ]
        )
    ]
    for load in loads:
        load.start()
    pl.semaphore_wait(barrier, 2 * N - 2)

    for half in range(2):
        for x, y, c in COL_ORDER:
            m = col_partner(x, y, c, col_c)
            send_block(inp.at[pl.ds(4 * m + 2 * half, 2)], xr.at[0], m, X1, half)
    sent(inp.at[pl.ds(0, 4 * N - 4)], X1)

    def pack(src, dst):
        for b in range(4):
            dst[:, 128 * b : 128 * b + 128] = src[:, 16 * b : 16 * b + 16, :].reshape(1024, 128)

    def build_kron(which):
        @pl.loop(0, 4)
        def _(i):
            rows = pl.ds(pl.multiple_of(256 * i, 256), 256)
            part = (dot_t if which == 0 else dot)(sel_v[rows, :], pw[...]).astype(BF)
            for j in range(4):
                full = dot_t(part, sel_v[256 * j : 256 * j + 256, :])
                same = (lax.broadcasted_iota(jnp.int32, (256, 256), 0) & 15) == (
                    lax.broadcasted_iota(jnp.int32, (256, 256), 1) & 15
                )
                kron_v[which, rows, 256 * j : 256 * j + 256] = jnp.where(same, full, 0.0).astype(BF)

    def apply_kron(which, src, dst):
        @pl.loop(0, 4)
        def _(i):
            rows = pl.ds(pl.multiple_of(256 * i, 256), 256)
            out = pl.ds(pl.multiple_of(16 * i, 16), 16)
            for h in range(2):
                res = dot(kron_v[which, rows, :], src[:, 256 * h : 256 * h + 256])
                for t in range(2):
                    y = 32 * h + 16 * t
                    dst[out, y : y + 16, :] = res[:, 128 * t : 128 * t + 128].reshape(16, 16, 128)

    def forward_x(src, phase, dst, half):
        acc = jnp.zeros((128, 256), F32)
        for x, y in CHIPS:
            chip = 4 * (col_x ^ x) + lax.rem(col_y + y, 4)
            blocks = []
            for c in range(2):
                slot = 2 * chip + c

                @pl.when(slot != col)
                def _(slot=slot):
                    wait_recv(src.at[half, slot], phase, N * half + slot)

                blocks.append(src[half, slot].reshape(128, 128))
            acc = acc + dot_t(jnp.concatenate(blocks, 1), tab_v[chip])
        acc = acc.astype(BF)
        parts = [jnp.concatenate([acc[0:TY, at : at + 128], acc[TY : 2 * TY, at : at + 128]], 1) for at in (0, 128)]
        dst[...] = dot(backt_v[...], jnp.concatenate(parts, 0)).astype(BF).reshape(N, 16, 256)

    def forward_y(src):
        total = jnp.sum(src[...].astype(F32), axis=0) * SCALE
        return [total[:, 0:128], total[:, 128:256]]

    def pack_t(tiles, dst):
        xt = jnp.concatenate(tiles + [jnp.zeros((64, 128), F32)], 0).astype(BF).astype(F32)
        x = xt.T.reshape(N, 8, 128)
        dst[...] = jnp.concatenate([x[:, 0:4, 0:64], x[:, 4:8, 0:64]], 2)

    def unpack_t(src):
        x = src[...]
        x = jnp.concatenate([x, pltpu.roll(x, 64, 2)], 1)
        return x.reshape(128, 128).T

    def to_modes(src):
        xt = unpack_t(src)
        rows = []
        for ri in range(2):
            cols = []
            for c in range(4):
                at = (2 * c + ri) * 8
                tile = xt[at : at + 8]
                cols.append(jnp.where(mask_k, tile[:, None, :], 0.0).reshape(64, 128))
            rows.append(jnp.concatenate(cols, 1))
        return dot(jnp.concatenate(rows, 0).astype(BF), e1_v[...])

    def from_modes(spec, dst):
        full = dot_t(spec.astype(BF), e1_v[...])
        tiles = []
        for c in range(4):
            for ri in range(2):
                part = full[64 * ri : 64 * ri + 64, 128 * c : 128 * c + 128].reshape(8, 8, 128)
                tiles.append(jnp.sum(jnp.where(mask_k, part, 0.0), axis=1))
        xt = jnp.concatenate(tiles + [jnp.zeros((64, 128), F32)], 0)
        x = xt.T.reshape(N, 8, 128)
        dst[...] = jnp.concatenate([x[:, 0:4, 0:64], x[:, 4:8, 0:64]], 2)

    def spread_modes(src, dst):
        xt = unpack_t(src)
        for half in range(2):
            pair = [xt[32 * half + 16 * c : 32 * half + 16 * c + 16] for c in range(2)]
            dst[half] = jnp.concatenate(pair, 1).astype(BF)

    def inverse_x(src, out, dst, phase, half):
        d = dot(back_v[...], src[...].reshape(256, 256)).astype(BF)
        real, imag = d[0:TY], d[TY : 2 * TY]
        rows = [jnp.concatenate([real[:, at : at + 128], imag[:, at : at + 128]], 1) for at in (0, 128)]
        yt = jnp.concatenate(rows, 0)
        late = None
        for x, y in CHIPS:
            chip = 4 * (col_x ^ x) + lax.rem(col_y + jnp.where(col_c == 0, y, 4 - y), 4)
            res = (dot(yt, tab_v[chip]) * SCALE).astype(BF)
            for c in range(2):
                out[half, 2 * chip + c] = res[:, 128 * c : 128 * c + 128].reshape(2, TY, TX)
            m = 2 * chip + col_c
            if (x, y) != (0, 0):
                send_block(out.at[half, m], dst, m, phase, half)
            else:
                dst[half, m] = out[half, m]
            if late is not None:
                send_block(out.at[half, late], dst, late, phase, half)
            late = m ^ 1
        send_block(out.at[half, late], dst, late, phase, half)

    lane = lax.broadcasted_iota(jnp.int32, (1024, 64), 1)
    first = lax.broadcasted_iota(jnp.int32, (1024, 64), 0)
    sel_v[...] = jnp.where((first >> 4) == lane, 1.0, 0.0).astype(BF)
    zsend[...] = jnp.zeros_like(zsend)
    loads[0].wait()
    build_kron(0)
    loads[2].wait()
    pack(inp_v, f2_v)
    apply_kron(0, f2_v, zp_v)
    first, lane = first[0:512], lane[0:512]
    at = (((first >> 3) & 15) << 2) + (first >> 7)
    e1_v[...] = jnp.where(at == lane, 1.0, 0.0).astype(BF)

    @pl.loop(0, 8)
    def _(i):
        channel = (lax.broadcasted_iota(jnp.int32, (64, 512), 1) >> 6) + 8 * i
        own = lax.broadcasted_iota(jnp.int32, (64, 512), 0)
        at = pl.ds(pl.multiple_of(i * 512, 512), 512)
        e_v[:, at] = jnp.where(channel == own, 1.0, 0.0).astype(BF)

    loads[8].wait()
    backt_v[...] = back_v[...].astype(F32).T.astype(BF)
    loads[3].wait()
    loads[4].wait()
    loads[5].wait()
    for half in range(2):
        forward_x(xr.at[0], X1, ysend.at[0, half], half)
        send_row(
            lambda r, half=half: ysend.at[0, half, r],
            yr.at[0, half],
            Y1,
            row,
            ysend.at[0, half, pl.ds(0, N - 1)],
            half,
        )
    build_kron(1)
    wait_recv(yr.at[0, 0], Y1, 0)
    first_half = forward_y(yr.at[0, 0])
    wait_recv(yr.at[0, 1], Y1, 1)
    pack_t(first_half + forward_y(yr.at[0, 1]), tsend.at[0])
    send_col(lambda m: tsend.at[0, m], tr.at[0], T1, tsend.at[0, pl.ds(0, N - 1)])
    loads[6].wait()

    @pl.loop(0, 8)
    def _(i):
        at = pl.ds(pl.multiple_of(i * 512, 512), 512)
        for p in range(2):
            wide_v[p, :, at] = w_v[p, :, :, at].astype(F32).reshape(64, 512)

    wait_recv(tr.at[0], T1)

    u = to_modes(tr.at[0])
    ug_v[0] = u
    u = u.astype(BF)

    def fold(t):
        return t[:, 0:128] + t[:, 128:256] + t[:, 256:384] + t[:, 384:512]

    def mix(i, carry):
        sr, si = carry
        at = pl.ds(pl.multiple_of(i * 512, 512), 512)
        ue = dot(u, e_v[:, at])
        ur, ui = ue[0:64], ue[64:128]
        wr, wi = wide_v[0, :, at], wide_v[1, :, at]
        return sr + fold(wr * ur - wi * ui), si + fold(wr * ui + wi * ur)

    zero = jnp.zeros((64, 128), F32)
    sr, si = lax.fori_loop(0, 8, mix, (zero, zero), unroll=True)
    both = jnp.concatenate([sr, si], 0)
    both = both + pltpu.roll(both, 64, 1)
    from_modes(both[:, 0:64], tsend.at[1])
    send_col(lambda m: tsend.at[1, m], tr.at[1], T2, tsend.at[1, pl.ds(0, N - 1)])

    wait_recv(tr.at[1], T2)
    spread_modes(tr.at[1], gsend.at[0])
    for half in range(2):
        send_row(
            lambda r, half=half: gsend.at[0, half],
            gath.at[0, half],
            Y2,
            row,
            gath.at[0, half, pl.ds(0, N - 1)],
            half,
        )
    for half in range(2):
        wait_recv(gath.at[0, half], Y2, half)
        inverse_x(gath.at[0, half], xsend.at[0], xr.at[1], X2, half)
        sent(xsend.at[0, half, pl.ds(0, N - 1)], X2)

    loads[1].wait()
    loads[7].wait()
    def slope(m, half):
        for c in range(2):
            at = 4 * m + 2 * half + c
            z = xr[1, half, m, c].astype(F32) + zp_v[at] + bias[at]
            dz = cot_v[at].astype(F32) * normal_slope(z)
            dz_v[at] = dz.astype(BF)

    for half in range(2):
        slope(col, half)
        xr[2, half, col] = dz_v[pl.ds(4 * col + 2 * half, 2)]

        @pl.loop(0, N - 1)
        def _(k, half=half):
            x, y, c = ordered(k)
            m = col_partner(x, 4 - y, c, col_c ^ c)
            wait_recv(xr.at[1, half, m], X2, N * half + m)
            slope(m, half)
            send_block(dz_v.at[pl.ds(4 * m + 2 * half, 2)], xr.at[2], m, X3, half)

    sent(dz_v.at[pl.ds(0, 4 * N - 4)], X3)

    pack(dz_v, dz2_v)

    @pl.loop(0, 4)
    def _(o):
        cols = pl.ds(pl.multiple_of(256 * o, 256), 256)
        dzo = dz2_v[cols, :]
        same = (lax.broadcasted_iota(jnp.int32, (256, 256), 0) & 15) == (
            lax.broadcasted_iota(jnp.int32, (256, 256), 1) & 15
        )
        for i in range(4):
            prod = dot_t(f2_v[256 * i : 256 * i + 256, :], dzo)
            prod = jnp.where(same, prod, 0.0).reshape(16, 16, 256)
            s_v[16 * i : 16 * i + 16, cols] = jnp.sum(prod, axis=1)
        s_v[64:72, cols] = dot_t(jnp.ones((16, 512), BF), dzo)[0:8]

    terms = s_v[...]
    high = terms.astype(BF)
    low = (terms - high.astype(F32)).astype(BF)
    terms = dot(high, sel_v[...]) + dot(low, sel_v[...])
    zsend[:, 0:4, 0:64] = terms[0:64].reshape(N, 4, 64)
    zsend[0, 4:5, 0:64] = terms[64:65]
    send_col(lambda m: zsend.at[m], zr.at[0], Z1, zsend.at[pl.ds(0, N - 1)])
    apply_kron(1, dz2_v, gz_v)

    for half in range(2):
        forward_x(xr.at[2], X3, ysend.at[1, half], half)
        send_row(
            lambda r, half=half: ysend.at[1, half, r],
            yr.at[1, half],
            Y3,
            row,
            ysend.at[1, half, pl.ds(0, N - 1)],
            half,
        )
    wait_recv(yr.at[1, 0], Y3, 0)
    first_half = forward_y(yr.at[1, 0])
    wait_recv(yr.at[1, 1], Y3, 1)
    pack_t(first_half + forward_y(yr.at[1, 1]), tsend.at[2])
    send_col(lambda m: tsend.at[2, m], tr.at[2], T3, tsend.at[2, pl.ds(0, N - 1)])
    wait_recv(zr.at[0], Z1)
    zr[3, 0] = jnp.sum(zr[0], axis=0)
    send_row(lambda r: zr.at[3, 0], zr.at[1], Z2, row, zsend.at[pl.ds(0, N - 1)])
    wait_recv(tr.at[2], T3)

    g = to_modes(tr.at[2])
    ug_v[1] = g
    g = jnp.concatenate([g, g], 1)
    gr, gi = g[0:64], g[64:128]
    gr4, gi4 = jnp.concatenate([gr] * 4, 1), jnp.concatenate([gi] * 4, 1)

    def mix_back(i, acc):
        at = pl.ds(pl.multiple_of(i * 512, 512), 512)
        wr, wi = wide_v[0, :, at], wide_v[1, :, at]
        both = jnp.concatenate([wr * gr4 + wi * gi4, wr * gi4 - wi * gr4], 0).astype(BF)
        return acc + dot_t(both, e_v[:, at])

    du = lax.fori_loop(0, 8, mix_back, jnp.zeros((128, 64), F32), unroll=True)
    from_modes(du, tsend.at[3])
    send_col(lambda m: tsend.at[3, m], tr.at[3], T4, tsend.at[3, pl.ds(0, N - 1)])

    out_ug = pltpu.make_async_copy(ug_v, ug, loc_sem.at[0])
    out_ug.start()
    pending.append(out_ug.wait)

    wait_recv(tr.at[3], T4)
    spread_modes(tr.at[3], gsend.at[1])
    for half in range(2):
        send_row(
            lambda r, half=half: gsend.at[1, half],
            gath.at[1, half],
            Y4,
            row,
            gath.at[1, half, pl.ds(0, N - 1)],
            half,
        )
    wait_recv(zr.at[1], Z2)
    zr[3, 1] = jnp.sum(zr[1], axis=0)
    send_col(lambda m: zr.at[3, 1], zr.at[2], Z3, zsend.at[pl.ds(0, N - 1)])
    for half in range(2):
        wait_recv(gath.at[1, half], Y4, half)
        inverse_x(gath.at[1, half], xsend.at[1], xr.at[3], X4, half)
    wait_recv(zr.at[2], Z3)
    out_z = pltpu.make_async_copy(zr.at[2], zsum, loc_sem.at[2])
    out_z.start()
    pending.append(out_z.wait)
    finish()

    def finish_block(m, half):
        at = pl.ds(4 * m + 2 * half, 2)
        gin_v[at] = (xr[3, half, m].astype(F32) + gz_v[at]).astype(BF)
        pltpu.make_async_copy(gin_v.at[at], gin.at[at], loc_sem.at[1]).start()

    for half in range(2):
        finish_block(col, half)

        @pl.loop(0, N - 1)
        def _(k, half=half):
            x, y, c = ordered(k)
            m = col_partner(x, 4 - y, c, col_c ^ c)
            wait_recv(xr.at[3, half, m], X4, N * half + m)
            finish_block(m, half)

    wait_sent(xsend.at[1, 0, pl.ds(0, N - 1)], X4)
    wait_sent(xsend.at[1, 1, pl.ds(0, N - 1)], X4)
    pltpu.make_async_copy(gin_v, gin, loc_sem.at[1]).wait()


def last_kernel(
    gin, ug, zsum, gin_out, sg, pg, bg, gin_v, ug_v, z_v, sg_v, pg_v, bg_v, sem
):
    pieces = ((ug, ug_v), (gin, gin_v), (zsum, z_v))
    loads = [pltpu.make_async_copy(a, b, sem.at[i]) for i, (a, b) in enumerate(pieces)]
    for load in loads:
        load.start()
    loads[0].wait()
    u = ug_v[0].astype(BF)
    g = jnp.concatenate([ug_v[1]] * 8, 1)
    gr, gi = g[0:64], g[64:128]
    own = lax.broadcasted_iota(jnp.int32, (64, 512), 0)
    group = lax.broadcasted_iota(jnp.int32, (64, 512), 1) >> 6
    out = pltpu.make_async_copy(gin_v, gin_out, sem.at[1])
    for i in range(8):
        at = slice(512 * i, 512 * i + 512)
        ue = dot(u, jnp.where(group + 8 * i == own, 1.0, 0.0).astype(BF))
        ur, ui = ue[0:64], ue[64:128]
        sg_v[0, :, :, at] = (gr * ur + gi * ui).reshape(8, 8, 512)
        sg_v[1, :, :, at] = (gi * ur - gr * ui).reshape(8, 8, 512)
        pltpu.make_async_copy(sg_v.at[:, :, :, at], sg.at[:, :, :, at], sem.at[3]).start()
        if i == 0:
            loads[1].wait()
            out.start()
            loads[2].wait()
            pg_v[...] = z_v[:, 0:4, 0:64].reshape(C, C) * SCALE
            bg_v[...] = z_v[0, 4:5, 0:64] * SCALE
            sums = (
                pltpu.make_async_copy(pg_v, pg, sem.at[0]),
                pltpu.make_async_copy(bg_v, bg, sem.at[2]),
            )
            for copy in sums:
                copy.start()
    for copy in sums:
        copy.wait()
    out.wait()
    pltpu.make_async_copy(sg_v, sg, sem.at[3]).wait()


def body(inputs, cotangent, spectral_weight, point_weight, bias):
    any_spec = pl.BlockSpec(memory_space=pl.ANY)
    field = (C, TY, TX)
    table, back = (jnp.asarray(t) for t in tables())
    grad_input, modes, sums = pl.pallas_call(
        kernel,
        out_shape=(
            jax.ShapeDtypeStruct(field, BF),
            jax.ShapeDtypeStruct((2, 128, C), F32),
            jax.ShapeDtypeStruct((N, 8, 128), F32),
        ),
        in_specs=[any_spec] * 7,
        out_specs=(any_spec, any_spec, any_spec),
        scratch_shapes=[
            pltpu.VMEM((C, C), BF),
            pltpu.SMEM((C,), F32),
            pltpu.VMEM(field, BF),
            pltpu.VMEM(field, BF),
            pltpu.VMEM((2, 8, 8, C * C), BF),
            pltpu.VMEM((2, 64, C * C), F32),
            pltpu.VMEM(table.shape, BF),
            pltpu.VMEM(back.shape[1:], BF),
            pltpu.VMEM((256, 128), BF),
            pltpu.VMEM((512, 64), BF),
            pltpu.VMEM((64, C * C), BF),
            pltpu.VMEM((1024, 64), BF),
            pltpu.VMEM((4, 2, N, 2, TY, TX), BF),
            pltpu.VMEM((2, 2, N, 16, 256), BF),
            pltpu.VMEM((4, N, 4, 128), F32),
            pltpu.VMEM((2, 2, N, 2, TY, TX), BF),
            pltpu.VMEM((2, 2, N, 16, 256), BF),
            pltpu.VMEM((4, N, 4, 128), F32),
            pltpu.VMEM((2, 2, 16, 256), BF),
            pltpu.VMEM((2, 2, N, 16, 256), BF),
            pltpu.VMEM((N, 8, 128), F32),
            pltpu.VMEM((4, N, 8, 128), F32),
            pltpu.VMEM((1024, 512), BF),
            pltpu.VMEM(field, BF),
            pltpu.VMEM((1024, 512), BF),
            pltpu.VMEM((2, 1024, 1024), BF),
            pltpu.VMEM(field, F32),
            pltpu.VMEM(field, F32),
            pltpu.VMEM((72, 1024), F32),
            pltpu.VMEM((2, 128, C), F32),
            pltpu.VMEM(field, BF),
            pltpu.SemaphoreType.DMA((15,)),
            pltpu.SemaphoreType.DMA((15, 2 * N)),
            pltpu.SemaphoreType.DMA((10,)),
        ],
        compiler_params=pltpu.CompilerParams(
            collective_id=0, has_side_effects=True, vmem_limit_bytes=VMEM_BYTES
        ),
    )(inputs, cotangent, spectral_weight, point_weight, bias, table, back)
    grad_input, spectral_grad, pointwise_grad, bias_grad = pl.pallas_call(
        last_kernel,
        out_shape=(
            jax.ShapeDtypeStruct(field, BF),
            jax.ShapeDtypeStruct((2, 8, 8, C * C), F32),
            jax.ShapeDtypeStruct((C, C), F32),
            jax.ShapeDtypeStruct((1, C), F32),
        ),
        in_specs=[any_spec] * 3,
        out_specs=(any_spec,) * 4,
        scratch_shapes=[
            pltpu.VMEM(field, BF),
            pltpu.VMEM((2, 128, C), F32),
            pltpu.VMEM((N, 8, 128), F32),
            pltpu.VMEM((2, 8, 8, C * C), F32),
            pltpu.VMEM((C, C), F32),
            pltpu.VMEM((1, C), F32),
            pltpu.SemaphoreType.DMA((4,)),
        ],
        compiler_params=pltpu.CompilerParams(vmem_limit_bytes=VMEM_BYTES),
    )(grad_input, modes, sums)
    return grad_input, spectral_grad, pointwise_grad, bias_grad.reshape(C)


def solution(mesh):
    in_specs = (P(None, "row", "col"), P(None, "row", "col"), P(None, "row", "col", None), P(), P())
    out_specs = (P(None, "row", "col"), P(None, "row", "col", None), P(), P())
    return jax.shard_map(body, mesh=mesh, in_specs=in_specs, out_specs=out_specs, check_vma=False)
```
